32 devices in a mesh: dp: 16 (over z, y, x), fsdp: 2 (over core).
Axes of the slice: x: 2, y: 2, z: 4, core: 2. Of those that a mesh axis runs over, the one named last changes fastest.
Arguments:
- tokens: bfloat16 [32, 1024, 512], P(('dp', 'fsdp')), may hold values from -6 to 6
- encoder: bfloat16 [32, 1024, 512], P(('dp', 'fsdp')), may hold values from -6 to 6
- out_grad: bfloat16 [32, 1024, 512], P(('dp', 'fsdp')), may hold values from -6 to 6
- self_qkv: bfloat16 [3, 512, 512], P(None, ('dp', 'fsdp')), may hold values from -0.25 to 0.25
- self_out: bfloat16 [512, 512], P(('dp', 'fsdp')), may hold values from -1 to 1
- cross_qkv: bfloat16 [3, 512, 512], P(None, ('dp', 'fsdp')), may hold values from -0.25 to 0.25
- cross_out: bfloat16 [512, 512], P(('dp', 'fsdp')), may hold values from -1 to 1
- ffn_in: bfloat16 [512, 2048], P(('dp', 'fsdp')), may hold values from -0.25 to 0.25
- ffn_out: bfloat16 [2048, 512], P(('dp', 'fsdp')), may hold values from -0.1875 to 0.1875
- ln_gain: bfloat16 [3, 512], P(None, ('dp', 'fsdp')), may hold values from 0.5 to 1.5
- ln_bias: bfloat16 [3, 512], P(None, ('dp', 'fsdp')), may hold values from -3 to 3
- tgt_lengths: int32 [32, 16], P(('dp', 'fsdp')), may hold values from 1 to 640, 1024 in all within a row
- tgt_pad: int32 [32], P(('dp', 'fsdp')), may hold values from 0 to 128
- src_segments: int32 [32, 1024], P(('dp', 'fsdp')), may hold values from 0 to 15, never falling along the last dimension, each value on 1 to 640 neighbouring positions
Outputs:
- out_tokens: bfloat16 [32, 1024, 512], P(('dp', 'fsdp'))
- tokens_grad: bfloat16 [32, 1024, 512], P(('dp', 'fsdp'))
- encoder_grad: bfloat16 [32, 1024, 512], P(('dp', 'fsdp'))
- self_qkv_grad: float32 [3, 512, 512], P(None, ('dp', 'fsdp'))
- self_out_grad: float32 [512, 512], P(('dp', 'fsdp'))
- cross_qkv_grad: float32 [3, 512, 512], P(None, ('dp', 'fsdp'))
- cross_out_grad: float32 [512, 512], P(('dp', 'fsdp'))
- ffn_in_grad: float32 [512, 2048], P(('dp', 'fsdp'))
- ffn_out_grad: float32 [2048, 512], P(('dp', 'fsdp'))
- ln_gain_grad: float32 [3, 512], P(None, ('dp', 'fsdp'))
- ln_bias_grad: float32 [3, 512], P(None, ('dp', 'fsdp'))
The draws below stay inside these ranges and needn't reach their ends.
All inputs are finite; a program needn't handle non-finite values.
Results may differ from the reference program's by a relative error of at most 0.023.
The reference program's roundings to bfloat16 on the way count: a program that leaves them out, or rounds other values in their place, can miss the bound.
Values may be sent and summed in bfloat16 or wider, within the bound.
No kernel may reach another device: no remote copies, remote signals or barrier semaphores. Data moves between devices by JAX's collectives and lax.ppermute only.
A program may use at most 192 MiB of HBM per device.

```python
import math
import jax
import jax.numpy as jnp
import numpy as np
from jax import lax

D = 512
HEADS = 8
FF = 2048
HEAD_DIM = 64
ROW = 1024
SRC = 1024
COUNT = 16
DOC_MOST = 640
PAD_MOST = 128
ROWS = 32


def plant(values, stream_key, smallest, top_value):
    spot = [jax.random.randint(jax.random.fold_in(stream_key, axis), (), 0, length) for axis, length in enumerate(values.shape)]
    main_axis = values.shape.index(max(values.shape))
    beside = spot[:main_axis] + [(spot[main_axis] + 1) % values.shape[main_axis]] + spot[main_axis + 1:]
    return values.at[tuple(spot)].set(smallest).at[tuple(beside)].set(top_value)


def raised(values, stream_key, source, target, shards_of, factor):
    def block_of(axis_at):
        return (jnp.arange(values.shape[axis_at]) // (values.shape[axis_at] // shards_of)).reshape((-1,) + (1,) * (values.ndim - 1 - axis_at))

    first = jax.random.permutation(stream_key, shards_of)[block_of(target)]
    second = (block_of(target) + shards_of // 2) % shards_of
    return jnp.where((block_of(source) == first) | (block_of(source) == second), factor * values, values)


def block_levels(own_key, shape, cuts, low, top_value):
    level, own = 1.0, jax.random.fold_in(own_key, 6)
    for dim, shards_of in cuts:
        draws = jnp.exp(jax.random.uniform(jax.random.fold_in(own, dim), (shards_of,), jnp.float32, low / len(cuts), top_value / len(cuts)))
        level = level * jnp.repeat(draws, shape[dim] // shards_of).reshape([-1 if axis == dim else 1 for axis in range(len(shape))])
    return level


def length_profile(count, total, limit, lean):
    loads = [(1 << 20) // math.isqrt(standing ** lean) + 1 for standing in range(2, count + 1)]
    spare, given = total - limit - (count - 1), [1] * (count - 1)
    while spare > 0:
        candidates = [i for i in range(count - 1) if given[i] < limit]
        mass, remaining = sum([loads[i] for i in candidates]), spare
        for i in candidates:
            extra = min(limit - given[i], max(1, remaining * loads[i] // mass), spare)
            given[i] = given[i] + extra
            spare = spare - extra
    return np.array([limit] + given)


def uneven_parts(rng, count, total, limit, slope):
    if count == 2:
        one = jax.random.randint(rng, (), max(1, total - limit), min(limit, total - 1) + 1)
        return jnp.stack([one, total - one])
    sizes = jnp.asarray(length_profile(count, total, limit, slope), jnp.int32)
    twos = (count - 1) // 2
    donor, receiver = sizes[1:1 + 2 * twos:2], sizes[2:2 + 2 * twos:2]
    slack = jnp.minimum(donor - 1, limit - receiver)
    passed = jax.random.randint(jax.random.fold_in(rng, 1), (twos,), 0, 1 << 20) % (slack + 1)
    sizes = sizes.at[1:1 + 2 * twos:2].set(donor - passed).at[2:2 + 2 * twos:2].set(receiver + passed)
    return sizes[jax.random.permutation(jax.random.fold_in(rng, 2), count)]


def scatter_about(own_key, shape, scale, reach, cuts=(), kind=jnp.bfloat16):
    factor_of = block_levels(own_key, shape, cuts, -0.22, 0.18) if cuts else 1.0
    values = jax.random.normal(own_key, shape, jnp.float32) * scale * factor_of
    return jnp.minimum(jnp.maximum(values, -reach), reach).astype(kind)


def noise_with(own_key, extent, scale, reach, pieces, heavy, kind=jnp.bfloat16):
    values = scale * jax.random.normal(own_key, extent, jnp.float32)
    if pieces:
        values = values * block_levels(own_key, extent, pieces, -0.22, 0.18)
    return jnp.clip(raised(values, jax.random.fold_in(own_key, 3), *heavy), -reach, reach).astype(kind)


def setup_inputs(seed: int = 0) -> dict:
    splits = jax.random.split(jax.random.key(seed), 15)
    tokens = scatter_about(splits[0], (ROWS, ROW, D), 1.0, 6.0, ((0, 32),))
    encoder = scatter_about(splits[1], (ROWS, SRC, D), 1.0, 6.0, ((0, 32),))
    out_grad = noise_with(splits[2], (ROWS, ROW, D), 1.0, 6.0, ((0, 32),), (0, 2, 32, 2.75))
    self_qkv = scatter_about(splits[3], (3, D, D), D ** -0.5, 0.25, ((1, 32),))
    self_out = scatter_about(splits[4], (D, D), (D // 16) ** -0.5, 1.0, ((0, 32),))
    cross_qkv = scatter_about(splits[5], (3, D, D), D ** -0.5, 0.25, ((1, 32),))
    cross_out = scatter_about(splits[6], (D, D), (D // 16) ** -0.5, 1.0, ((0, 32),))
    ffn_in = scatter_about(splits[7], (D, FF), D ** -0.5, 0.25, ((0, 32),))
    ffn_out = scatter_about(splits[8], (FF, D), (FF // 2) ** -0.5, 0.1875, ((0, 32),))
    ln_gain = jnp.clip(1.0 + 0.1 * jax.random.normal(splits[9], (3, D), jnp.float32), 0.5, 1.5).astype(jnp.bfloat16)
    ln_bias = scatter_about(splits[10], (3, D), 0.5, 3.0, ((1, 32),))
    tgt_lengths = jax.vmap(lambda own: uneven_parts(own, COUNT, ROW, DOC_MOST, 2))(jax.random.split(splits[11], ROWS)).reshape((ROWS, COUNT)).astype(jnp.int32)
    tgt_pad = plant(jax.random.randint(splits[12], (ROWS,), 0, PAD_MOST + 1), jax.random.fold_in(splits[12], 1), 0, PAD_MOST).astype(jnp.int32)
    src_segments = jax.vmap(lambda own: jnp.searchsorted(jnp.cumsum(uneven_parts(own, COUNT, SRC, DOC_MOST, 2)), jnp.arange(SRC), side="right"))(jax.random.split(splits[13], ROWS)).reshape((ROWS, SRC)).astype(jnp.int32)
    return dict(tokens=tokens, encoder=encoder, out_grad=out_grad, self_qkv=self_qkv, self_out=self_out, cross_qkv=cross_qkv, cross_out=cross_out, ffn_in=ffn_in, ffn_out=ffn_out, ln_gain=ln_gain, ln_bias=ln_bias, tgt_lengths=tgt_lengths, tgt_pad=tgt_pad, src_segments=src_segments)


@jax.custom_vjp
def low(v):
    return lax.optimization_barrier(v.astype(jnp.bfloat16)).astype(jnp.float32)

@jax.custom_vjp
def low_back(v):
    return v

def low_keep(v):
    return (low(v), None)

def low_pass(kept, grad):
    return (grad,)

def back_keep(v):
    return (v, None)

def back_low(kept, grad):
    return (low(grad),)
low.defvjp(low_keep, low_pass)
low_back.defvjp(back_keep, back_low)

def product(left, right):
    return jnp.dot(left, right, precision=lax.Precision.HIGHEST, preferred_element_type=jnp.float32)

def layer_norm(hidden, gain_row, offset):
    center = hidden - lax.optimization_barrier(jnp.mean(hidden, axis=-1, keepdims=True))
    spread = lax.optimization_barrier(jnp.mean(center * center, axis=-1, keepdims=True))
    return center * lax.rsqrt(spread + 1e-05) * gain_row + offset

def attend(queries, key_rows, value_rows, allowed):
    query_count = queries.shape[0]
    key_count = key_rows.shape[0]
    query_heads = queries.reshape(query_count, HEADS, HEAD_DIM)
    key_heads = key_rows.reshape(key_count, HEADS, HEAD_DIM)
    value_heads = value_rows.reshape(key_count, HEADS, HEAD_DIM)
    scores = jnp.einsum('thd,shd->hts', query_heads, key_heads, precision=lax.Precision.HIGHEST)
    scores = low_back(scores * HEAD_DIM ** (-0.5))
    scores = jnp.where(allowed[None], scores, -1e+30)
    weights = low(jax.nn.softmax(scores, axis=-1))
    mixed_out = jnp.einsum('hts,shd->thd', weights, value_heads, precision=lax.Precision.HIGHEST)
    return low_back(low(mixed_out.reshape(query_count, D)))

def forward(tokens_row, encoder_row, self_qkv, self_out, cross_qkv, cross_out, ffn_in, ffn_out, ln_gain, ln_bias, self_allowed, cross_allowed):
    queries = low_back(low(product(tokens_row, self_qkv[0])))
    key_rows = low_back(low(product(tokens_row, self_qkv[1])))
    value_rows = low_back(low(product(tokens_row, self_qkv[2])))
    attended = attend(queries, key_rows, value_rows, self_allowed)
    first_norm = layer_norm(tokens_row + low_back(product(attended, self_out)), ln_gain[0], ln_bias[0])
    first_low = low(first_norm)
    cross_queries = low_back(low(product(first_low, cross_qkv[0])))
    cross_keys = low_back(low(product(encoder_row, cross_qkv[1])))
    cross_values = low_back(low(product(encoder_row, cross_qkv[2])))
    cross_mixed = attend(cross_queries, cross_keys, cross_values, cross_allowed)
    second_norm = layer_norm(first_norm + low_back(product(cross_mixed, cross_out)), ln_gain[1], ln_bias[1])
    second_low = low(second_norm)
    inner_pre = low_back(product(second_low, ffn_in))
    active = low(jax.nn.gelu(inner_pre))
    return layer_norm(second_norm + low_back(product(active, ffn_out)), ln_gain[2], ln_bias[2])

def segment_ids(lengths, padding):
    places = jnp.arange(ROW, dtype=jnp.int32)
    seg_ends = jnp.cumsum(lengths).astype(jnp.int32)
    labels = lax.optimization_barrier(jnp.sum((places[:, None] >= seg_ends[None, :]).astype(jnp.int32), axis=1)).astype(jnp.int32)
    return jnp.where(places < ROW - padding, labels, COUNT).astype(jnp.int32)

def reference(tokens, encoder, out_grad, self_qkv, self_out, cross_qkv, cross_out, ffn_in, ffn_out, ln_gain, ln_bias, tgt_lengths, tgt_pad, src_segments):
    weights = tuple((weight_item.astype(jnp.float32) for weight_item in (self_qkv, self_out, cross_qkv, cross_out, ffn_in, ffn_out, ln_gain, ln_bias)))

    def one_row(summed, row_data):
        tokens_row, encoder_row, cotangent, lengths, padding, source_ids = row_data
        target_ids = segment_ids(lengths, padding)
        cross_ids = jnp.minimum(target_ids, COUNT - 1)
        self_allowed = target_ids[:, None] == target_ids[None, :]
        cross_allowed = cross_ids[:, None] == source_ids[None, :]

        def layer_fn(tokens_in, encoder_in, *params):
            return forward(tokens_in, encoder_in, *params, self_allowed, cross_allowed)
        result, pullback = jax.vjp(layer_fn, tokens_row.astype(jnp.float32), encoder_row.astype(jnp.float32), *weights)
        grad_parts = pullback(cotangent.astype(jnp.float32))
        summed = tuple((running + grad_item for running, grad_item in zip(summed, grad_parts[2:])))
        return (summed, (result.astype(jnp.bfloat16), grad_parts[0].astype(jnp.bfloat16), grad_parts[1].astype(jnp.bfloat16)))
    start_sums = tuple((jnp.zeros(weight_item.shape, jnp.float32) for weight_item in weights))
    summed, row_outs = lax.scan(one_row, start_sums, (tokens, encoder, out_grad, tgt_lengths, tgt_pad, src_segments))
    return (row_outs[0], row_outs[1], row_outs[2], summed[0], summed[1], summed[2], summed[3], summed[4], summed[5], summed[6], summed[7])
```

```python
import math

import jax
import jax.numpy as jnp
from jax import lax
from jax.experimental import pallas as pl
from jax.experimental.pallas import tpu as pltpu
from jax.sharding import PartitionSpec as P

F32 = jnp.float32
BF16 = jnp.bfloat16
HEAD_DIM = 64
PAIR = 2 * HEAD_DIM
TILE = 128
BLOCK = 16
AXES = ("dp", "fsdp")
QUERY_SCALE = math.log2(math.e) / math.sqrt(HEAD_DIM)
MASK_ROWS = 32
MASKED = -1e30
WINDOWS = (2, 4, 6, 8)
VMEM = pl.BlockSpec(memory_space=pltpu.VMEM)
SMEM = pl.BlockSpec(memory_space=pltpu.SMEM)


def dot(left, right):
    return jnp.dot(left, right, preferred_element_type=F32)


def dot_tn(left, right):
    return lax.dot_general(left, right, (((0,), (0,)), ((), ())), preferred_element_type=F32)


def dot_nt(left, right):
    return lax.dot_general(left, right, (((1,), (1,)), ((), ())), preferred_element_type=F32)


def iota(shape, axis):
    return lax.broadcasted_iota(jnp.int32, shape, axis)


def call(body, name, outs, ins, in_smem, micros, scratch=(), out_smem=()):
    return pl.pallas_call(
        body,
        name=name,
        out_shape=[jax.ShapeDtypeStruct(shape, kind) for shape, kind in outs],
        in_specs=[SMEM if at in in_smem else VMEM for at in range(len(ins))],
        out_specs=[SMEM if at in out_smem else VMEM for at in range(len(outs))],
        scratch_shapes=[pltpu.VMEM(shape, kind) for shape, kind in scratch],
        compiler_params=pltpu.CompilerParams(vmem_limit_bytes=56 * 2**20),
        cost_estimate=pl.CostEstimate(flops=int(micros * 1e9), bytes_accessed=0, transcendentals=0),
    )(*ins)


def prep_body(lengths, padding, src_grid, src_column, self_kaug, self_qaug, cross_kaug, cross_qaug, windows):
    rows = self_kaug.shape[0]
    count = lengths.shape[0]
    edge = rows - padding[0]
    ends, total = [], 0
    for at in range(count):
        total = total + lengths[at]
        ends.append(total)

    def labels(places):
        found = sum((places >= end).astype(jnp.int32) for end in ends)
        return jnp.where(places < edge, found, count)

    row_ids = labels(iota((8, rows), 1))[0:1]
    mask_rows = iota((MASK_ROWS, rows), 0)
    self_qaug[...] = jnp.where(row_ids != mask_rows, 1.0, 0.0).astype(BF16)
    cross_qaug[...] = jnp.where(jnp.minimum(row_ids, count - 1) != mask_rows, 1.0, 0.0).astype(BF16)
    lanes = iota((TILE, TILE), 1)
    ones_lanes = jnp.where((lanes >= MASK_ROWS) & (lanes < MASK_ROWS + 3), 1.0, 0.0)
    for tile in range(rows // TILE):
        part = slice(tile * TILE, (tile + 1) * TILE)
        column_ids = labels(iota((TILE, TILE), 0) + tile * TILE)
        self_kaug[part, :] = jnp.where(column_ids == lanes, MASKED, ones_lanes).astype(BF16)
        cross_kaug[part, :] = jnp.where(src_column[part, :] == lanes, MASKED, ones_lanes).astype(BF16)
    for tile in range(rows // TILE):
        first, last = tile * TILE, tile * TILE + TILE - 1
        start, stop, first_id, last_id = 0, edge, 0, 0
        for end in ends:
            start = jnp.where(end <= first, end, start)
            first_id = first_id + jnp.where(end <= first, 1, 0)
            last_id = last_id + jnp.where(end <= last, 1, 0)
        for end in reversed(ends):
            stop = jnp.where(end > last, jnp.minimum(end, edge), stop)
        start = jnp.where(first >= edge, edge, start)
        stop = jnp.where(last >= edge, rows, stop)
        first_id = jnp.where(first < edge, jnp.minimum(first_id, count - 1), count - 1)
        last_id = jnp.where(last < edge, jnp.minimum(last_id, count - 1), count - 1)
        low = start // TILE
        windows[0, tile] = low
        windows[1, tile] = (stop + TILE - 1) // TILE - low
        source = src_grid[...]
        below = jnp.sum(jnp.where(source < first_id, 1, 0))
        upto = jnp.sum(jnp.where(source <= last_id, 1, 0))
        low = below // TILE
        windows[2, tile] = low
        windows[3, tile] = (upto + TILE - 1) // TILE - low


def pair_columns(block):
    upper = iota(block.shape, 0) < HEAD_DIM
    none = jnp.zeros_like(block)
    return jnp.concatenate([jnp.where(upper, block, none), jnp.where(upper, none, block)], axis=1)


def pair_rows(block):
    left = iota(block.shape, 1) < HEAD_DIM
    none = jnp.zeros_like(block)
    return jnp.concatenate([jnp.where(left, block, none), jnp.where(left, none, block)], axis=0)


def twice(block):
    return jnp.concatenate([block, block], axis=1)


def split_three(row):
    first = row.astype(BF16).astype(F32)
    second = (row - first).astype(BF16).astype(F32)
    third = row - first - second
    at = iota((BLOCK, row.shape[1]), 0)
    none = jnp.zeros((BLOCK, row.shape[1]), F32)
    picked = jnp.where(at == 0, first, jnp.where(at == 1, second, jnp.where(at == 2, third, none)))
    return picked.astype(BF16)


def over_windows(windows, row, rows, run):
    tiles = rows // TILE

    def one_tile(tile, _):
        low, width = windows[row, tile], windows[row + 1, tile]
        before = 0
        for most in WINDOWS:
            start = jnp.minimum(low, tiles - most) * TILE

            @pl.when((width > before) & (width <= most))
            def _():
                run(pl.multiple_of(tile * TILE, TILE), pl.multiple_of(start, TILE), most * TILE)

            before = most
        return 0

    lax.fori_loop(0, tiles, one_tile, 0)


def attend(windows, row, queries_t, keys, values_t, kaug, qaug, mixed_t, log_mass):
    rows, width = keys.shape

    def run(query_at, key_at, key_count):
        query_part, key_part = pl.ds(query_at, TILE), pl.ds(key_at, key_count)
        mask_part = twice(qaug[:, query_part])
        empty = jnp.zeros((PAIR - MASK_ROWS, 2 * TILE), BF16)
        key_mask = kaug[key_part, :]
        ones = jnp.ones((BLOCK, key_count), BF16)
        for pair in range(width // PAIR):
            part = slice(pair * PAIR, (pair + 1) * PAIR)
            right = jnp.concatenate([pair_columns(queries_t[part, query_part]), mask_part, empty], axis=0)
            left = jnp.concatenate([keys[key_part, part], key_mask], axis=1)
            scores = dot(left, right)
            peak = jnp.max(scores, axis=0, keepdims=True)
            raised = jnp.exp2(scores - peak).astype(BF16)
            mixed = dot(jnp.concatenate([values_t[part, key_part], ones], axis=0), raised)
            mass = mixed[PAIR : PAIR + 1]
            scale = 1.0 / mass
            logs = peak + jnp.log2(mass)
            for head in range(2):
                spot = slice(head * TILE, (head + 1) * TILE)
                inner = slice(head * HEAD_DIM, (head + 1) * HEAD_DIM)
                outer = slice(pair * PAIR + head * HEAD_DIM, pair * PAIR + (head + 1) * HEAD_DIM)
                mixed_t[outer, query_part] = (mixed[inner, spot] * scale[:, spot]).astype(BF16)
                at = 2 * pair + head
                log_mass[at : at + 1, query_part] = logs[:, spot]

    over_windows(windows, row, rows, run)


def attend_back(
    windows, row, queries, queries_t, keys, keys_t, values, kaug, qaug, log_mass, delta, grad, grad_t,
    query_grad_t, key_grad, value_grad,
):
    rows, width = keys.shape
    key_grad[...] = jnp.zeros_like(key_grad)
    value_grad[...] = jnp.zeros_like(value_grad)

    def run(query_at, key_at, key_count):
        query_part, key_part = pl.ds(query_at, TILE), pl.ds(key_at, key_count)
        mask_part = twice(qaug[:, query_part])
        no_mask = jnp.zeros((MASK_ROWS, 2 * TILE), BF16)
        empty = jnp.zeros((PAIR - MASK_ROWS - BLOCK, 2 * TILE), BF16)
        key_mask = kaug[key_part, :]
        for pair in range(width // PAIR):
            part = slice(pair * PAIR, (pair + 1) * PAIR)
            masses = jnp.concatenate([log_mass[2 * pair + head : 2 * pair + head + 1, query_part] for head in (0, 1)], axis=1)
            deltas = jnp.concatenate([delta[2 * pair + head : 2 * pair + head + 1, query_part] for head in (0, 1)], axis=1)
            right = jnp.concatenate(
                [pair_columns(queries_t[part, query_part]), mask_part, split_three(-masses), empty], axis=0
            )
            probs = jnp.exp2(dot(jnp.concatenate([keys[key_part, part], key_mask], axis=1), right))
            right = jnp.concatenate(
                [pair_columns(grad_t[part, query_part]), no_mask, split_three(-deltas), empty], axis=0
            )
            grad_probs = dot(jnp.concatenate([values[key_part, part], key_mask], axis=1), right)
            grad_scores = (probs * grad_probs).astype(BF16)
            value_grad[key_part, part] += dot(probs.astype(BF16), pair_rows(grad[query_part, part]))
            key_grad[key_part, part] += dot(grad_scores, pair_rows(queries[query_part, part]))
            mixed = dot(keys_t[part, key_part], grad_scores)
            for head in range(2):
                spot = slice(head * TILE, (head + 1) * TILE)
                inner = slice(head * HEAD_DIM, (head + 1) * HEAD_DIM)
                outer = slice(pair * PAIR + head * HEAD_DIM, pair * PAIR + (head + 1) * HEAD_DIM)
                query_grad_t[outer, query_part] = mixed[inner, spot]

    over_windows(windows, row, rows, run)


def row_deltas(mixed_t, grad_t, delta):
    width, rows = mixed_t.shape
    for head in range(width // HEAD_DIM):
        part = slice(head * HEAD_DIM, (head + 1) * HEAD_DIM)
        product = mixed_t[part, :].astype(F32) * grad_t[part, :].astype(F32)
        delta[head : head + 1, :] = jnp.sum(product, axis=0, keepdims=True)


def normalize(hidden):
    center = hidden - jnp.mean(hidden, axis=-1, keepdims=True)
    spread = jnp.mean(center * center, axis=-1, keepdims=True)
    inverse = lax.rsqrt(spread + 1e-05)
    return center * inverse, inverse


def normalize_back(incoming, normal, inverse, gain):
    scaled = incoming * gain
    average = jnp.mean(scaled, axis=-1, keepdims=True)
    along = jnp.mean(scaled * normal, axis=-1, keepdims=True)
    return inverse * (scaled - average - normal * along)


def chunks(rows, step, run):
    def one(at, _):
        run(pl.ds(pl.multiple_of(at * step, step), step))
        return 0

    lax.fori_loop(0, rows // step, one, 0)


def fold_rows(block):
    return jnp.sum(block.reshape(-1, 8, block.shape[1]), axis=0)


def take_blocks(order, low, high, row, target):
    half = low.shape[0]
    for spot in range(2 * half):
        source = low if spot < half else high
        place = pl.multiple_of(order[spot] * BLOCK, BLOCK)
        target[pl.ds(place, BLOCK), :] = source[spot % half, row : row + BLOCK, :]


def put_blocks(place, grads, first, rows_each, row, value):
    for at in range(value.shape[0] // rows_each):
        grads[place[first + at], row : row + rows_each, :] = value[at * rows_each : (at + 1) * rows_each]


def hand_out(grads, keep, send):
    half = keep.shape[0]
    for spot in range(half):
        keep[spot] = grads[spot]
        send[spot] = grads[half + spot]


def self_forward_body(
    tokens, low, high, order, windows, kaug, qaug,
    hidden, queries, keys, values, mixed_t, log_mass, weights,
    queries_t, values_t,
):
    for which in range(4):
        take_blocks(order, low, high, which * BLOCK, weights.at[which])

    def project(part):
        rows = tokens[part, :]
        query_rows = (dot(rows, weights[0]) * QUERY_SCALE).astype(BF16)
        queries[part, :] = query_rows
        queries_t[:, part] = query_rows.T
        keys[part, :] = dot(rows, weights[1]).astype(BF16)
        value_rows = dot(rows, weights[2]).astype(BF16)
        values[part, :] = value_rows
        values_t[:, part] = value_rows.T

    chunks(tokens.shape[0], 256, project)
    attend(windows, 0, queries_t, keys, values_t, kaug, qaug, mixed_t, log_mass)

    def finish(part):
        hidden[part, :] = tokens[part, :].astype(F32) + dot_tn(mixed_t[:, part], weights[3])

    chunks(tokens.shape[0], 256, finish)


def cross_forward_body(
    hidden, encoder, low, high, order, windows, kaug, qaug,
    hidden_two, queries, keys, values, mixed_t, log_mass, weights, scales,
    queries_t, values_t, first,
):
    for which in range(4):
        take_blocks(order, low, high, which * BLOCK, weights.at[which])
    half = low.shape[0]
    gathered = jnp.zeros(scales.shape, F32)
    for spot in range(2 * half):
        source = low if spot < half else high
        block = source[spot % half, 4 * BLOCK : 5 * BLOCK, :].astype(F32)
        gathered = gathered + pltpu.roll(block, order[spot] * BLOCK, 1)
    scales[...] = gathered
    gain, offset = scales[0:1, :], scales[3:4, :]

    def project(part):
        rows = encoder[part, :]
        keys[part, :] = dot(rows, weights[1]).astype(BF16)
        value_rows = dot(rows, weights[2]).astype(BF16)
        values[part, :] = value_rows
        values_t[:, part] = value_rows.T
        normal, _ = normalize(hidden[part, :])
        first_rows = normal * gain + offset
        first[part, :] = first_rows
        query_rows = (dot(first_rows.astype(BF16), weights[0]) * QUERY_SCALE).astype(BF16)
        queries[part, :] = query_rows
        queries_t[:, part] = query_rows.T

    chunks(encoder.shape[0], 256, project)
    attend(windows, 2, queries_t, keys, values_t, kaug, qaug, mixed_t, log_mass)

    def finish(part):
        hidden_two[part, :] = first[part, :] + dot_tn(mixed_t[:, part], weights[3])

    chunks(encoder.shape[0], 256, finish)


def feed_forward_body(
    hidden, out_grad, gathered, cross_mixed_t, scales, place,
    out, grad_two, scale_grads, keep, send,
    inner, outer, inner_t, outer_t, second_low, active, slope, branch, grad_inner, cross_branch, sums, grads,
):
    rows, width = hidden.shape
    wide = outer.shape[0]
    parts = wide // width
    each = wide // (width // BLOCK)
    for block in range(width // BLOCK):
        for part in range(parts):
            inner[block * BLOCK : (block + 1) * BLOCK, part * width : (part + 1) * width] = gathered[
                block, part * BLOCK : (part + 1) * BLOCK, :
            ]
        outer[block * each : (block + 1) * each, :] = gathered[block, parts * BLOCK : parts * BLOCK + each, :]
    for part in range(parts):
        span = slice(part * width, (part + 1) * width)
        inner_t[span, :] = inner[:, span].T
        outer_t[:, span] = outer[span, :].T
    sums[...] = jnp.zeros_like(sums)
    root = math.sqrt(2.0 / math.pi)

    def one(part):
        normal_two, inverse_two = normalize(hidden[part, :])
        second = normal_two * scales[1:2, :] + scales[4:5, :]
        low = second.astype(BF16)
        second_low[part, :] = low
        for at in range(parts):
            span = slice(at * width, (at + 1) * width)
            value = dot(low, inner[:, span])
            square = value * value
            curve = jnp.tanh(root * (value + 0.044715 * (value * square)))
            active[part, span] = (0.5 * value * (1.0 + curve)).astype(BF16)
            slope[:, span] = 0.5 * (1.0 + curve) + (0.5 * root) * value * (1.0 - curve * curve) * (1.0 + 0.134145 * square)
        normal_three, inverse_three = normalize(second + dot(active[part, :], outer[...]))
        out[part, :] = (normal_three * scales[2:3, :] + scales[5:6, :]).astype(BF16)
        incoming = out_grad[part, :].astype(F32)
        sums[2] += fold_rows(incoming * normal_three)
        sums[5] += fold_rows(incoming)
        grad_three = normalize_back(incoming, normal_three, inverse_three, scales[2:3, :])
        grad_low = grad_three.astype(BF16)
        branch[part, :] = grad_low
        for at in range(parts):
            span = slice(at * width, (at + 1) * width)
            grad_inner[part, span] = (dot(grad_low, outer_t[:, span]) * slope[:, span]).astype(BF16)
        grad_second = grad_three + dot(grad_inner[part, :], inner_t[...])
        sums[1] += fold_rows(grad_second * normal_two)
        sums[4] += fold_rows(grad_second)
        result = normalize_back(grad_second, normal_two, inverse_two, scales[1:2, :])
        grad_two[part, :] = result
        cross_branch[part, :] = result.astype(BF16)

    chunks(rows, 256, one)
    for at in range(parts):
        span = slice(at * width, (at + 1) * width)
        value = dot_tn(second_low[...], grad_inner[:, span]).astype(BF16)
        put_blocks(place, grads, 0, BLOCK, at * BLOCK, value)
        value = dot_tn(active[:, span], branch[...]).astype(BF16)
        put_blocks(place, grads, at * width // each, each, parts * BLOCK, value)
    value = dot(cross_mixed_t[...], cross_branch[...]).astype(BF16)
    put_blocks(place, grads, 0, BLOCK, parts * BLOCK + each, value)
    hand_out(grads, keep, send)
    scale_grads[...] = jnp.sum(sums[...], axis=1)


def back_projections(grad_rows, weight, grad, grad_t):
    def one(part):
        value = dot_nt(grad_rows[part, :], weight[...]).astype(BF16)
        grad[part, :] = value
        grad_t[:, part] = value.T

    chunks(grad.shape[0], 256, one)


def round_grads(query_grad_t, key_grad, value_grad, query_low, key_low, value_low):
    def one(part):
        query_low[part, :] = (query_grad_t[:, part] * HEAD_DIM**-0.5).T.astype(BF16)
        key_low[part, :] = (key_grad[part, :] * math.log(2.0)).astype(BF16)
        value_low[part, :] = value_grad[part, :].astype(BF16)

    chunks(key_low.shape[0], 256, one)


def cross_backward_body(
    grad_two, hidden, encoder, weights, scales, queries, keys, values, mixed_t, log_mass, self_mixed_t,
    kaug, qaug, scale_grads, windows, place,
    grad_one, self_branch, key_low, value_low, keep, send,
    branch, first_low, query_low, grad, grad_t, queries_t, keys_t, delta, query_grad_t, key_grad, value_grad, sums, grads,
):
    rows, width = hidden.shape

    def prepare(part):
        branch[part, :] = grad_two[part, :].astype(BF16)
        queries_t[:, part] = queries[part, :].T
        keys_t[:, part] = keys[part, :].T
        normal, _ = normalize(hidden[part, :])
        first_low[part, :] = (normal * scales[0:1, :] + scales[3:4, :]).astype(BF16)

    chunks(rows, 256, prepare)
    back_projections(branch, weights.at[3], grad, grad_t)
    row_deltas(mixed_t, grad_t, delta)
    attend_back(
        windows, 2, queries, queries_t, keys, keys_t, values, kaug, qaug, log_mass, delta, grad, grad_t,
        query_grad_t, key_grad, value_grad,
    )
    round_grads(query_grad_t, key_grad, value_grad, query_low, key_low, value_low)
    sums[...] = jnp.zeros_like(sums)

    def finish(part):
        normal, inverse = normalize(hidden[part, :])
        incoming = grad_two[part, :] + dot_nt(query_low[part, :], weights[0])
        sums[0] += fold_rows(incoming * normal)
        sums[1] += fold_rows(incoming)
        result = normalize_back(incoming, normal, inverse, scales[0:1, :])
        grad_one[part, :] = result
        self_branch[part, :] = result.astype(BF16)

    chunks(rows, 256, finish)
    put_blocks(place, grads, 0, BLOCK, 0, dot_tn(first_low[...], query_low[...]).astype(BF16))
    put_blocks(place, grads, 0, BLOCK, BLOCK, dot_tn(encoder[...], key_low[...]).astype(BF16))
    put_blocks(place, grads, 0, BLOCK, 2 * BLOCK, dot_tn(encoder[...], value_low[...]).astype(BF16))
    put_blocks(place, grads, 0, BLOCK, 3 * BLOCK, dot(self_mixed_t[...], self_branch[...]).astype(BF16))
    at = iota((BLOCK, width), 0)
    own = jnp.sum(sums[...], axis=1)
    below = jnp.concatenate([scale_grads[...], jnp.zeros_like(scale_grads)], axis=0)
    every = jnp.where(at == 0, own[0:1], jnp.where(at == 3, own[1:2], below))
    for block in range(width // BLOCK):
        shift = (width - block * BLOCK) % width
        turned = every if shift == 0 else pltpu.roll(every, shift, 1)
        grads[place[block], 4 * BLOCK : 5 * BLOCK, :] = turned.astype(BF16)
    hand_out(grads, keep, send)


def self_backward_body(
    branch, tokens, weights, queries, keys, values, mixed_t, log_mass, kaug, qaug, windows, place,
    query_low, key_low, value_low, keep, send,
    grad, grad_t, queries_t, keys_t, delta, query_grad_t, key_grad, value_grad, grads,
):
    rows, width = tokens.shape

    def prepare(part):
        queries_t[:, part] = queries[part, :].T
        keys_t[:, part] = keys[part, :].T

    chunks(rows, 256, prepare)
    back_projections(branch, weights.at[3], grad, grad_t)
    row_deltas(mixed_t, grad_t, delta)
    attend_back(
        windows, 0, queries, queries_t, keys, keys_t, values, kaug, qaug, log_mass, delta, grad, grad_t,
        query_grad_t, key_grad, value_grad,
    )
    round_grads(query_grad_t, key_grad, value_grad, query_low, key_low, value_low)
    put_blocks(place, grads, 0, BLOCK, 0, dot_tn(tokens[...], query_low[...]).astype(BF16))
    put_blocks(place, grads, 0, BLOCK, BLOCK, dot_tn(tokens[...], key_low[...]).astype(BF16))
    put_blocks(place, grads, 0, BLOCK, 2 * BLOCK, dot_tn(tokens[...], value_low[...]).astype(BF16))
    hand_out(grads, keep, send)


def input_grads_body(
    grad_one, weights, query_low, key_low, value_low, cross_weights, cross_key_low, cross_value_low,
    tokens_grad, encoder_grad,
):
    def one(part):
        value = dot_nt(query_low[part, :], weights[0])
        value = value + dot_nt(key_low[part, :], weights[1])
        value = value + dot_nt(value_low[part, :], weights[2])
        tokens_grad[part, :] = (grad_one[part, :] + value).astype(BF16)
        value = dot_nt(cross_key_low[part, :], cross_weights[1])
        value = value + dot_nt(cross_value_low[part, :], cross_weights[2])
        encoder_grad[part, :] = value.astype(BF16)

    chunks(grad_one.shape[0], 256, one)


def exchange(value, bit, devices):
    return lax.ppermute(value, AXES, [(at, at ^ (1 << bit)) for at in range(devices)])


def bit_count(devices):
    return devices.bit_length() - 1


def gather_blocks(block, devices):
    held = block[None]
    for bit in reversed(range(1, bit_count(devices))):
        held = jnp.concatenate([held, exchange(held, bit, devices)], axis=0)
    return held, exchange(held, 0, devices)


def gather_plain(block, per, blocks):
    every = lax.all_gather(block, AXES, axis=0, tiled=False)
    parts = every.shape[1] // per
    every = every.reshape(every.shape[0], parts, per, every.shape[2]).transpose(1, 0, 2, 3)
    every = every.reshape(parts, blocks, -1, every.shape[3]).transpose(1, 0, 2, 3)
    every = every.reshape(blocks, -1, every.shape[3])
    return every[: blocks // 2], every[blocks // 2 :]


def scatter_blocks(keep, send, devices):
    for bit in range(bit_count(devices)):
        received = exchange(send, bit, devices)
        total = keep.astype(F32) + received.astype(F32)
        if total.shape[0] > 1:
            half = total.shape[0] // 2
            low = total.astype(BF16)
            keep, send = low[:half], low[half:]
    return total[0]


def add_back(every, parts):
    return lax.psum_scatter(every, AXES, scatter_dimension=0, tiled=True)


def local(
    tokens, encoder, out_grad, self_qkv, self_out, cross_qkv, cross_out, ffn_in, ffn_out, ln_gain, ln_bias,
    tgt_lengths, tgt_pad, src_segments,
):
    devices = lax.axis_size("dp") * lax.axis_size("fsdp")
    me = lax.axis_index(AXES)
    token_rows, encoder_rows = tokens[0], encoder[0]
    rows, width = token_rows.shape
    wide = ffn_in.shape[1]
    own = self_out.shape[0]
    blocks = width // BLOCK
    direct = devices == blocks
    parts = wide // width
    each = wide // blocks
    pairs = width // PAIR
    heads = width // HEAD_DIM

    spots = jnp.arange(blocks, dtype=jnp.int32)
    if direct:
        mirrored = sum(((spots >> bit) & 1) << (bit_count(devices) - 1 - bit) for bit in range(bit_count(devices)))
        order = mirrored ^ me.astype(jnp.int32)
        flipped = spots ^ me.astype(jnp.int32)
        place = sum(((flipped >> bit) & 1) << (bit_count(devices) - 1 - bit) for bit in range(bit_count(devices)))
    else:
        order, place = spots, spots

    self_block = jnp.concatenate([self_qkv.reshape(-1, width), self_out], axis=0)
    scale_rows = jnp.concatenate([ln_gain, ln_bias], axis=0)
    inner_rows = jnp.concatenate([ffn_in[:, at * width : (at + 1) * width] for at in range(parts)], axis=0)
    cross_block = jnp.concatenate([cross_qkv.reshape(-1, width), cross_out], axis=0)
    if direct:
        scale_block = jnp.pad(scale_rows, ((0, BLOCK - scale_rows.shape[0]), (0, width - own)))
        cross_block = jnp.concatenate([cross_block, scale_block], axis=0)
        self_low, self_high = gather_blocks(self_block, devices)
        cross_low, cross_high = gather_blocks(cross_block, devices)
        ffn_all = lax.all_gather(jnp.concatenate([inner_rows, ffn_out], axis=0), AXES, axis=0, tiled=False)
    else:
        self_low, self_high = gather_plain(self_block, own, blocks)
        cross_low, cross_high = gather_plain(cross_block, own, blocks)
        scale_all = lax.all_gather(scale_rows, AXES, axis=1, tiled=True)
        scale_all = scale_all.reshape(-1, blocks, BLOCK).transpose(1, 0, 2)
        scale_all = jnp.pad(scale_all, ((0, 0), (0, BLOCK - scale_all.shape[1]), (0, width - BLOCK)))
        cross_low = jnp.concatenate([cross_low, scale_all[: blocks // 2]], axis=1)
        cross_high = jnp.concatenate([cross_high, scale_all[blocks // 2 :]], axis=1)
        inner_all = jnp.concatenate(gather_plain(inner_rows, own, blocks), axis=0)
        outer_all = jnp.concatenate(gather_plain(ffn_out, ffn_out.shape[0], blocks), axis=0)
        ffn_all = jnp.concatenate([inner_all, outer_all], axis=1)

    square, tall = (rows, width), (width, rows)
    self_kaug, self_qaug, cross_kaug, cross_qaug, windows = call(
        prep_body, "prep",
        [((rows, TILE), BF16), ((MASK_ROWS, rows), BF16), ((rows, TILE), BF16), ((MASK_ROWS, rows), BF16), ((4, rows // TILE), jnp.int32)],
        [tgt_lengths[0], tgt_pad, src_segments[0].reshape(-1, TILE), src_segments[0].reshape(-1, 1)],
        (0, 1), 2, out_smem=(4,),
    )
    saved = [(square, BF16)] * 3 + [(tall, BF16), ((heads, rows), F32), ((4, width, width), BF16)]
    hidden_one, queries, keys, values, mixed_t, log_mass, weights = call(
        self_forward_body, "self_forward", [(square, F32)] + saved,
        [token_rows, self_low, self_high, order, windows, self_kaug, self_qaug],
        (3, 4), 15, [(tall, BF16), (tall, BF16)],
    )
    hidden_two, cross_queries, cross_keys, cross_values, cross_mixed_t, cross_mass, cross_weights, scales = call(
        cross_forward_body, "cross_forward", [(square, F32)] + saved + [((BLOCK, width), F32)],
        [hidden_one, encoder_rows, cross_low, cross_high, order, windows, cross_kaug, cross_qaug],
        (4, 5), 18, [(tall, BF16), (tall, BF16), (square, F32)],
    )
    most = parts * BLOCK + each + BLOCK
    result, grad_two, scale_grads, ffn_keep, ffn_send = call(
        feed_forward_body, "feed_forward",
        [(square, BF16), (square, F32), ((8, width), F32)] + [((blocks // 2, most, width), BF16)] * 2,
        [hidden_two, out_grad[0], ffn_all, cross_mixed_t, scales, place],
        (5,), 30,
        [
            ((width, wide), BF16), ((wide, width), BF16), ((wide, width), BF16), ((width, wide), BF16),
            (square, BF16), ((rows, wide), BF16), ((256, wide), F32), (square, BF16), ((rows, wide), BF16), (square, BF16),
            ((8, 8, width), F32), ((blocks, most, width), BF16),
        ],
    )
    work = [(square, BF16), (tall, BF16), (tall, BF16), (tall, BF16), ((heads, rows), F32), (tall, F32), (square, F32), (square, F32)]
    grad_one, self_branch, cross_key_low, cross_value_low, cross_keep, cross_send = call(
        cross_backward_body, "cross_backward",
        [(square, F32)] + [(square, BF16)] * 3 + [((blocks // 2, 5 * BLOCK, width), BF16)] * 2,
        [
            grad_two, hidden_one, encoder_rows, cross_weights, scales, cross_queries, cross_keys, cross_values,
            cross_mixed_t, cross_mass, mixed_t, cross_kaug, cross_qaug, scale_grads, windows, place,
        ],
        (14, 15), 30,
        [(square, BF16)] * 3 + work + [((2, 8, width), F32), ((blocks, 5 * BLOCK, width), BF16)],
    )
    query_low, key_low, value_low, self_keep, self_send = call(
        self_backward_body, "self_backward",
        [(square, BF16)] * 3 + [((blocks // 2, 3 * BLOCK, width), BF16)] * 2,
        [self_branch, token_rows, weights, queries, keys, values, mixed_t, log_mass, self_kaug, self_qaug, windows, place],
        (10, 11), 30, work + [((blocks, 3 * BLOCK, width), BF16)],
    )
    tokens_grad, encoder_grad = call(
        input_grads_body, "input_grads", [(square, BF16)] * 2,
        [grad_one, weights, query_low, key_low, value_low, cross_weights, cross_key_low, cross_value_low],
        (), 8,
    )
    if direct:
        ffn_sum = scatter_blocks(ffn_keep, ffn_send, devices)
        cross_sum = scatter_blocks(cross_keep, cross_send, devices)
        self_sum = scatter_blocks(self_keep, self_send, devices)
        ffn_in_grad = jnp.concatenate([ffn_sum[at * BLOCK : (at + 1) * BLOCK] for at in range(parts)], axis=1)
        ffn_out_grad = ffn_sum[parts * BLOCK : parts * BLOCK + each]
        cross_out_grad = ffn_sum[parts * BLOCK + each :]
        cross_qkv_grad = cross_sum[: 3 * BLOCK].reshape(3, BLOCK, width)
        self_out_grad = cross_sum[3 * BLOCK : 4 * BLOCK]
        scale_sum = cross_sum[4 * BLOCK : 4 * BLOCK + 6, :BLOCK]
        self_qkv_grad = self_sum.reshape(3, BLOCK, width)
    else:

        def add_up(grads, first, last, per):
            piece = grads[:, first:last].reshape(blocks, -1, per, width).transpose(1, 0, 2, 3)
            piece = piece.reshape(piece.shape[0], blocks * per, width)
            return lax.psum_scatter(piece.astype(F32), AXES, scatter_dimension=1, tiled=True)

        ffn_grads = jnp.concatenate([ffn_keep, ffn_send], axis=0)
        cross_grads = jnp.concatenate([cross_keep, cross_send], axis=0)
        self_grads = jnp.concatenate([self_keep, self_send], axis=0)
        inner_sum = add_up(ffn_grads, 0, parts * BLOCK, BLOCK)
        ffn_in_grad = inner_sum.transpose(1, 0, 2).reshape(own, wide)
        ffn_out_grad = add_up(ffn_grads, parts * BLOCK, parts * BLOCK + each, each)[0]
        cross_out_grad = add_up(ffn_grads, parts * BLOCK + each, most, BLOCK)[0]
        cross_qkv_grad = add_up(cross_grads, 0, 3 * BLOCK, BLOCK)
        self_out_grad = add_up(cross_grads, 3 * BLOCK, 4 * BLOCK, BLOCK)[0]
        scale_parts = cross_grads[:, 4 * BLOCK : 4 * BLOCK + 6, :BLOCK].astype(F32)
        scale_parts = scale_parts.transpose(1, 0, 2).reshape(6, width)
        scale_sum = lax.psum_scatter(scale_parts, AXES, scatter_dimension=1, tiled=True)
        self_qkv_grad = add_up(self_grads, 0, 3 * BLOCK, BLOCK)
    return (
        result[None], tokens_grad[None], encoder_grad[None], self_qkv_grad, self_out_grad, cross_qkv_grad,
        cross_out_grad, ffn_in_grad, ffn_out_grad, scale_sum[:3], scale_sum[3:],
    )


def solution(mesh):
    rows, first, second = P(AXES, None, None), P(AXES, None), P(None, AXES, None)
    columns = P(None, AXES)
    in_specs = (
        rows, rows, rows, second, first, second, first, first, first, columns, columns, first, P(AXES), first,
    )
    out_specs = (rows, rows, rows, second, first, second, first, first, first, columns, columns)
    return jax.shard_map(local, mesh=mesh, in_specs=in_specs, out_specs=out_specs, check_vma=False)
```

```python
import math

import jax
import jax.numpy as jnp
from jax import lax
from jax.experimental import pallas as pl
from jax.experimental.pallas import tpu as pltpu
from jax.sharding import PartitionSpec as P

F32 = jnp.float32
BF16 = jnp.bfloat16
HEAD_DIM = 64
PAIR = 2 * HEAD_DIM
TILE = 128
BLOCK = 16
AXES = ("dp", "fsdp")
QUERY_SCALE = math.log2(math.e) / math.sqrt(HEAD_DIM)
MASK_ROWS = 32
MASKED = -1e30
WINDOWS = (2, 4, 6, 8)
SMEM = pl.BlockSpec(memory_space=pltpu.SMEM)
ANYWHERE = pl.BlockSpec(memory_space=pl.ANY)
HBM = pl.BlockSpec(memory_space=pltpu.HBM)
VMEM = pl.BlockSpec(memory_space=pltpu.VMEM)


def dot(left, right):
    return jnp.dot(left, right, preferred_element_type=F32)


def dot_tn(left, right):
    return lax.dot_general(left, right, (((0,), (0,)), ((), ())), preferred_element_type=F32)


def dot_nt(left, right):
    return lax.dot_general(left, right, (((1,), (1,)), ((), ())), preferred_element_type=F32)


def iota(shape, axis):
    return lax.broadcasted_iota(jnp.int32, shape, axis)


def part_shape(shape, index):
    if index is None:
        return shape
    index = index if isinstance(index, tuple) else (index,)
    taken = [one.stop - one.start for one in index if isinstance(one, slice)]
    return (*taken, *shape[len(index) :])


class Copies:

    def __init__(self, semaphores):
        self.semaphores = semaphores
        self.used = 0
        self.coming = {}
        self.going = {}
        self.started = []

    def start(self, source, target):
        copy = pltpu.make_async_copy(source, target, self.semaphores.at[self.used])
        self.used += 1
        copy.start()
        return copy

    def need(self, *refs):
        for ref in refs:
            self.coming.pop(id(ref)).wait()

    def push(self, *refs):
        for ref in refs:
            self.started.append(self.start(ref, self.going.pop(id(ref))))

    def push_part(self, source, target):
        self.started.append(self.start(source, target))

    def finish(self):
        for copy in self.coming.values():
            copy.wait()
        for copy in self.started:
            copy.wait()


def call(body, name, outs, ins, in_smem, micros, scratch=(), out_smem=(), after=(), by_part=(), near=(), limit=58):
    ins = [one if isinstance(one, tuple) else (one, None) for one in ins]
    indexes = [index for _, index in ins]
    ins = [array for array, _ in ins]
    in_count, out_count = len(ins), len(outs)
    moved_in = [at for at in range(in_count) if at not in in_smem and at not in near]
    moved_out = [at for at in range(out_count) if at not in out_smem and at not in by_part]

    def ordered(*refs):
        sources, refs = list(refs[:in_count]), refs[in_count + len(after) :]
        targets, refs = list(refs[:out_count]), refs[out_count:]
        buffers_in, refs = refs[: len(moved_in)], refs[len(moved_in) :]
        buffers_out, refs = refs[: len(moved_out)], refs[len(moved_out) :]
        copies = Copies(refs[0])
        for at, buffer in zip(moved_in, buffers_in):
            source = sources[at] if indexes[at] is None else sources[at].at[indexes[at]]
            copies.coming[id(buffer)] = copies.start(source, buffer)
            sources[at] = buffer
        for at, buffer in zip(moved_out, buffers_out):
            copies.going[id(buffer)] = targets[at]
            targets[at] = buffer
        body(copies, *sources, *targets, *refs[1:])
        copies.finish()

    return pl.pallas_call(
        ordered,
        name=name,
        out_shape=[jax.ShapeDtypeStruct(shape, kind) for shape, kind in outs],
        in_specs=[SMEM if at in in_smem else VMEM if at in near else HBM for at in range(in_count)] + [ANYWHERE] * len(after),
        out_specs=[SMEM if at in out_smem else HBM for at in range(out_count)],
        scratch_shapes=[pltpu.VMEM(part_shape(ins[at].shape, indexes[at]), ins[at].dtype) for at in moved_in]
        + [pltpu.VMEM(*outs[at]) for at in moved_out]
        + [pltpu.SemaphoreType.DMA((len(moved_in) + len(moved_out) + 4 * len(by_part),))]
        + [pltpu.VMEM(shape, kind) for shape, kind in scratch],
        compiler_params=pltpu.CompilerParams(vmem_limit_bytes=limit * 2**20),
        cost_estimate=pl.CostEstimate(flops=int(micros * 1e9), bytes_accessed=0, transcendentals=0),
    )(*ins, *after)


def call_near(body, name, outs, ins, micros, after=()):
    count = len(ins)
    return pl.pallas_call(
        lambda *refs: body(*refs[:count], *refs[count + len(after) :]),
        name=name,
        out_shape=[jax.ShapeDtypeStruct(shape, kind) for shape, kind in outs],
        in_specs=[VMEM] * count + [ANYWHERE] * len(after),
        out_specs=[VMEM] * len(outs),
        compiler_params=pltpu.CompilerParams(vmem_limit_bytes=16 * 2**20),
        cost_estimate=pl.CostEstimate(flops=int(micros * 1e9), bytes_accessed=0, transcendentals=0),
    )(*ins, *after)


def prep_body(copies, lengths, padding, src_grid, src_column, self_kaug, self_qaug, cross_kaug, cross_qaug, windows, zero):
    zero[0] = 0
    copies.need(src_grid, src_column)
    rows = self_kaug.shape[0]
    count = lengths.shape[0]
    edge = rows - padding[0]
    ends, total = [], 0
    for at in range(count):
        total = total + lengths[at]
        ends.append(total)

    def labels(places):
        found = sum((places >= end).astype(jnp.int32) for end in ends)
        return jnp.where(places < edge, found, count)

    row_ids = labels(iota((8, rows), 1))[0:1]
    mask_rows = iota((MASK_ROWS, rows), 0)
    self_qaug[...] = jnp.where(row_ids != mask_rows, 1.0, 0.0).astype(BF16)
    cross_qaug[...] = jnp.where(jnp.minimum(row_ids, count - 1) != mask_rows, 1.0, 0.0).astype(BF16)
    lanes = iota((TILE, TILE), 1)
    ones_lanes = jnp.where((lanes >= MASK_ROWS) & (lanes < MASK_ROWS + 3), 1.0, 0.0)
    for tile in range(rows // TILE):
        part = slice(tile * TILE, (tile + 1) * TILE)
        column_ids = labels(iota((TILE, TILE), 0) + tile * TILE)
        self_kaug[part, :] = jnp.where(column_ids == lanes, MASKED, ones_lanes).astype(BF16)
        cross_kaug[part, :] = jnp.where(src_column[part, :] == lanes, MASKED, ones_lanes).astype(BF16)
    copies.push(self_kaug, self_qaug, cross_kaug, cross_qaug)
    for tile in range(rows // TILE):
        first, last = tile * TILE, tile * TILE + TILE - 1
        start, stop, first_id, last_id = 0, edge, 0, 0
        for end in ends:
            start = jnp.where(end <= first, end, start)
            first_id = first_id + jnp.where(end <= first, 1, 0)
            last_id = last_id + jnp.where(end <= last, 1, 0)
        for end in reversed(ends):
            stop = jnp.where(end > last, jnp.minimum(end, edge), stop)
        start = jnp.where(first >= edge, edge, start)
        stop = jnp.where(last >= edge, rows, stop)
        first_id = jnp.where(first < edge, jnp.minimum(first_id, count - 1), count - 1)
        last_id = jnp.where(last < edge, jnp.minimum(last_id, count - 1), count - 1)
        low = start // TILE
        windows[0, tile] = low
        windows[1, tile] = (stop + TILE - 1) // TILE - low
        source = src_grid[...]
        below = jnp.sum(jnp.where(source < first_id, 1, 0))
        upto = jnp.sum(jnp.where(source <= last_id, 1, 0))
        low = below // TILE
        windows[2, tile] = low
        windows[3, tile] = (upto + TILE - 1) // TILE - low


def pair_columns(block):
    upper = iota(block.shape, 0) < HEAD_DIM
    none = jnp.zeros_like(block)
    return jnp.concatenate([jnp.where(upper, block, none), jnp.where(upper, none, block)], axis=1)


def pair_rows(block):
    left = iota(block.shape, 1) < HEAD_DIM
    none = jnp.zeros_like(block)
    return jnp.concatenate([jnp.where(left, block, none), jnp.where(left, none, block)], axis=0)


def twice(block):
    return jnp.concatenate([block, block], axis=1)


def split_three(row):
    first = row.astype(BF16).astype(F32)
    second = (row - first).astype(BF16).astype(F32)
    third = row - first - second
    at = iota((BLOCK, row.shape[1]), 0)
    none = jnp.zeros((BLOCK, row.shape[1]), F32)
    picked = jnp.where(at == 0, first, jnp.where(at == 1, second, jnp.where(at == 2, third, none)))
    return picked.astype(BF16)


def over_windows(windows, row, rows, run):
    tiles = rows // TILE

    def one_tile(tile, _):
        low, width = windows[row, tile], windows[row + 1, tile]
        before = 0
        for most in WINDOWS:
            start = jnp.minimum(low, tiles - most) * TILE

            @pl.when((width > before) & (width <= most))
            def _():
                run(pl.multiple_of(tile * TILE, TILE), pl.multiple_of(start, TILE), most * TILE)

            before = most
        return 0

    lax.fori_loop(0, tiles, one_tile, 0)


def places(pair):
    inner = (pair % 2) * PAIR
    return pair // 2, slice(inner, inner + PAIR)


def head_places(pair, head):
    inner = (pair % 2) * PAIR + head * HEAD_DIM
    return pair // 2, slice(inner, inner + HEAD_DIM), slice((pair % 2) * 2 + head, (pair % 2) * 2 + head + 1)


def attend(windows, row, queries_t, keys, values_t, kaug, qaug, mixed_t, log_mass, scores, raised):
    halves, rows, width = keys.shape
    pairs = halves * width // PAIR

    def run(query_at, key_at, key_count):
        query_part, key_part = pl.ds(query_at, TILE), pl.ds(key_at, key_count)
        mask_part = twice(qaug[:, query_part])
        empty = jnp.zeros((PAIR - MASK_ROWS, 2 * TILE), BF16)
        ones = jnp.ones((BLOCK, key_count), BF16)
        rights, found, peaks = [], [None] * pairs, [None] * pairs
        for pair in range(pairs):
            half, part = places(pair)
            rights.append(jnp.concatenate([pair_columns(queries_t[half, part, query_part]), mask_part, empty], axis=0))

        def score(pair, at):
            half, part = places(pair)
            here, span = pl.ds(key_at + at, TILE * 2), slice(at, at + TILE * 2)
            value = dot(jnp.concatenate([keys[half, here, part], kaug[here, :]], axis=1), rights[pair])
            scores[pair % 2, span, :] = value
            most = jnp.max(value.reshape(-1, 8, 2 * TILE), axis=0)
            found[pair] = most if at == 0 else jnp.maximum(found[pair], most)

        def raise_up(pair, at):
            span = slice(at, at + TILE * 2)
            if at == 0:
                peaks[pair] = jnp.max(found[pair], axis=0, keepdims=True)
            raised[pair % 2, span, :] = jnp.exp2(scores[pair % 2, span, :] - peaks[pair]).astype(BF16)

        def mix(pair):
            half, part = places(pair)
            left = jnp.concatenate([values_t[half, part, key_part], ones], axis=0)
            mixed = dot(left, raised[pair % 2, 0:key_count, :])
            mass = mixed[PAIR : PAIR + 1]
            scale = 1.0 / mass
            logs = peaks[pair] + jnp.log2(mass)
            for head in range(2):
                spot = slice(head * TILE, (head + 1) * TILE)
                inner = slice(head * HEAD_DIM, (head + 1) * HEAD_DIM)
                half, outer, at = head_places(pair, head)
                mixed_t[half, outer, query_part] = (mixed[inner, spot] * scale[:, spot]).astype(BF16)
                log_mass[half, at, query_part] = logs[:, spot]

        for step in range(pairs + 2):
            for at in range(0, key_count, TILE * 2):
                if step < pairs:
                    score(step, at)
                if 0 <= step - 1 < pairs:
                    raise_up(step - 1, at)
                if at == 0 and 0 <= step - 2 < pairs:
                    mix(step - 2)

    over_windows(windows, row, rows, run)


def attend_back(
    windows, row, queries, queries_t, keys, keys_t, values, kaug, qaug, log_mass, delta, grad, grad_t,
    query_grad_t, key_grad, value_grad,
):
    halves, rows, width = keys.shape
    key_grad[...] = jnp.zeros_like(key_grad)
    value_grad[...] = jnp.zeros_like(value_grad)

    def run(query_at, key_at, key_count):
        query_part, key_part = pl.ds(query_at, TILE), pl.ds(key_at, key_count)
        mask_part = twice(qaug[:, query_part])
        no_mask = jnp.zeros((MASK_ROWS, 2 * TILE), BF16)
        empty = jnp.zeros((PAIR - MASK_ROWS - BLOCK, 2 * TILE), BF16)
        key_mask = kaug[key_part, :]
        for pair in range(halves * width // PAIR):
            half, part = places(pair)
            heads = [head_places(pair, head) for head in range(2)]
            masses = jnp.concatenate([log_mass[half, at, query_part] for half, _, at in heads], axis=1)
            deltas = jnp.concatenate([delta[half, at, query_part] for half, _, at in heads], axis=1)
            right = jnp.concatenate(
                [pair_columns(queries_t[half, part, query_part]), mask_part, split_three(-masses), empty], axis=0
            )
            probs = jnp.exp2(dot(jnp.concatenate([keys[half, key_part, part], key_mask], axis=1), right))
            right = jnp.concatenate(
                [pair_columns(grad_t[half, part, query_part]), no_mask, split_three(-deltas), empty], axis=0
            )
            grad_probs = dot(jnp.concatenate([values[half, key_part, part], key_mask], axis=1), right)
            grad_scores = (probs * grad_probs).astype(BF16)
            value_grad[half, key_part, part] += dot(probs.astype(BF16), pair_rows(grad[half, query_part, part]))
            key_grad[half, key_part, part] += dot(grad_scores, pair_rows(queries[half, query_part, part]))
            mixed = dot(keys_t[half, part, key_part], grad_scores)
            for head, (half, outer, _) in enumerate(heads):
                spot = slice(head * TILE, (head + 1) * TILE)
                inner = slice(head * HEAD_DIM, (head + 1) * HEAD_DIM)
                query_grad_t[half, outer, query_part] = mixed[inner, spot]

    over_windows(windows, row, rows, run)


def row_deltas(mixed_t, grad_t, delta):
    halves, width, rows = mixed_t.shape
    for half in range(halves):
        for head in range(width // HEAD_DIM):
            part = slice(head * HEAD_DIM, (head + 1) * HEAD_DIM)
            product = mixed_t[half, part, :].astype(F32) * grad_t[half, part, :].astype(F32)
            delta[half, head : head + 1, :] = jnp.sum(product, axis=0, keepdims=True)


def normalize(hidden):
    center = hidden - jnp.mean(hidden, axis=-1, keepdims=True)
    spread = jnp.mean(center * center, axis=-1, keepdims=True)
    inverse = lax.rsqrt(spread + 1e-05)
    return center * inverse, inverse


def normalize_back(incoming, normal, inverse, gain):
    scaled = incoming * gain
    average = jnp.mean(scaled, axis=-1, keepdims=True)
    along = jnp.mean(scaled * normal, axis=-1, keepdims=True)
    return inverse * (scaled - average - normal * along)


def chunks(rows, step, run):
    def one(at, _):
        run(pl.ds(pl.multiple_of(at * step, step), step))
        return 0

    lax.fori_loop(0, rows // step, one, 0)


def fold_rows(block):
    return jnp.sum(block.reshape(-1, 8, block.shape[1]), axis=0)


def mirrored(number):
    return sum(((number >> bit) & 1) << (4 - bit) for bit in range(5))


def origin(spots, spot):
    return jnp.where(spots[0] == 1, mirrored(spot) ^ spots[1], spot)


def place(spots, block):
    return jnp.where(spots[0] == 1, mirrored(block) ^ spots[2], block)


def take_blocks(spots, low, high, row, target):
    half = low.shape[0]
    for spot in range(2 * half):
        source = low if spot < half else high
        start = pl.multiple_of(origin(spots, spot) * BLOCK, BLOCK)
        target[pl.ds(start, BLOCK), :] = source[spot % half, row : row + BLOCK, :]


def put_blocks(spots, grads, first, rows_each, row, value):
    for at in range(value.shape[0] // rows_each):
        grads[place(spots, first + at), row : row + rows_each, :] = value[at * rows_each : (at + 1) * rows_each]


def hand_out(copies, grads, keep, send):
    half = keep.shape[0]
    copies.push_part(grads.at[half : 2 * half], send)
    copies.push_part(grads.at[0:half], keep)


def pack_body(copies, self_qkv, self_out, cross_qkv, cross_out, ffn_in, ffn_out, gain, offset, self_block, cross_block, ffn_block):
    copies.need(self_qkv, self_out, cross_qkv, cross_out, ffn_in, ffn_out, gain, offset)
    width = self_out.shape[1]
    own = gain.shape[1]
    for which in range(3):
        rows = slice(which * BLOCK, (which + 1) * BLOCK)
        self_block[0, rows, :] = self_qkv[which]
        cross_block[0, rows, :] = cross_qkv[which]
    cross_block[0, 3 * BLOCK : 4 * BLOCK, :] = cross_out[...]
    cross_block[0, 4 * BLOCK : 5 * BLOCK, :] = self_out[...]
    scales = jnp.concatenate([gain[...].astype(F32), offset[...].astype(F32), jnp.zeros((BLOCK - 6, own), F32)], axis=0)
    scales = jnp.concatenate([scales, jnp.zeros((BLOCK, width - own), F32)], axis=1)
    cross_block[0, 5 * BLOCK : 6 * BLOCK, :] = scales.astype(BF16)
    parts = ffn_in.shape[1] // width
    for part in range(parts):
        ffn_block[part * BLOCK : (part + 1) * BLOCK, :] = ffn_in[:, part * width : (part + 1) * width]
    ffn_block[parts * BLOCK :, :] = ffn_out[...]
    copies.push(self_block, cross_block, ffn_block)


def lay_rows(value, target, part):
    wide = target.shape[2]
    for half in range(target.shape[0]):
        target[half, part, :] = value[:, half * wide : (half + 1) * wide]


def lay_columns(value, target, part):
    wide = target.shape[1]
    turned = value.T
    for half in range(target.shape[0]):
        target[half, :, part] = turned[half * wide : (half + 1) * wide]


def mixed_product(mixed_t, part, weight):
    wide = mixed_t.shape[1]
    return sum(dot_tn(mixed_t[half, :, part], weight[half * wide : (half + 1) * wide, :]) for half in range(mixed_t.shape[0]))


def self_forward_body(
    copies, low, high, tokens, kaug, qaug, spots, windows,
    queries, queries_t, keys, keys_t, values, mixed_t, log_mass, weights, zero,
    values_t, scores, raised,
):
    zero[0] = 0
    for which in range(3):
        take_blocks(spots, low, high, which * BLOCK, weights.at[which])
    copies.push(weights)
    copies.need(tokens)

    def project(part):
        rows = tokens[part, :]
        query_rows = (dot(rows, weights[0]) * QUERY_SCALE).astype(BF16)
        lay_rows(query_rows, queries, part)
        lay_columns(query_rows, queries_t, part)
        key_rows = dot(rows, weights[1]).astype(BF16)
        lay_rows(key_rows, keys, part)
        lay_columns(key_rows, keys_t, part)
        value_rows = dot(rows, weights[2]).astype(BF16)
        lay_rows(value_rows, values, part)
        lay_columns(value_rows, values_t, part)

    chunks(tokens.shape[0], 256, project)
    copies.push(queries, queries_t, keys, keys_t, values)
    copies.need(kaug, qaug)
    attend(windows, 0, queries_t, keys, values_t, kaug, qaug, mixed_t, log_mass, scores, raised)
    copies.push(mixed_t, log_mass)


def cross_forward_body(
    copies, low, high, tokens, self_mixed_t, encoder, kaug, qaug, spots, windows,
    hidden, hidden_two, first_low, queries, queries_t, keys, keys_t, values, mixed_t, log_mass, weights, scales,
    values_t, scores, raised, first,
):
    for which in range(5):
        take_blocks(spots, low, high, which * BLOCK, weights.at[which])
    half = low.shape[0]
    gathered = jnp.zeros(scales.shape, F32)
    for spot in range(2 * half):
        source = low if spot < half else high
        block = source[spot % half, 5 * BLOCK : 6 * BLOCK, :].astype(F32)
        gathered = gathered + pltpu.roll(block, origin(spots, spot) * BLOCK, 1)
    scales[...] = gathered
    copies.push(weights, scales)
    gain, offset = scales[0:1, :], scales[3:4, :]
    copies.need(tokens, self_mixed_t, encoder)

    def project(part):
        rows = encoder[part, :]
        key_rows = dot(rows, weights[1]).astype(BF16)
        lay_rows(key_rows, keys, part)
        lay_columns(key_rows, keys_t, part)
        value_rows = dot(rows, weights[2]).astype(BF16)
        lay_rows(value_rows, values, part)
        lay_columns(value_rows, values_t, part)
        before = tokens[part, :].astype(F32) + mixed_product(self_mixed_t, part, weights.at[4])
        hidden[part, :] = before
        normal, _ = normalize(before)
        first_rows = normal * gain + offset
        first[part, :] = first_rows
        low_rows = first_rows.astype(BF16)
        first_low[part, :] = low_rows
        query_rows = (dot(low_rows, weights[0]) * QUERY_SCALE).astype(BF16)
        lay_rows(query_rows, queries, part)
        lay_columns(query_rows, queries_t, part)

    chunks(encoder.shape[0], 256, project)
    copies.push(hidden, first_low, queries, queries_t, keys, keys_t, values)
    copies.need(kaug, qaug)
    attend(windows, 2, queries_t, keys, values_t, kaug, qaug, mixed_t, log_mass, scores, raised)
    copies.push(mixed_t, log_mass)

    def finish(part):
        hidden_two[part, :] = first[part, :] + mixed_product(mixed_t, part, weights.at[3])

    chunks(encoder.shape[0], 256, finish)
    copies.push(hidden_two)


def feed_forward_body(
    copies, gathered, hidden, out_grad, scales, cross_mixed_t, spots,
    out, grad_two, scale_grads, weight_grads,
    inner, outer, inner_t, outer_t, second_low, active, slope, branch, grad_inner, cross_branch, sums, grads,
):
    rows, width = hidden.shape
    wide = outer.shape[0]
    parts = wide // width
    each = wide // (width // BLOCK)
    copies.need(gathered)
    for block in range(width // BLOCK):
        for part in range(parts):
            inner[block * BLOCK : (block + 1) * BLOCK, part * width : (part + 1) * width] = gathered[
                block, part * BLOCK : (part + 1) * BLOCK, :
            ]
        outer[block * each : (block + 1) * each, :] = gathered[block, parts * BLOCK : parts * BLOCK + each, :]
    for part in range(parts):
        span = slice(part * width, (part + 1) * width)
        inner_t[span, :] = inner[:, span].T
        outer_t[:, span] = outer[span, :].T
    sums[...] = jnp.zeros_like(sums)
    root = math.sqrt(2.0 / math.pi)
    copies.need(hidden, out_grad, scales)

    def one(part):
        normal_two, inverse_two = normalize(hidden[part, :])
        second = normal_two * scales[1:2, :] + scales[4:5, :]
        low = second.astype(BF16)
        second_low[part, :] = low
        for at in range(parts):
            span = slice(at * width, (at + 1) * width)
            value = dot(low, inner[:, span])
            square = value * value
            curve = jnp.tanh(root * (value + 0.044715 * (value * square)))
            active[part, span] = (0.5 * value * (1.0 + curve)).astype(BF16)
            slope[:, span] = 0.5 * (1.0 + curve) + (0.5 * root) * value * (1.0 - curve * curve) * (1.0 + 0.134145 * square)
        normal_three, inverse_three = normalize(second + dot(active[part, :], outer[...]))
        out[part, :] = (normal_three * scales[2:3, :] + scales[5:6, :]).astype(BF16)
        incoming = out_grad[part, :].astype(F32)
        sums[2] += fold_rows(incoming * normal_three)
        sums[5] += fold_rows(incoming)
        grad_three = normalize_back(incoming, normal_three, inverse_three, scales[2:3, :])
        grad_low = grad_three.astype(BF16)
        branch[part, :] = grad_low
        for at in range(parts):
            span = slice(at * width, (at + 1) * width)
            grad_inner[part, span] = (dot(grad_low, outer_t[:, span]) * slope[:, span]).astype(BF16)
        grad_second = grad_three + dot(grad_inner[part, :], inner_t[...])
        sums[1] += fold_rows(grad_second * normal_two)
        sums[4] += fold_rows(grad_second)
        result = normalize_back(grad_second, normal_two, inverse_two, scales[1:2, :])
        grad_two[part, :] = result
        cross_branch[part, :] = result.astype(BF16)

    chunks(rows, 256, one)
    scale_grads[...] = jnp.sum(sums[...], axis=1)
    copies.push(out, grad_two, scale_grads)
    inside = parts * BLOCK

    def put(first, rows_each, row, value):
        for at in range(value.shape[0] // rows_each):
            block = first + at
            spot = jnp.where(spots[0] == 1, (block % 8) * 4 + block // 8, block)
            grads[spot, row : row + rows_each, :] = value[at * rows_each : (at + 1) * rows_each]

    for at in range(parts):
        span = slice(at * width, (at + 1) * width)
        put(at * width // each, each, inside + BLOCK, dot_tn(active[:, span], branch[...]).astype(BF16))
    for at in range(parts):
        span = slice(at * width, (at + 1) * width)
        put(0, BLOCK, at * BLOCK, dot_tn(second_low[...], grad_inner[:, span]).astype(BF16))
    copies.push_part(grads.at[:, 0:inside, :], weight_grads.at[:, 0:inside, :])
    copies.push_part(grads.at[:, inside + BLOCK :, :], weight_grads.at[:, inside + BLOCK :, :])
    copies.need(cross_mixed_t)
    half_width = cross_mixed_t.shape[1]
    for half in range(cross_mixed_t.shape[0]):
        put(half * half_width // BLOCK, BLOCK, inside, dot(cross_mixed_t[half], cross_branch[...]).astype(BF16))
    copies.push_part(grads.at[:, inside : inside + BLOCK, :], weight_grads.at[:, inside : inside + BLOCK, :])


def back_projections(grad_rows, weight, grad, grad_t):
    def one(part):
        value = dot_nt(grad_rows[part, :], weight[...]).astype(BF16)
        lay_rows(value, grad, part)
        lay_columns(value, grad_t, part)

    chunks(grad.shape[1], 256, one)


def round_grads(query_grad_t, key_grad, value_grad, query_low, key_low, value_low):
    def one(part):
        for half in range(key_low.shape[0]):
            query_low[half, part, :] = (query_grad_t[half, :, part] * HEAD_DIM**-0.5).T.astype(BF16)
            key_low[half, part, :] = (key_grad[half, part, :] * math.log(2.0)).astype(BF16)
            value_low[half, part, :] = value_grad[half, part, :].astype(BF16)

    chunks(key_low.shape[1], 256, one)


def back_product(low, part, weight):
    wide = low.shape[2]
    return sum(dot_nt(low[half, part, :], weight[:, half * wide : (half + 1) * wide]) for half in range(low.shape[0]))


def weight_grad(spots, grads, row, left, low):
    wide = low.shape[2]
    for half in range(low.shape[0]):
        value = dot_tn(left[...], low[half]).astype(BF16)
        span = slice(half * wide, (half + 1) * wide)
        for at in range(value.shape[0] // BLOCK):
            grads[place(spots, at), row : row + BLOCK, span] = value[at * BLOCK : (at + 1) * BLOCK]


def cross_backward_body(
    copies, grad_two, out_weight, mixed_t, queries_t, keys, kaug, qaug, values, log_mass, queries, keys_t,
    query_weight, scales, hidden, first_low, encoder, self_mixed_t, scale_grads, windows, spots,
    grad_one, self_branch, key_low, value_low, keep, send,
    branch, query_low, grad, grad_t, delta, query_grad_t, key_grad, value_grad, sums, grads,
):
    rows, width = hidden.shape
    copies.need(grad_two, out_weight)

    def prepare(part):
        branch[part, :] = grad_two[part, :].astype(BF16)

    chunks(rows, 256, prepare)
    back_projections(branch, out_weight, grad, grad_t)
    copies.need(mixed_t)
    row_deltas(mixed_t, grad_t, delta)
    copies.need(queries_t, keys, kaug, qaug, values, log_mass, queries, keys_t)
    attend_back(
        windows, 2, queries, queries_t, keys, keys_t, values, kaug, qaug, log_mass, delta, grad, grad_t,
        query_grad_t, key_grad, value_grad,
    )
    round_grads(query_grad_t, key_grad, value_grad, query_low, key_low, value_low)
    copies.push(key_low, value_low)
    copies.need(query_weight, scales, hidden)
    sums[...] = jnp.zeros_like(sums)

    def finish(part):
        normal, inverse = normalize(hidden[part, :])
        incoming = grad_two[part, :] + back_product(query_low, part, query_weight)
        sums[0] += fold_rows(incoming * normal)
        sums[1] += fold_rows(incoming)
        result = normalize_back(incoming, normal, inverse, scales[0:1, :])
        grad_one[part, :] = result
        self_branch[part, :] = result.astype(BF16)

    chunks(rows, 256, finish)
    copies.push(self_branch, grad_one)
    copies.need(first_low, encoder, self_mixed_t, scale_grads)
    weight_grad(spots, grads, 0, first_low, query_low)
    weight_grad(spots, grads, BLOCK, encoder, key_low)
    weight_grad(spots, grads, 2 * BLOCK, encoder, value_low)
    half_width = self_mixed_t.shape[1]
    for half in range(self_mixed_t.shape[0]):
        value = dot(self_mixed_t[half], self_branch[...]).astype(BF16)
        put_blocks(spots, grads, half * half_width // BLOCK, BLOCK, 3 * BLOCK, value)
    at = iota((BLOCK, width), 0)
    own = jnp.sum(sums[...], axis=1)
    below = jnp.concatenate([scale_grads[...], jnp.zeros_like(scale_grads)], axis=0)
    every = jnp.where(at == 0, own[0:1], jnp.where(at == 3, own[1:2], below))
    for block in range(width // BLOCK):
        shift = (width - block * BLOCK) % width
        turned = every if shift == 0 else pltpu.roll(every, shift, 1)
        grads[place(spots, block), 4 * BLOCK : 5 * BLOCK, :] = turned.astype(BF16)
    hand_out(copies, grads, keep, send)


def self_backward_body(
    copies, branch, weight, mixed_t, queries_t, keys, kaug, qaug, values, log_mass, queries, keys_t, tokens, windows, spots,
    query_low, key_low, value_low, keep, send,
    grad, grad_t, delta, query_grad_t, key_grad, value_grad, grads,
):
    copies.need(branch, weight)
    back_projections(branch, weight, grad, grad_t)
    copies.need(mixed_t)
    row_deltas(mixed_t, grad_t, delta)
    copies.need(queries_t, keys, kaug, qaug, values, log_mass, queries, keys_t)
    attend_back(
        windows, 0, queries, queries_t, keys, keys_t, values, kaug, qaug, log_mass, delta, grad, grad_t,
        query_grad_t, key_grad, value_grad,
    )
    round_grads(query_grad_t, key_grad, value_grad, query_low, key_low, value_low)
    copies.push(query_low, key_low, value_low)
    copies.need(tokens)
    for which, low in enumerate((query_low, key_low, value_low)):
        weight_grad(spots, grads, which * BLOCK, tokens, low)
    hand_out(copies, grads, keep, send)


def encoder_grad_body(copies, key_low, value_low, weights, encoder_grad):
    copies.need(key_low, value_low, weights)

    def one(part):
        value = back_product(key_low, part, weights.at[0]) + back_product(value_low, part, weights.at[1])
        encoder_grad[part, :] = value.astype(BF16)

    chunks(encoder_grad.shape[0], 256, one)
    copies.push(encoder_grad)


def tokens_grad_body(copies, grad_one, weights, query_low, key_low, value_low, tokens_grad):
    copies.need(grad_one, weights, query_low, key_low, value_low)

    def one(part):
        value = grad_one[part, :]
        for which, low in enumerate((query_low, key_low, value_low)):
            value = value + back_product(low, part, weights.at[which])
        tokens_grad[part, :] = value.astype(BF16)

    chunks(grad_one.shape[0], 256, one)
    copies.push(tokens_grad)


def fold_body(groups, *refs):
    count = sum(2 * len(terms) for terms, _ in groups)
    terms_refs, results = list(refs[:count]), list(refs[count:])
    for terms, axis in groups:
        keep, send = results.pop(0), results.pop(0)
        for row, column in terms:
            kept, came = terms_refs.pop(0), terms_refs.pop(0)
            lead, (high, wide) = kept.shape[:-2], kept.shape[-2:]
            for number in range(math.prod(lead)):
                index, left = [], number
                for size in reversed(lead):
                    index.insert(0, left % size)
                    left //= size
                value = (kept[tuple(index)].astype(F32) + came[tuple(index)].astype(F32)).astype(BF16)
                target = keep if index.pop(axis) == 0 else send
                target[(*index, slice(row, row + high), slice(column, column + wide))] = value


def total_body(keep, came, cross_qkv, self_out, gain, offset, self_qkv):
    def total(first, rows):
        return keep[first : first + rows, :].astype(F32) + came[first : first + rows, :].astype(F32)

    for which in range(3):
        cross_qkv[which] = total(which * BLOCK, BLOCK)
        self_qkv[which] = total((5 + which) * BLOCK, BLOCK)
    self_out[...] = total(3 * BLOCK, BLOCK)
    scales = total(4 * BLOCK, BLOCK)
    gain[...] = scales[0:3, : gain.shape[1]]
    offset[...] = scales[3:6, : offset.shape[1]]


def exchange(value, bit, devices):
    with jax.named_scope("across_" + ("core", "x", "y", "z", "zz")[bit] if bit < 5 else "across"):
        return exchange_bit(value, bit, devices)


def exchange_bit(value, bit, devices):
    return lax.ppermute(value, AXES, [(at, at ^ (1 << bit)) for at in range(devices)])


def bit_count(devices):
    return devices.bit_length() - 1


def join(first, second, zero):
    both = jnp.concatenate([first, jnp.zeros_like(second)], axis=0)
    return lax.dynamic_update_slice(both, second, (first.shape[0] + zero, 0, 0))


def gather_blocks(block, devices, zero):
    held = block
    for bit in reversed(range(2, bit_count(devices))):
        held = jnp.concatenate([held, exchange(held, bit, devices)], axis=0)
    held = join(held, exchange(held, 1, devices), zero)
    return held, exchange(held, 0, devices)


def gather_plain(block, per, blocks):
    every = lax.all_gather(block, AXES, axis=0, tiled=False)
    parts = every.shape[1] // per
    every = every.reshape(every.shape[0], parts, per, every.shape[2]).transpose(1, 0, 2, 3)
    every = every.reshape(parts, blocks, -1, every.shape[3]).transpose(1, 0, 2, 3)
    every = every.reshape(blocks, -1, every.shape[3])
    return every[: blocks // 2], every[blocks // 2 :]


def fold(name, groups, after=()):
    ins, outs, shapes = [], [], []
    for terms, axis in groups:
        high = max(row + kept.shape[-2] for kept, _, row, _ in terms)
        wide = max(column + kept.shape[-1] for kept, _, _, column in terms)
        lead = list(terms[0][0].shape[:-2])
        lead.pop(axis)
        for kept, came, _, _ in terms:
            ins += [kept, came]
        outs += [((*lead, high, wide), BF16)] * 2
        shapes.append(([(row, column) for _, _, row, column in terms], axis))
    results = call_near(lambda *refs: fold_body(shapes, *refs), name, outs, ins, 2, after)
    return [tuple(results[at : at + 2]) for at in range(0, len(results), 2)]


def local(
    tokens, encoder, out_grad, self_qkv, self_out, cross_qkv, cross_out, ffn_in, ffn_out, ln_gain, ln_bias,
    tgt_lengths, tgt_pad, src_segments,
):
    devices = lax.axis_size("dp") * lax.axis_size("fsdp")
    me = lax.axis_index(AXES)
    token_rows, encoder_rows = tokens[0], encoder[0]
    rows, width = token_rows.shape
    wide = ffn_in.shape[1]
    own = self_out.shape[0]
    blocks = width // BLOCK
    direct = devices == blocks and devices == 32
    parts = wide // width
    each = wide // blocks
    heads = width // HEAD_DIM

    number = me.astype(jnp.int32)
    if direct:
        spots = jnp.stack([jnp.int32(1), number, mirrored(number)])
    else:
        spots = jnp.zeros((3,), jnp.int32)

    square, tall = (rows, width), (width, rows)
    self_kaug, self_qaug, cross_kaug, cross_qaug, windows, prep_zero = call(
        prep_body, "prep",
        [((rows, TILE), BF16), ((MASK_ROWS, rows), BF16)] * 2 + [((4, rows // TILE), jnp.int32), ((1,), jnp.int32)],
        [tgt_lengths[0], tgt_pad, src_segments[0].reshape(-1, TILE), src_segments[0].reshape(-1, 1)],
        (0, 1), 2, out_smem=(4, 5),
    )
    if direct:
        self_block, cross_block, ffn_block = call(
            pack_body, "pack",
            [((1, 3 * BLOCK, width), BF16), ((1, 6 * BLOCK, width), BF16), ((parts * BLOCK + each, width), BF16)],
            [self_qkv, self_out, cross_qkv, cross_out, ffn_in, ffn_out, ln_gain, ln_bias], (), 1,
        )
        self_low, self_high = gather_blocks(self_block, devices, prep_zero[0])
        cross_held = cross_block
        for bit in reversed(range(2, bit_count(devices))):
            cross_held = jnp.concatenate([cross_held, exchange(cross_held, bit, devices)], axis=0)
        cross_came = exchange(cross_held, 1, devices)
        ffn_all = lax.all_gather(ffn_block, AXES, axis=0, tiled=False)
    else:
        inner_rows = jnp.concatenate([ffn_in[:, at * width : (at + 1) * width] for at in range(parts)], axis=0)
        cross_block = jnp.concatenate([cross_qkv.reshape(-1, width), cross_out, self_out], axis=0)
        self_low, self_high = gather_plain(self_qkv.reshape(-1, width), own, blocks)
        cross_low, cross_high = gather_plain(cross_block, own, blocks)
        scale_all = lax.all_gather(jnp.concatenate([ln_gain, ln_bias], axis=0), AXES, axis=1, tiled=True)
        scale_all = scale_all.reshape(-1, blocks, BLOCK).transpose(1, 0, 2)
        scale_all = jnp.pad(scale_all, ((0, 0), (0, BLOCK - scale_all.shape[1]), (0, width - BLOCK)))
        cross_low = jnp.concatenate([cross_low, scale_all[: blocks // 2]], axis=1)
        cross_high = jnp.concatenate([cross_high, scale_all[blocks // 2 :]], axis=1)
        inner_all = jnp.concatenate(gather_plain(inner_rows, own, blocks), axis=0)
        outer_all = jnp.concatenate(gather_plain(ffn_out, ffn_out.shape[0], blocks), axis=0)
        ffn_all = jnp.concatenate([inner_all, outer_all], axis=1)

    halves, halves_t, masses = (2, rows, width // 2), (2, width // 2, rows), (2, 8, rows)
    saved = [(halves, BF16), (halves_t, BF16), (halves, BF16), (halves_t, BF16), (halves, BF16), (halves_t, BF16), (masses, F32)]
    pipeline = [(halves_t, BF16), ((2, rows, 2 * TILE), F32), ((2, rows, 2 * TILE), BF16)]
    queries, queries_t, keys, keys_t, values, mixed_t, log_mass, weights, zero = call(
        self_forward_body, "self_forward", saved + [((3, width, width), BF16), ((1,), jnp.int32)],
        [self_low, self_high, token_rows, self_kaug, self_qaug, spots, windows],
        (5, 6), 15, pipeline, out_smem=(8,), near=(0, 1), limit=44,
    )
    if direct:
        cross_low = join(cross_held, cross_came, zero[0])
        cross_high = exchange(cross_low, 0, devices)
    (
        hidden_one, hidden_two, first_low, cross_queries, cross_queries_t, cross_keys, cross_keys_t, cross_values,
        cross_mixed_t, cross_mass, cross_weights, scales,
    ) = call(
        cross_forward_body, "cross_forward",
        [(square, F32)] * 2 + [(square, BF16)] + saved + [((5, width, width), BF16), ((BLOCK, width), F32)],
        [cross_low, cross_high, token_rows, mixed_t, encoder_rows, cross_kaug, cross_qaug, spots, windows],
        (7, 8), 18, pipeline + [(square, F32)], near=(0, 1), limit=50,
    )
    inside = parts * BLOCK + BLOCK
    most = inside + each
    result, grad_two, scale_grads, ffn_grads = call(
        feed_forward_body, "feed_forward",
        [(square, BF16), (square, F32), ((8, width), F32), ((blocks, most, width), BF16)],
        [ffn_all, hidden_two, out_grad[0], scales, cross_mixed_t, spots],
        (5,), 30,
        [
            ((width, wide), BF16), ((wide, width), BF16), ((wide, width), BF16), ((width, wide), BF16),
            (square, BF16), ((rows, wide), BF16), ((256, wide), F32), (square, BF16), ((rows, wide), BF16), (square, BF16),
            ((8, 8, width), F32), ((blocks, most, width), BF16),
        ],
        by_part=(3,),
    )
    if direct:
        near_groups = [[8 * at + other for other in range(8)] for at in range(4)]
        far_groups = [[at + 8 * other for other in range(4)] for at in range(8)]
        ffn_sum = lax.psum_scatter(ffn_grads, AXES, scatter_dimension=0, axis_index_groups=near_groups, tiled=True)
        ffn_sum = lax.psum_scatter(ffn_sum, AXES, scatter_dimension=0, axis_index_groups=far_groups, tiled=True)
        ffn_sum = ffn_sum[0].astype(F32)
        ffn_in_grad = jnp.concatenate([ffn_sum[at * BLOCK : (at + 1) * BLOCK] for at in range(parts)], axis=1)
        cross_out_grad = ffn_sum[parts * BLOCK : inside]
        ffn_out_grad = ffn_sum[inside:]
    work = [(halves, BF16), (halves_t, BF16), (masses, F32), (halves_t, F32), (halves, F32), (halves, F32)]
    grad_one, self_branch, cross_key_low, cross_value_low, cross_keep, cross_send = call(
        cross_backward_body, "cross_backward",
        [(square, F32), (square, BF16)] + [(halves, BF16)] * 2 + [((blocks // 2, 5 * BLOCK, width), BF16)] * 2,
        [
            grad_two, (cross_weights, 3), cross_mixed_t, cross_queries_t, cross_keys, cross_kaug, cross_qaug, cross_values,
            cross_mass, cross_queries, cross_keys_t, (cross_weights, 0), scales, hidden_one, first_low, encoder_rows, mixed_t,
            scale_grads, windows, spots,
        ],
        (18, 19), 25,
        [(square, BF16), (halves, BF16)] + work + [((2, 8, width), F32), ((blocks, 5 * BLOCK, width), BF16)],
        by_part=(4, 5),
    )

    grid = (2, 2, 2, 2)
    if direct:
        cross_came = exchange(cross_send, 0, devices)
    query_low, key_low, value_low, self_keep, self_send = call(
        self_backward_body, "self_backward",
        [(halves, BF16)] * 3 + [((blocks // 2, 3 * BLOCK, width), BF16)] * 2,
        [
            self_branch, (cross_weights, 4), mixed_t, queries_t, keys, self_kaug, self_qaug, values, log_mass, queries, keys_t,
            token_rows, windows, spots,
        ],
        (12, 13), 25, work + [((blocks, 3 * BLOCK, width), BF16)], by_part=(3, 4),
    )
    after = ()
    if direct:

        def cube(value):
            return value.reshape(grid + value.shape[1:])

        self_came = exchange(self_send, 0, devices)
        ((cross_keep, cross_send),) = fold(
            "fold_cross", [([(cube(cross_keep), cube(cross_came), 0, 0)], 0)], (query_low,)
        )
        cross_came = exchange(cross_send, 1, devices)
        ((self_keep, self_send),) = fold("fold_self", [([(cube(self_keep), cube(self_came), 0, 0)], 1)], (cross_send,))
        self_came = exchange(self_send, 2, devices)
        after = (cross_send, self_send)
    (encoder_grad,) = call(
        encoder_grad_body, "encoder_grad", [(square, BF16)],
        [cross_key_low, cross_value_low, (cross_weights, slice(1, 3))], (), 4, after=after, limit=32,
    )
    if direct:
        (cross_keep, cross_send), (self_keep, self_send) = fold(
            "fold_second", [([(cross_keep, cross_came, 0, 0)], 0), ([(self_keep, self_came, 0, 0)], 0)], (encoder_grad,)
        )
        cross_came = exchange(cross_send, 2, devices)
        self_came = exchange(self_send, 1, devices)
        after = (cross_send, self_send)
    (tokens_grad,) = call(
        tokens_grad_body, "tokens_grad", [(square, BF16)], [grad_one, weights, query_low, key_low, value_low], (), 5,
        after=after, limit=32,
    )
    if direct:
        ((rest_keep, rest_send),) = fold(
            "fold_third", [([(cross_keep, cross_came, 0, 0), (self_keep, self_came, 5 * BLOCK, 0)], 0)], (tokens_grad,)
        )
        rest_came = exchange(rest_send, 3, devices)
        ((rest_keep, rest_send),) = fold("fold_fourth", [([(rest_keep, rest_came, 0, 0)], 0)])
        rest_came = exchange(rest_send, 4, devices)
        cross_qkv_grad, self_out_grad, gain_grad, offset_grad, self_qkv_grad = call_near(
            total_body, "total",
            [((3, own, width), F32), ((own, width), F32), ((3, own), F32), ((3, own), F32), ((3, own, width), F32)],
            [rest_keep, rest_came], 1,
        )
    else:

        def add_up(grads, first, last, per):
            piece = grads[:, first:last].reshape(blocks, -1, per, width).transpose(1, 0, 2, 3)
            piece = piece.reshape(piece.shape[0], blocks * per, width)
            return lax.psum_scatter(piece.astype(F32), AXES, scatter_dimension=1, tiled=True)

        cross_grads = jnp.concatenate([cross_keep, cross_send], axis=0)
        self_grads = jnp.concatenate([self_keep, self_send], axis=0)
        inner_sum = add_up(ffn_grads, 0, parts * BLOCK, BLOCK)
        ffn_in_grad = inner_sum.transpose(1, 0, 2).reshape(own, wide)
        ffn_out_grad = add_up(ffn_grads, inside, most, each)[0]
        cross_out_grad = add_up(ffn_grads, parts * BLOCK, inside, BLOCK)[0]
        cross_qkv_grad = add_up(cross_grads, 0, 3 * BLOCK, BLOCK)
        self_out_grad = add_up(cross_grads, 3 * BLOCK, 4 * BLOCK, BLOCK)[0]
        scale_parts = cross_grads[:, 4 * BLOCK : 4 * BLOCK + 6, :BLOCK].astype(F32)
        scale_parts = scale_parts.transpose(1, 0, 2).reshape(6, width)
        scale_sum = lax.psum_scatter(scale_parts, AXES, scatter_dimension=1, tiled=True)
        gain_grad, offset_grad = scale_sum[:3], scale_sum[3:]
        self_qkv_grad = add_up(self_grads, 0, 3 * BLOCK, BLOCK)
    return (
        result[None], tokens_grad[None], encoder_grad[None], self_qkv_grad, self_out_grad, cross_qkv_grad,
        cross_out_grad, ffn_in_grad, ffn_out_grad, gain_grad, offset_grad,
    )


def solution(mesh):
    rows, first, second = P(AXES, None, None), P(AXES, None), P(None, AXES, None)
    columns = P(None, AXES)
    in_specs = (
        rows, rows, rows, second, first, second, first, first, first, columns, columns, first, P(AXES), first,
    )
    out_specs = (rows, rows, rows, second, first, second, first, first, first, columns, columns)
    return jax.shard_map(local, mesh=mesh, in_specs=in_specs, out_specs=out_specs, check_vma=False)
```

```python
import math

import jax
import jax.numpy as jnp
from jax import lax
from jax.experimental import pallas as pl
from jax.experimental.pallas import tpu as pltpu
from jax.sharding import PartitionSpec as P

F32 = jnp.float32
BF16 = jnp.bfloat16
HEAD_DIM = 64
PAIR = 2 * HEAD_DIM
TILE = 128
BLOCK = 16
AXES = ("dp", "fsdp")
QUERY_SCALE = math.log2(math.e) / math.sqrt(HEAD_DIM)
MASK_ROWS = 32
MASKED = -1e30
WINDOWS = (2, 4, 6, 8)
SMEM = pl.BlockSpec(memory_space=pltpu.SMEM)
ANYWHERE = pl.BlockSpec(memory_space=pl.ANY)
HBM = pl.BlockSpec(memory_space=pltpu.HBM)
VMEM = pl.BlockSpec(memory_space=pltpu.VMEM)


def dot(left, right):
    return jnp.dot(left, right, preferred_element_type=F32)


def dot_tn(left, right):
    return lax.dot_general(left, right, (((0,), (0,)), ((), ())), preferred_element_type=F32)


def dot_nt(left, right):
    return lax.dot_general(left, right, (((1,), (1,)), ((), ())), preferred_element_type=F32)


def iota(shape, axis):
    return lax.broadcasted_iota(jnp.int32, shape, axis)


def part_shape(shape, index):
    if index is None:
        return shape
    index = index if isinstance(index, tuple) else (index,)
    taken = [one.stop - one.start for one in index if isinstance(one, slice)]
    return (*taken, *shape[len(index) :])


class Copies:

    def __init__(self, semaphores):
        self.semaphores = semaphores
        self.used = 0
        self.coming = {}
        self.going = {}
        self.started = []

    def start(self, source, target):
        copy = pltpu.make_async_copy(source, target, self.semaphores.at[self.used])
        self.used += 1
        copy.start()
        return copy

    def need(self, *refs):
        for ref in refs:
            if id(ref) in self.coming:
                self.coming.pop(id(ref)).wait()

    def push(self, *refs):
        for ref in refs:
            self.started.append(self.start(*self.going.pop(id(ref))))

    def push_part(self, source, target):
        self.started.append(self.start(source, target))

    def finish(self):
        for copy in self.coming.values():
            copy.wait()
        for ref, target in self.going.values():
            self.started.append(self.start(ref, target))
        for copy in self.started:
            copy.wait()


def call(body, name, outs, ins, in_smem, micros, scratch=(), out_smem=(), after=(), by_part=(), stay=(), near=(), through=(), limit=48):
    ins = [one if isinstance(one, tuple) else (one, None) for one in ins]
    indexes = [index for _, index in ins]
    ins = [array for array, _ in ins]
    in_count, out_count = len(ins), len(outs)
    moved_in = [at for at in range(in_count) if at not in in_smem and at not in near]
    moved_out = [at for at in range(out_count) if at not in out_smem and at not in by_part and at not in stay]
    ins = [pltpu.with_memory_space_constraint(one, pltpu.HBM) if at in moved_in else one for at, one in enumerate(ins)]

    def ordered(*refs):
        sources, refs = list(refs[:in_count]), refs[in_count + len(after) + len(through) :]
        targets, refs = list(refs[:out_count]), refs[out_count + len(through) :]
        buffers_in, refs = refs[: len(moved_in)], refs[len(moved_in) :]
        buffers_out, refs = refs[: len(moved_out)], refs[len(moved_out) :]
        copies = Copies(refs[0])
        for at, buffer in zip(moved_in, buffers_in):
            source = sources[at] if indexes[at] is None else sources[at].at[indexes[at]]
            copies.coming[id(buffer)] = copies.start(source, buffer)
            sources[at] = buffer
        for at, buffer in zip(moved_out, buffers_out):
            copies.going[id(buffer)] = (buffer, targets[at])
            targets[at] = buffer
        body(copies, *sources, *targets, *refs[1:])
        copies.finish()

    return pl.pallas_call(
        ordered,
        name=name,
        out_shape=[
            jax.ShapeDtypeStruct(shape, kind) if at in out_smem else (pltpu.VMEM if at in stay else pltpu.HBM)(shape, kind)
            for at, (shape, kind) in enumerate(outs)
        ]
        + [jax.ShapeDtypeStruct(one.shape, one.dtype) for one in through],
        in_specs=[SMEM if at in in_smem else VMEM if at in near else HBM for at in range(in_count)]
        + [ANYWHERE] * (len(after) + len(through)),
        out_specs=[SMEM if at in out_smem else VMEM if at in stay else HBM for at in range(out_count)]
        + [ANYWHERE] * len(through),
        input_output_aliases={in_count + len(after) + at: out_count + at for at in range(len(through))},
        scratch_shapes=[pltpu.VMEM(part_shape(ins[at].shape, indexes[at]), ins[at].dtype) for at in moved_in]
        + [pltpu.VMEM(*outs[at]) for at in moved_out]
        + [pltpu.SemaphoreType.DMA((len(moved_in) + len(moved_out) + 4 * len(by_part) + len(stay) + 1,))]
        + [pltpu.VMEM(shape, kind) for shape, kind in scratch],
        compiler_params=pltpu.CompilerParams(vmem_limit_bytes=limit * 2**20),
        cost_estimate=pl.CostEstimate(flops=int(micros * 1e9), bytes_accessed=0, transcendentals=0),
    )(*ins, *after, *through)


def call_near(body, name, outs, ins, micros, after=(), through=(), stay=True):
    count, skipped = len(ins), len(ins) + len(after) + len(through)
    after = [pltpu.with_memory_space_constraint(one, pltpu.HBM) for one in after]
    results = pl.pallas_call(
        lambda *refs: body(*refs[:count], *refs[skipped : skipped + len(outs)]),
        name=name,
        out_shape=[pltpu.VMEM(shape, kind) if stay else jax.ShapeDtypeStruct(shape, kind) for shape, kind in outs]
        + [jax.ShapeDtypeStruct(one.shape, one.dtype) for one in through],
        in_specs=[VMEM] * count + [HBM] * len(after) + [ANYWHERE] * len(through),
        out_specs=[VMEM] * len(outs) + [ANYWHERE] * len(through),
        input_output_aliases={count + len(after) + at: len(outs) + at for at in range(len(through))},
        compiler_params=pltpu.CompilerParams(vmem_limit_bytes=16 * 2**20),
        cost_estimate=pl.CostEstimate(flops=int(micros * 1e9), bytes_accessed=0, transcendentals=0),
    )(*ins, *after, *through)
    return results[: len(outs)], results[len(outs) :]


def prep_body(copies, lengths, padding, src_grid, self_kaug, self_qaug, cross_kaug, cross_qaug, windows):
    copies.need(src_grid)
    rows = self_kaug.shape[0]
    count = lengths.shape[0]
    edge = rows - padding[0]
    ends, total = [], 0
    for at in range(count):
        total = total + lengths[at]
        ends.append(total)

    def labels(places):
        found = sum((places >= end).astype(jnp.int32) for end in ends)
        return jnp.where(places < edge, found, count)

    row_ids = labels(iota((8, rows), 1))[0:1]
    mask_rows = iota((MASK_ROWS, rows), 0)
    self_qaug[...] = jnp.where(row_ids != mask_rows, 1.0, 0.0).astype(BF16)
    cross_qaug[...] = jnp.where(jnp.minimum(row_ids, count - 1) != mask_rows, 1.0, 0.0).astype(BF16)
    lanes = iota((TILE, TILE), 1)
    ones_lanes = jnp.where((lanes >= MASK_ROWS) & (lanes < MASK_ROWS + 3), 1.0, 0.0)
    for tile in range(rows // TILE):
        part = slice(tile * TILE, (tile + 1) * TILE)
        column_ids = labels(iota((TILE, TILE), 0) + tile * TILE)
        self_kaug[part, :] = jnp.where(column_ids == lanes, MASKED, ones_lanes).astype(BF16)
        source_row = src_grid[tile : tile + 1, :].astype(F32)
        source_column = jnp.broadcast_to(source_row, (TILE, TILE)).T
        cross_kaug[part, :] = jnp.where(source_column == lanes.astype(F32), MASKED, ones_lanes).astype(BF16)
    copies.push(self_kaug, self_qaug, cross_kaug, cross_qaug)
    for tile in range(rows // TILE):
        first, last = tile * TILE, tile * TILE + TILE - 1
        start, stop, first_id, last_id = 0, edge, 0, 0
        for end in ends:
            start = jnp.where(end <= first, end, start)
            first_id = first_id + jnp.where(end <= first, 1, 0)
            last_id = last_id + jnp.where(end <= last, 1, 0)
        for end in reversed(ends):
            stop = jnp.where(end > last, jnp.minimum(end, edge), stop)
        start = jnp.where(first >= edge, edge, start)
        stop = jnp.where(last >= edge, rows, stop)
        first_id = jnp.where(first < edge, jnp.minimum(first_id, count - 1), count - 1)
        last_id = jnp.where(last < edge, jnp.minimum(last_id, count - 1), count - 1)
        low = start // TILE
        windows[0, tile] = low
        windows[1, tile] = (stop + TILE - 1) // TILE - low
        source = src_grid[...]
        below = jnp.sum(jnp.where(source < first_id, 1, 0))
        upto = jnp.sum(jnp.where(source <= last_id, 1, 0))
        low = below // TILE
        windows[2, tile] = low
        windows[3, tile] = (upto + TILE - 1) // TILE - low


def pair_columns(block):
    upper = iota(block.shape, 0) < HEAD_DIM
    none = jnp.zeros_like(block)
    return jnp.concatenate([jnp.where(upper, block, none), jnp.where(upper, none, block)], axis=1)


def pair_rows(block):
    left = iota(block.shape, 1) < HEAD_DIM
    none = jnp.zeros_like(block)
    return jnp.concatenate([jnp.where(left, block, none), jnp.where(left, none, block)], axis=0)


def twice(block):
    return jnp.concatenate([block, block], axis=1)


def split_three(row):
    first = row.astype(BF16).astype(F32)
    second = (row - first).astype(BF16).astype(F32)
    third = row - first - second
    at = iota((BLOCK, row.shape[1]), 0)
    none = jnp.zeros((BLOCK, row.shape[1]), F32)
    picked = jnp.where(at == 0, first, jnp.where(at == 1, second, jnp.where(at == 2, third, none)))
    return picked.astype(BF16)


def over_windows(windows, row, rows, run):
    tiles = rows // TILE

    def one_tile(tile, _):
        low, width = windows[row, tile], windows[row + 1, tile]
        before = 0
        for most in WINDOWS:
            start = jnp.minimum(low, tiles - most) * TILE

            @pl.when((width > before) & (width <= most))
            def _():
                run(pl.multiple_of(tile * TILE, TILE), pl.multiple_of(start, TILE), most * TILE)

            before = most
        return 0

    lax.fori_loop(0, tiles, one_tile, 0)


def places(pair):
    inner = (pair % 2) * PAIR
    return pair // 2, slice(inner, inner + PAIR)


def head_places(pair, head):
    inner = (pair % 2) * PAIR + head * HEAD_DIM
    return pair // 2, slice(inner, inner + HEAD_DIM), slice((pair % 2) * 2 + head, (pair % 2) * 2 + head + 1)


def attend(windows, row, queries_t, keys, values_t, kaug, qaug, mixed_t, log_mass, scores, raised):
    halves, rows, width = keys.shape
    pairs = halves * width // PAIR

    def run(query_at, key_at, key_count):
        query_part, key_part = pl.ds(query_at, TILE), pl.ds(key_at, key_count)
        mask_part = twice(qaug[:, query_part])
        empty = jnp.zeros((PAIR - MASK_ROWS, 2 * TILE), BF16)
        ones = jnp.ones((BLOCK, key_count), BF16)
        rights, found, peaks = [], [None] * pairs, [None] * pairs
        for pair in range(pairs):
            half, part = places(pair)
            rights.append(jnp.concatenate([pair_columns(queries_t[half, part, query_part]), mask_part, empty], axis=0))

        def score(pair, at):
            half, part = places(pair)
            here, span = pl.ds(key_at + at, TILE * 2), slice(at, at + TILE * 2)
            value = dot(jnp.concatenate([keys[half, here, part], kaug[here, :]], axis=1), rights[pair])
            scores[pair % 2, span, :] = value
            most = jnp.max(value.reshape(-1, 8, 2 * TILE), axis=0)
            found[pair] = most if at == 0 else jnp.maximum(found[pair], most)

        def raise_up(pair, at):
            span = slice(at, at + TILE * 2)
            if at == 0:
                peaks[pair] = jnp.max(found[pair], axis=0, keepdims=True)
            raised[pair % 2, span, :] = jnp.exp2(scores[pair % 2, span, :] - peaks[pair]).astype(BF16)

        def mix(pair):
            half, part = places(pair)
            left = jnp.concatenate([values_t[half, part, key_part], ones], axis=0)
            mixed = dot(left, raised[pair % 2, 0:key_count, :])
            mass = mixed[PAIR : PAIR + 1]
            scale = 1.0 / mass
            logs = peaks[pair] + jnp.log2(mass)
            for head in range(2):
                spot = slice(head * TILE, (head + 1) * TILE)
                inner = slice(head * HEAD_DIM, (head + 1) * HEAD_DIM)
                half, outer, at = head_places(pair, head)
                mixed_t[half, outer, query_part] = (mixed[inner, spot] * scale[:, spot]).astype(BF16)
                log_mass[half, at, query_part] = logs[:, spot]

        for step in range(pairs + 2):
            for at in range(0, key_count, TILE * 2):
                if step < pairs:
                    score(step, at)
                if 0 <= step - 1 < pairs:
                    raise_up(step - 1, at)
                if at == 0 and 0 <= step - 2 < pairs:
                    mix(step - 2)

    over_windows(windows, row, rows, run)


def attend_back(
    windows, row, queries, queries_t, keys, keys_t, values, kaug, qaug, log_mass, delta, grad, grad_t,
    query_grad_t, key_grad, value_grad,
):
    halves, rows, width = keys.shape
    key_grad[...] = jnp.zeros_like(key_grad)
    value_grad[...] = jnp.zeros_like(value_grad)

    def run(query_at, key_at, key_count):
        query_part, key_part = pl.ds(query_at, TILE), pl.ds(key_at, key_count)
        mask_part = twice(qaug[:, query_part])
        no_mask = jnp.zeros((MASK_ROWS, 2 * TILE), BF16)
        empty = jnp.zeros((PAIR - MASK_ROWS - BLOCK, 2 * TILE), BF16)
        key_mask = kaug[key_part, :]
        for pair in range(halves * width // PAIR):
            half, part = places(pair)
            heads = [head_places(pair, head) for head in range(2)]
            masses = jnp.concatenate([log_mass[half, at, query_part] for half, _, at in heads], axis=1)
            deltas = jnp.concatenate([delta[half, at, query_part] for half, _, at in heads], axis=1)
            right = jnp.concatenate(
                [pair_columns(queries_t[half, part, query_part]), mask_part, split_three(-masses), empty], axis=0
            )
            probs = jnp.exp2(dot(jnp.concatenate([keys[half, key_part, part], key_mask], axis=1), right))
            right = jnp.concatenate(
                [pair_columns(grad_t[half, part, query_part]), no_mask, split_three(-deltas), empty], axis=0
            )
            grad_probs = dot(jnp.concatenate([values[half, key_part, part], key_mask], axis=1), right)
            grad_scores = (probs * grad_probs).astype(BF16)
            value_grad[half, key_part, part] += dot(probs.astype(BF16), pair_rows(grad[half, query_part, part]))
            key_grad[half, key_part, part] += dot(grad_scores, pair_rows(queries[half, query_part, part]))
            mixed = dot(keys_t[half, part, key_part], grad_scores)
            for head, (half, outer, _) in enumerate(heads):
                spot = slice(head * TILE, (head + 1) * TILE)
                inner = slice(head * HEAD_DIM, (head + 1) * HEAD_DIM)
                query_grad_t[half, outer, query_part] = mixed[inner, spot]

    over_windows(windows, row, rows, run)


def row_deltas(mixed_t, grad_t, delta):
    halves, width, rows = mixed_t.shape
    for half in range(halves):
        for head in range(width // HEAD_DIM):
            part = slice(head * HEAD_DIM, (head + 1) * HEAD_DIM)
            product = mixed_t[half, part, :].astype(F32) * grad_t[half, part, :].astype(F32)
            delta[half, head : head + 1, :] = jnp.sum(product, axis=0, keepdims=True)


def normalize(hidden):
    center = hidden - jnp.mean(hidden, axis=-1, keepdims=True)
    spread = jnp.mean(center * center, axis=-1, keepdims=True)
    inverse = lax.rsqrt(spread + 1e-05)
    return center * inverse, inverse


def normalize_back(incoming, normal, inverse, gain):
    scaled = incoming * gain
    average = jnp.mean(scaled, axis=-1, keepdims=True)
    along = jnp.mean(scaled * normal, axis=-1, keepdims=True)
    return inverse * (scaled - average - normal * along)


def chunks(rows, step, run):
    def one(at, _):
        run(pl.ds(pl.multiple_of(at * step, step), step))
        return 0

    lax.fori_loop(0, rows // step, one, 0)


def fold_rows(block):
    return jnp.sum(block.reshape(-1, 8, block.shape[1]), axis=0)


def mirrored(number):
    return sum(((number >> bit) & 1) << (4 - bit) for bit in range(5))


def origin(spots, spot, swapped=False):
    number = mirrored(spot)
    if swapped:
        number = (number & 25) | ((number & 2) << 1) | ((number & 4) >> 1)
    return jnp.where(spots[0] == 1, number ^ spots[1], spot)


def place(spots, block):
    return jnp.where(spots[0] == 1, mirrored(block) ^ spots[2], block)


def take_blocks(spots, pieces, row, target, swapped=False):
    each = pieces[0].shape[0]
    for spot in range(each * len(pieces)):
        start = pl.multiple_of(origin(spots, spot, swapped) * BLOCK, BLOCK)
        target[pl.ds(start, BLOCK), :] = pieces[spot // each][spot % each, row : row + BLOCK, :]


def put_blocks(spots, grads, first, rows_each, row, value):
    for at in range(value.shape[0] // rows_each):
        grads[place(spots, first + at), row : row + rows_each, :] = value[at * rows_each : (at + 1) * rows_each]


def hand_out(copies, grads, keep, send):
    half = keep.shape[0]
    copies.push_part(grads.at[half : 2 * half], send)
    copies.push_part(grads.at[0:half], keep)


def pack_body(copies, self_qkv, self_out, cross_qkv, cross_out, ffn_in, ffn_out, gain, offset, self_block, cross_block, ffn_block):
    copies.need(self_qkv, self_out, cross_qkv, cross_out, ffn_in, ffn_out, gain, offset)
    width = self_out.shape[1]
    own = gain.shape[1]
    for which in range(3):
        rows = slice(which * BLOCK, (which + 1) * BLOCK)
        self_block[0, rows, :] = self_qkv[which]
        cross_block[0, rows, :] = cross_qkv[which]
    cross_block[0, 3 * BLOCK : 4 * BLOCK, :] = cross_out[...]
    cross_block[0, 4 * BLOCK : 5 * BLOCK, :] = self_out[...]
    scales = jnp.concatenate([gain[...].astype(F32), offset[...].astype(F32), jnp.zeros((BLOCK - 6, own), F32)], axis=0)
    scales = jnp.concatenate([scales, jnp.zeros((BLOCK, width - own), F32)], axis=1)
    cross_block[0, 5 * BLOCK : 6 * BLOCK, :] = scales.astype(BF16)
    parts = ffn_in.shape[1] // width
    for part in range(parts):
        ffn_block[part * BLOCK : (part + 1) * BLOCK, :] = ffn_in[:, part * width : (part + 1) * width]
    ffn_block[parts * BLOCK :, :] = ffn_out[...]
    copies.push(self_block, cross_block, ffn_block)


def lay_rows(value, target, part):
    wide = target.shape[2]
    for half in range(target.shape[0]):
        target[half, part, :] = value[:, half * wide : (half + 1) * wide]


def lay_columns(value, target, part):
    wide = target.shape[1]
    turned = value.T
    for half in range(target.shape[0]):
        target[half, :, part] = turned[half * wide : (half + 1) * wide]


def mixed_product(mixed_t, part, weight):
    wide = mixed_t.shape[1]
    return sum(dot_tn(mixed_t[half, :, part], weight[half * wide : (half + 1) * wide, :]) for half in range(mixed_t.shape[0]))


def self_forward_body(
    copies, piece_one, piece_two, piece_three, piece_four, tokens, kaug, qaug, spots, windows,
    queries, queries_t, keys, keys_t, values, mixed_t, log_mass, weights,
    values_t, scores, raised,
):
    pieces = (piece_one, piece_two, piece_three, piece_four)
    copies.need(*pieces)
    for which in range(3):
        take_blocks(spots, pieces, which * BLOCK, weights.at[which])
    copies.push(weights)
    copies.need(tokens)

    def project(part):
        rows = tokens[part, :]
        query_rows = (dot(rows, weights[0]) * QUERY_SCALE).astype(BF16)
        lay_rows(query_rows, queries, part)
        lay_columns(query_rows, queries_t, part)
        key_rows = dot(rows, weights[1]).astype(BF16)
        lay_rows(key_rows, keys, part)
        lay_columns(key_rows, keys_t, part)
        value_rows = dot(rows, weights[2]).astype(BF16)
        lay_rows(value_rows, values, part)
        lay_columns(value_rows, values_t, part)

    chunks(tokens.shape[0], 256, project)
    copies.push(queries, queries_t, keys, keys_t, values)
    copies.need(kaug, qaug)
    attend(windows, 0, queries_t, keys, values_t, kaug, qaug, mixed_t, log_mass, scores, raised)
    copies.push(mixed_t, log_mass)


def cross_forward_body(
    copies, upper_one, upper_two, upper_three, upper_four, lower_one, lower_two, lower_three, lower_four,
    tokens, self_mixed_t, encoder, kaug, qaug, spots, windows,
    hidden, hidden_two, first_low, queries, queries_t, keys, keys_t, values, mixed_t, log_mass, weights, scales,
    values_t, scores, raised, first,
):
    upper = (upper_one, upper_two, upper_three, upper_four)
    lower = (lower_one, lower_two, lower_three, lower_four)
    copies.need(*upper, *lower)
    for which in range(3):
        take_blocks(spots, upper, which * BLOCK, weights.at[which])
    for which in range(2):
        take_blocks(spots, lower, which * BLOCK, weights.at[3 + which], True)
    each = lower_one.shape[0]
    gathered = jnp.zeros(scales.shape, F32)
    for spot in range(4 * each):
        block = lower[spot // each][spot % each, 2 * BLOCK : 3 * BLOCK, :].astype(F32)
        gathered = gathered + pltpu.roll(block, origin(spots, spot, True) * BLOCK, 1)
    scales[...] = gathered
    copies.push(weights, scales)
    gain, offset = scales[0:1, :], scales[3:4, :]
    copies.need(tokens, self_mixed_t, encoder)

    def project(part):
        rows = encoder[part, :]
        key_rows = dot(rows, weights[1]).astype(BF16)
        lay_rows(key_rows, keys, part)
        lay_columns(key_rows, keys_t, part)
        value_rows = dot(rows, weights[2]).astype(BF16)
        lay_rows(value_rows, values, part)
        lay_columns(value_rows, values_t, part)
        before = tokens[part, :].astype(F32) + mixed_product(self_mixed_t, part, weights.at[4])
        hidden[part, :] = before
        normal, _ = normalize(before)
        first_rows = normal * gain + offset
        first[part, :] = first_rows
        low_rows = first_rows.astype(BF16)
        first_low[part, :] = low_rows
        query_rows = (dot(low_rows, weights[0]) * QUERY_SCALE).astype(BF16)
        lay_rows(query_rows, queries, part)
        lay_columns(query_rows, queries_t, part)

    chunks(encoder.shape[0], 256, project)
    copies.push(hidden, first_low, queries, queries_t, keys, keys_t, values)
    copies.need(kaug, qaug)
    attend(windows, 2, queries_t, keys, values_t, kaug, qaug, mixed_t, log_mass, scores, raised)
    copies.push(mixed_t, log_mass)

    def finish(part):
        hidden_two[part, :] = first[part, :] + mixed_product(mixed_t, part, weights.at[3])

    chunks(encoder.shape[0], 256, finish)
    copies.push(hidden_two)


def feed_forward_body(
    copies, gathered, hidden, out_grad, scales, cross_mixed_t, spots,
    out, grad_two, scale_grads, inner_grads, keep, send,
    inner, outer, inner_t, outer_t, second_low, active, slope, branch, grad_inner, cross_branch, sums, grads, grads_out,
):
    rows, width = hidden.shape
    wide = outer.shape[0]
    parts = wide // width
    each = wide // (width // BLOCK)
    copies.need(gathered)
    for block in range(width // BLOCK):
        for part in range(parts):
            inner[block * BLOCK : (block + 1) * BLOCK, part * width : (part + 1) * width] = gathered[
                block, part * BLOCK : (part + 1) * BLOCK, :
            ]
        outer[block * each : (block + 1) * each, :] = gathered[block, parts * BLOCK : parts * BLOCK + each, :]
    for part in range(parts):
        span = slice(part * width, (part + 1) * width)
        inner_t[span, :] = inner[:, span].T
        outer_t[:, span] = outer[span, :].T
    sums[...] = jnp.zeros_like(sums)
    root = math.sqrt(2.0 / math.pi)
    copies.need(hidden, out_grad, scales)

    def one(part):
        normal_two, inverse_two = normalize(hidden[part, :])
        second = normal_two * scales[1:2, :] + scales[4:5, :]
        low = second.astype(BF16)
        second_low[part, :] = low
        for at in range(parts):
            span = slice(at * width, (at + 1) * width)
            value = dot(low, inner[:, span])
            square = value * value
            curve = jnp.tanh(root * (value + 0.044715 * (value * square)))
            active[part, span] = (0.5 * value * (1.0 + curve)).astype(BF16)
            slope[:, span] = 0.5 * (1.0 + curve) + (0.5 * root) * value * (1.0 - curve * curve) * (1.0 + 0.134145 * square)
        normal_three, inverse_three = normalize(second + dot(active[part, :], outer[...]))
        out[part, :] = (normal_three * scales[2:3, :] + scales[5:6, :]).astype(BF16)
        incoming = out_grad[part, :].astype(F32)
        sums[2] += fold_rows(incoming * normal_three)
        sums[5] += fold_rows(incoming)
        grad_three = normalize_back(incoming, normal_three, inverse_three, scales[2:3, :])
        grad_low = grad_three.astype(BF16)
        branch[part, :] = grad_low
        for at in range(parts):
            span = slice(at * width, (at + 1) * width)
            grad_inner[part, span] = (dot(grad_low, outer_t[:, span]) * slope[:, span]).astype(BF16)
        grad_second = grad_three + dot(grad_inner[part, :], inner_t[...])
        sums[1] += fold_rows(grad_second * normal_two)
        sums[4] += fold_rows(grad_second)
        result = normalize_back(grad_second, normal_two, inverse_two, scales[1:2, :])
        grad_two[part, :] = result
        cross_branch[part, :] = result.astype(BF16)

    chunks(rows, 256, one)
    scale_grads[...] = jnp.sum(sums[...], axis=1)
    copies.push(out, grad_two, scale_grads)
    inside = parts * BLOCK

    def put(first, row, value):
        for at in range(value.shape[0] // BLOCK):
            block = first + at
            spot = jnp.where(spots[0] == 1, (block % 8) * 4 + block // 8, block)
            grads[spot, row : row + BLOCK, :] = value[at * BLOCK : (at + 1) * BLOCK]

    for at in range(parts):
        span = slice(at * width, (at + 1) * width)
        put(0, at * BLOCK, dot_tn(second_low[...], grad_inner[:, span]).astype(BF16))
    copies.push_part(grads.at[:, 0:inside, :], inner_grads.at[:, 0:inside, :])
    copies.need(cross_mixed_t)
    half_width = cross_mixed_t.shape[1]
    for half in range(cross_mixed_t.shape[0]):
        put(half * half_width // BLOCK, inside, dot(cross_mixed_t[half], cross_branch[...]).astype(BF16))
    copies.push_part(grads.at[:, inside : inside + BLOCK, :], inner_grads.at[:, inside : inside + BLOCK, :])
    for at in range(parts):
        span = slice(at * width, (at + 1) * width)
        value = dot_tn(active[:, span], branch[...]).astype(BF16)
        put_blocks(spots, grads_out, at * width // each, each, 0, value)
    hand_out(copies, grads_out, keep, send)


def back_projections(grad_rows, weight, grad, grad_t):
    def one(part):
        value = dot_nt(grad_rows[part, :], weight[...]).astype(BF16)
        lay_rows(value, grad, part)
        lay_columns(value, grad_t, part)

    chunks(grad.shape[1], 256, one)


def round_grads(query_grad_t, key_grad, value_grad, query_low, key_low, value_low):
    def one(part):
        for half in range(key_low.shape[0]):
            query_low[half, part, :] = (query_grad_t[half, :, part] * HEAD_DIM**-0.5).T.astype(BF16)
            key_low[half, part, :] = (key_grad[half, part, :] * math.log(2.0)).astype(BF16)
            value_low[half, part, :] = value_grad[half, part, :].astype(BF16)

    chunks(key_low.shape[1], 256, one)


def back_product(low, part, weight):
    wide = low.shape[2]
    return sum(dot_nt(low[half, part, :], weight[:, half * wide : (half + 1) * wide]) for half in range(low.shape[0]))


def weight_grad(spots, grads, row, left, low):
    wide = low.shape[2]
    for half in range(low.shape[0]):
        value = dot_tn(left[...], low[half]).astype(BF16)
        span = slice(half * wide, (half + 1) * wide)
        for at in range(value.shape[0] // BLOCK):
            grads[place(spots, at), row : row + BLOCK, span] = value[at * BLOCK : (at + 1) * BLOCK]


def cross_backward_body(
    copies, grad_two, out_weight, mixed_t, queries_t, keys, kaug, qaug, values, log_mass, queries, keys_t,
    query_weight, scales, hidden, first_low, encoder, self_mixed_t, scale_grads, windows, spots,
    grad_one, self_branch, key_low, value_low, keep, send,
    branch, query_low, grad, grad_t, delta, query_grad_t, key_grad, value_grad, sums, grads,
):
    rows, width = hidden.shape
    copies.need(grad_two, out_weight)

    def prepare(part):
        branch[part, :] = grad_two[part, :].astype(BF16)

    chunks(rows, 256, prepare)
    back_projections(branch, out_weight, grad, grad_t)
    copies.need(mixed_t)
    row_deltas(mixed_t, grad_t, delta)
    copies.need(queries_t, keys, kaug, qaug, values, log_mass, queries, keys_t)
    attend_back(
        windows, 2, queries, queries_t, keys, keys_t, values, kaug, qaug, log_mass, delta, grad, grad_t,
        query_grad_t, key_grad, value_grad,
    )
    round_grads(query_grad_t, key_grad, value_grad, query_low, key_low, value_low)
    copies.push(key_low, value_low)
    copies.need(query_weight, scales, hidden)
    sums[...] = jnp.zeros_like(sums)

    def finish(part):
        normal, inverse = normalize(hidden[part, :])
        incoming = grad_two[part, :] + back_product(query_low, part, query_weight)
        sums[0] += fold_rows(incoming * normal)
        sums[1] += fold_rows(incoming)
        result = normalize_back(incoming, normal, inverse, scales[0:1, :])
        grad_one[part, :] = result
        self_branch[part, :] = result.astype(BF16)

    chunks(rows, 256, finish)
    copies.push(self_branch, grad_one)
    copies.need(first_low, encoder, self_mixed_t, scale_grads)
    weight_grad(spots, grads, 0, first_low, query_low)
    weight_grad(spots, grads, BLOCK, encoder, key_low)
    weight_grad(spots, grads, 2 * BLOCK, encoder, value_low)
    half_width = self_mixed_t.shape[1]
    for half in range(self_mixed_t.shape[0]):
        value = dot(self_mixed_t[half], self_branch[...]).astype(BF16)
        put_blocks(spots, grads, half * half_width // BLOCK, BLOCK, 3 * BLOCK, value)
    at = iota((BLOCK, width), 0)
    own = jnp.sum(sums[...], axis=1)
    below = jnp.concatenate([scale_grads[...], jnp.zeros_like(scale_grads)], axis=0)
    every = jnp.where(at == 0, own[0:1], jnp.where(at == 3, own[1:2], below))
    for block in range(width // BLOCK):
        shift = (width - block * BLOCK) % width
        turned = every if shift == 0 else pltpu.roll(every, shift, 1)
        grads[place(spots, block), 4 * BLOCK : 5 * BLOCK, :] = turned.astype(BF16)
    hand_out(copies, grads, keep, send)


def self_backward_body(
    copies, branch, weight, mixed_t, queries_t, keys, kaug, qaug, values, log_mass, queries, keys_t, tokens, windows, spots,
    query_low, key_low, value_low, keep, send,
    grad, grad_t, delta, query_grad_t, key_grad, value_grad, grads,
):
    copies.need(branch, weight)
    back_projections(branch, weight, grad, grad_t)
    copies.need(mixed_t)
    row_deltas(mixed_t, grad_t, delta)
    copies.need(queries_t, keys, kaug, qaug, values, log_mass, queries, keys_t)
    attend_back(
        windows, 0, queries, queries_t, keys, keys_t, values, kaug, qaug, log_mass, delta, grad, grad_t,
        query_grad_t, key_grad, value_grad,
    )
    round_grads(query_grad_t, key_grad, value_grad, query_low, key_low, value_low)
    copies.push(query_low, key_low, value_low)
    copies.need(tokens)
    for which, low in enumerate((query_low, key_low, value_low)):
        weight_grad(spots, grads, which * BLOCK, tokens, low)
    hand_out(copies, grads, keep, send)


def encoder_grad_body(copies, key_low, value_low, weights, encoder_grad):
    copies.need(key_low, value_low, weights)

    def one(part):
        value = back_product(key_low, part, weights.at[0]) + back_product(value_low, part, weights.at[1])
        encoder_grad[part, :] = value.astype(BF16)

    chunks(encoder_grad.shape[0], 256, one)
    copies.push(encoder_grad)


def tokens_grad_body(copies, grad_one, weights, query_low, key_low, value_low, tokens_grad):
    copies.need(grad_one, weights, query_low, key_low, value_low)

    def one(part):
        value = grad_one[part, :]
        for which, low in enumerate((query_low, key_low, value_low)):
            value = value + back_product(low, part, weights.at[which])
        tokens_grad[part, :] = value.astype(BF16)

    chunks(grad_one.shape[0], 256, one)
    copies.push(tokens_grad)


def fold_body(groups, copies, *refs):
    count = sum(2 * len(terms) for terms, _ in groups)
    terms_refs, results = list(refs[:count]), list(refs[count:])
    for terms, axis in groups:
        keep, send = results.pop(0), results.pop(0)
        for row, column in terms:
            kept, came = terms_refs.pop(0), terms_refs.pop(0)
            copies.need(kept)
            lead, (high, wide) = kept.shape[:-2], kept.shape[-2:]
            for number in range(math.prod(lead)):
                index, left = [], number
                for size in reversed(lead):
                    index.insert(0, left % size)
                    left //= size
                value = (kept[tuple(index)].astype(F32) + came[tuple(index)].astype(F32)).astype(BF16)
                target = keep if index.pop(axis) == 0 else send
                target[(*index, slice(row, row + high), slice(column, column + wide))] = value


def order_body(copies, total, spots, keep, send):
    copies.need(total)
    near, far = (spots[1] >> 3) & 1, (spots[1] >> 4) & 1
    for block in range(2):
        keep[block] = total[near + 2 * (far ^ block)]
        send[block] = total[(1 - near) + 2 * (far ^ block)]


def inner_total_body(keep, came, ffn_in, cross_out):
    width = cross_out.shape[1]
    parts = ffn_in.shape[1] // width

    def total(first):
        return keep[first : first + BLOCK, :].astype(F32) + came[first : first + BLOCK, :].astype(F32)

    for part in range(parts):
        ffn_in[:, part * width : (part + 1) * width] = total(part * BLOCK)
    cross_out[...] = total(parts * BLOCK)


def total_body(keep, came, cross_qkv, self_out, gain, offset, self_qkv, ffn_out):
    def total(first, rows):
        return keep[first : first + rows, :].astype(F32) + came[first : first + rows, :].astype(F32)

    for which in range(3):
        cross_qkv[which] = total(which * BLOCK, BLOCK)
        self_qkv[which] = total((5 + which) * BLOCK, BLOCK)
    self_out[...] = total(3 * BLOCK, BLOCK)
    ffn_out[...] = total(8 * BLOCK, ffn_out.shape[0])
    scales = total(4 * BLOCK, BLOCK)
    gain[...] = scales[0:3, : gain.shape[1]]
    offset[...] = scales[3:6, : offset.shape[1]]


def exchange(value, bit, devices):
    with jax.named_scope("across_" + ("core", "x", "y", "z", "zz")[bit] if bit < 5 else "across"):
        return exchange_bit(value, bit, devices)


def exchange_bit(value, bit, devices):
    return lax.ppermute(value, AXES, [(at, at ^ (1 << bit)) for at in range(devices)])


def bit_count(devices):
    return devices.bit_length() - 1


def join_body(*refs):
    count = len(refs) // 3
    for at in range(count):
        first, second, target = refs[2 * at], refs[2 * at + 1], refs[2 * count + at]
        for block in range(first.shape[0]):
            target[block] = first[block]
            target[first.shape[0] + block] = second[block]


def join(name, pairs, after=(), through=()):
    outs = [((2 * first.shape[0], *first.shape[1:]), first.dtype) for first, _ in pairs]
    return call_near(join_body, name, outs, [one for pair in pairs for one in pair], 1, after, through)


def join_split_body(first, second, upper, lower):
    rows = upper.shape[1]
    for block in range(2 * first.shape[0]):
        source = first if block < first.shape[0] else second
        upper[block] = source[block % first.shape[0], 0:rows, :]
        lower[block] = source[block % first.shape[0], rows:, :]


def gather_both(self_held, cross_held, prepared, devices):
    for bit in (4, 3, 2):
        come = exchange(self_held, bit, devices)
        (self_held,), _ = join(f"join_self_{bit}", [(self_held, come)], prepared if bit == 2 else ())
    come = exchange(self_held, 1, devices)
    cross_come = exchange(cross_held, 4, devices)
    (cross_held,), _ = join("join_cross", [(cross_held, cross_come)])
    cross_come = exchange(cross_held, 3, devices)
    blocks, rows, width = cross_held.shape
    (upper, lower), _ = call_near(
        join_split_body, "join_split", [((2 * blocks, rows // 2, width), BF16)] * 2, [cross_held, cross_come], 1
    )
    upper_come, lower_come = exchange(upper, 2, devices), exchange(lower, 1, devices)
    (upper, lower), _ = join("join_halves", [(upper, upper_come), (lower, lower_come)])
    self_pieces = [self_held, come, exchange(self_held, 0, devices), exchange(come, 0, devices)]
    return self_pieces, (upper, lower, exchange(upper, 1, devices), exchange(lower, 2, devices))


def gather_plain(block, per, blocks):
    every = lax.all_gather(block, AXES, axis=0, tiled=False)
    parts = every.shape[1] // per
    every = every.reshape(every.shape[0], parts, per, every.shape[2]).transpose(1, 0, 2, 3)
    every = every.reshape(parts, blocks, -1, every.shape[3]).transpose(1, 0, 2, 3)
    every = every.reshape(blocks, -1, every.shape[3])
    return [every[at : at + blocks // 4] for at in range(0, blocks, blocks // 4)]


def fold(name, groups, after=(), through=(), far=False):
    ins, outs, shapes = [], [], []
    for terms, axis in groups:
        high = max(row + kept.shape[-2] for kept, _, row, _ in terms)
        wide = max(column + kept.shape[-1] for kept, _, _, column in terms)
        lead = list(terms[0][0].shape[:-2])
        lead.pop(axis)
        for kept, came, _, _ in terms:
            ins += [kept, came]
        outs += [((*lead, high, wide), BF16)] * 2
        shapes.append(([(row, column) for _, _, row, column in terms], axis))
    after = [pltpu.with_memory_space_constraint(one, pltpu.HBM) for one in after]
    near = range(1 if far else 0, len(ins), 2 if far else 1)
    stay = range(1 if far == "both" else 0, len(outs), 2 if far == "both" else 1)
    results = call(
        lambda *refs: fold_body(shapes, *refs), name, outs, ins, (), 2, after=after, through=through, near=near, stay=stay,
        limit=16,
    )
    passed = results[len(outs) :]
    return [tuple(results[at : at + 2]) for at in range(0, len(outs), 2)] + list(passed)


def local(
    tokens, encoder, out_grad, self_qkv, self_out, cross_qkv, cross_out, ffn_in, ffn_out, ln_gain, ln_bias,
    tgt_lengths, tgt_pad, src_segments,
):
    devices = lax.axis_size("dp") * lax.axis_size("fsdp")
    me = lax.axis_index(AXES)
    token_rows, encoder_rows = tokens[0], encoder[0]
    rows, width = token_rows.shape
    wide = ffn_in.shape[1]
    own = self_out.shape[0]
    blocks = width // BLOCK
    direct = devices == blocks and devices == 32
    parts = wide // width
    each = wide // blocks
    heads = width // HEAD_DIM

    number = me.astype(jnp.int32)
    if direct:
        spots = jnp.stack([jnp.int32(1), number, mirrored(number)])
    else:
        spots = jnp.zeros((3,), jnp.int32)

    square, tall = (rows, width), (width, rows)
    self_kaug, self_qaug, cross_kaug, cross_qaug, windows = call(
        prep_body, "prep",
        [((rows, TILE), BF16), ((MASK_ROWS, rows), BF16)] * 2 + [((4, rows // TILE), jnp.int32)],
        [tgt_lengths[0], tgt_pad, src_segments[0].reshape(-1, TILE)],
        (0, 1), 2, out_smem=(4,),
    )
    if direct:
        self_block, cross_block, ffn_block = call(
            pack_body, "pack",
            [((1, 3 * BLOCK, width), BF16), ((1, 6 * BLOCK, width), BF16), ((parts * BLOCK + each, width), BF16)],
            [self_qkv, self_out, cross_qkv, cross_out, ffn_in, ffn_out, ln_gain, ln_bias], (), 1,
        )
        self_pieces, (upper, lower, upper_came, lower_came) = gather_both(self_block, cross_block, (self_kaug,), devices)
        ffn_all = lax.all_gather(ffn_block, AXES, axis=0, tiled=False)
    else:
        inner_rows = jnp.concatenate([ffn_in[:, at * width : (at + 1) * width] for at in range(parts)], axis=0)
        cross_block = jnp.concatenate([cross_qkv.reshape(-1, width), cross_out, self_out], axis=0)
        self_pieces = gather_plain(self_qkv.reshape(-1, width), own, blocks)
        cross_pieces = gather_plain(cross_block, own, blocks)
        scale_all = lax.all_gather(jnp.concatenate([ln_gain, ln_bias], axis=0), AXES, axis=1, tiled=True)
        scale_all = scale_all.reshape(-1, blocks, BLOCK).transpose(1, 0, 2)
        scale_all = jnp.pad(scale_all, ((0, 0), (0, BLOCK - scale_all.shape[1]), (0, width - BLOCK)))
        lower_pieces = [
            jnp.concatenate([piece[:, 3 * BLOCK :], scale_all[at * blocks // 4 : (at + 1) * blocks // 4]], axis=1)
            for at, piece in enumerate(cross_pieces)
        ]
        cross_pieces = [piece[:, : 3 * BLOCK] for piece in cross_pieces] + lower_pieces
        inner_all = jnp.concatenate(gather_plain(inner_rows, own, blocks), axis=0)
        outer_all = jnp.concatenate(gather_plain(ffn_out, ffn_out.shape[0], blocks), axis=0)
        ffn_all = jnp.concatenate([inner_all, outer_all], axis=1)

    halves, halves_t, masses = (2, rows, width // 2), (2, width // 2, rows), (2, 8, rows)
    cross_ready = (upper, lower) if direct else ()
    saved = [(halves, BF16), (halves_t, BF16), (halves, BF16), (halves_t, BF16), (halves, BF16), (halves_t, BF16), (masses, F32)]
    pipeline = [(halves_t, BF16), ((2, rows, 2 * TILE), F32), ((2, rows, 2 * TILE), BF16)]
    queries, queries_t, keys, keys_t, values, mixed_t, log_mass, weights = call(
        self_forward_body, "self_forward", saved + [((3, width, width), BF16)],
        [*self_pieces, token_rows, self_kaug, self_qaug, spots, windows],
        (7, 8), 15, pipeline, after=cross_ready, limit=30,
    )
    if direct:
        _, (upper_came, lower_came) = call_near(
            lambda: None, "gate", [], [], 1, (mixed_t,), (upper_came, lower_came)
        )
        cross_pieces = [
            upper, upper_came, exchange(upper, 0, devices), exchange(upper_came, 0, devices),
            lower, lower_came, exchange(lower, 0, devices), exchange(lower_came, 0, devices),
        ]
    (
        hidden_one, hidden_two, first_low, cross_queries, cross_queries_t, cross_keys, cross_keys_t, cross_values,
        cross_mixed_t, cross_mass, cross_weights, scales,
    ) = call(
        cross_forward_body, "cross_forward",
        [(square, F32)] * 2 + [(square, BF16)] + saved + [((5, width, width), BF16), ((BLOCK, width), F32)],
        [*cross_pieces, token_rows, mixed_t, encoder_rows, cross_kaug, cross_qaug, spots, windows],
        (13, 14), 18, pipeline + [(square, F32)], near=(3, 7) if direct else (), limit=40,
    )
    inside = parts * BLOCK + BLOCK
    result, grad_two, scale_grads, inner_grads, outer_keep, outer_send = call(
        feed_forward_body, "feed_forward",
        [(square, BF16), (square, F32), ((8, width), F32), ((blocks, inside, width), BF16)]
        + [((blocks // 2, each, width), BF16)] * 2,
        [ffn_all, hidden_two, out_grad[0], scales, cross_mixed_t, spots],
        (5,), 30,
        [
            ((width, wide), BF16), ((wide, width), BF16), ((wide, width), BF16), ((width, wide), BF16),
            (square, BF16), ((rows, wide), BF16), ((256, wide), F32), (square, BF16), ((rows, wide), BF16), (square, BF16),
            ((8, 8, width), F32), ((blocks, inside, width), BF16), ((blocks, each, width), BF16),
        ],
        by_part=(3, 4), stay=(5,),
    )
    if direct:
        outer_came = exchange(outer_send, 0, devices)
        near_groups = [[8 * at + other for other in range(8)] for at in range(4)]
        inner_sum = lax.psum_scatter(inner_grads, AXES, scatter_dimension=0, axis_index_groups=near_groups, tiled=True)
    work = [(halves, BF16), (halves_t, BF16), (masses, F32), (halves_t, F32), (halves, F32), (halves, F32)]
    grad_one, self_branch, cross_key_low, cross_value_low, cross_keep, cross_send = call(
        cross_backward_body, "cross_backward",
        [(square, F32), (square, BF16)] + [(halves, BF16)] * 2 + [((blocks // 2, 5 * BLOCK, width), BF16)] * 2,
        [
            grad_two, (cross_weights, 3), cross_mixed_t, cross_queries_t, cross_keys, cross_kaug, cross_qaug, cross_values,
            cross_mass, cross_queries, cross_keys_t, (cross_weights, 0), scales, hidden_one, first_low, encoder_rows, mixed_t,
            scale_grads, windows, spots,
        ],
        (18, 19), 25,
        [(square, BF16), (halves, BF16)] + work + [((2, 8, width), F32), ((blocks, 5 * BLOCK, width), BF16)],
        by_part=(4,), stay=(5,),
    )

    grid = (2, 2, 2, 2)
    after = ()
    if direct:

        def cube(value):
            return value.reshape(grid + value.shape[1:])

        (outer_keep, outer_send), cross_send = fold(
            "fold_outer", [([(cube(outer_keep), cube(outer_came), 0, 0)], 0)], (self_branch,), (cross_send,), "both"
        )
        cross_came = exchange(cross_send, 0, devices)
        outer_came = exchange(outer_send, 1, devices)
        after = (outer_send,)
    query_low, key_low, value_low, self_keep, self_send = call(
        self_backward_body, "self_backward",
        [(halves, BF16)] * 3 + [((blocks // 2, 3 * BLOCK, width), BF16)] * 2,
        [
            self_branch, (cross_weights, 4), mixed_t, queries_t, keys, self_kaug, self_qaug, values, log_mass, queries, keys_t,
            token_rows, windows, spots,
        ],
        (12, 13), 25, work + [((blocks, 3 * BLOCK, width), BF16)], after=after, by_part=(3,), stay=(4,), limit=36,
    )
    after = ()
    if direct:
        (outer_keep, outer_send), (cross_keep, cross_send), self_send, inner_sum = fold(
            "fold_first",
            [([(outer_keep, outer_came, 0, 0)], 0), ([(cube(cross_keep), cube(cross_came), 0, 0)], 0)], (query_low,),
            (self_send, pltpu.with_memory_space_constraint(inner_sum, pltpu.HBM)), "in",
        )
        self_came = exchange(self_send, 0, devices)
        inner_keep, inner_send = call(
            order_body, "inner_order", [((2, inside, width), BF16)] * 2, [inner_sum, spots], (1,), 1, stay=(0, 1), limit=16,
        )
        inner_came = exchange(inner_send, 3, devices)
        outer_came = exchange(outer_send, 2, devices)
        cross_came = exchange(cross_send, 1, devices)
        ((self_keep, self_send),) = fold(
            "fold_self", [([(cube(self_keep), cube(self_came), 0, 0)], 1)], far="in"
        )
        self_came = exchange(self_send, 2, devices)
        after = (cross_send, self_send)
    (encoder_grad,) = call(
        encoder_grad_body, "encoder_grad", [(square, BF16)],
        [cross_key_low, cross_value_low, (cross_weights, slice(1, 3))], (), 4, after=after, limit=16,
    )
    if direct:
        (inner_keep, inner_send), (cross_keep, cross_send), (self_keep, self_send) = fold(
            "fold_second",
            [
                ([(inner_keep, inner_came, 0, 0)], 0), ([(cross_keep, cross_came, 0, 0)], 0),
                ([(self_keep, self_came, 0, 0)], 0),
            ],
            (encoder_grad,),
        )
        inner_came = exchange(inner_send, 4, devices)
        cross_came = exchange(cross_send, 2, devices)
        self_came = exchange(self_send, 1, devices)
        after = (cross_send, self_send)
    (tokens_grad,) = call(
        tokens_grad_body, "tokens_grad", [(square, BF16)], [grad_one, weights, query_low, key_low, value_low], (), 5,
        after=after, limit=20,
    )
    if direct:
        (ffn_in_grad, cross_out_grad), _ = call_near(
            inner_total_body, "inner_total", [((own, wide), F32), ((own, width), F32)], [inner_keep, inner_came], 1,
            stay=False,
        )
        ((rest_keep, rest_send),) = fold(
            "fold_third",
            [
                ([(cross_keep, cross_came, 0, 0), (self_keep, self_came, 5 * BLOCK, 0), (outer_keep, outer_came, 8 * BLOCK, 0)], 0),
            ],
            (tokens_grad, ffn_in_grad),
        )
        rest_came = exchange(rest_send, 3, devices)
        ((rest_keep, rest_send),) = fold("fold_fourth", [([(rest_keep, rest_came, 0, 0)], 0)])
        rest_came = exchange(rest_send, 4, devices)
        (cross_qkv_grad, self_out_grad, gain_grad, offset_grad, self_qkv_grad, ffn_out_grad), _ = call_near(
            total_body, "total",
            [
                ((3, own, width), F32), ((own, width), F32), ((3, own), F32), ((3, own), F32), ((3, own, width), F32),
                ((each, width), F32),
            ],
            [rest_keep, rest_came], 1, stay=False,
        )
    else:

        def add_up(grads, first, last, per):
            piece = grads[:, first:last].reshape(blocks, -1, per, width).transpose(1, 0, 2, 3)
            piece = piece.reshape(piece.shape[0], blocks * per, width)
            return lax.psum_scatter(piece.astype(F32), AXES, scatter_dimension=1, tiled=True)

        cross_grads = jnp.concatenate([cross_keep, cross_send], axis=0)
        self_grads = jnp.concatenate([self_keep, self_send], axis=0)
        inner_sum = add_up(inner_grads, 0, parts * BLOCK, BLOCK)
        ffn_in_grad = inner_sum.transpose(1, 0, 2).reshape(own, wide)
        ffn_out_grad = add_up(jnp.concatenate([outer_keep, outer_send], axis=0), 0, each, each)[0]
        cross_out_grad = add_up(inner_grads, parts * BLOCK, inside, BLOCK)[0]
        cross_qkv_grad = add_up(cross_grads, 0, 3 * BLOCK, BLOCK)
        self_out_grad = add_up(cross_grads, 3 * BLOCK, 4 * BLOCK, BLOCK)[0]
        scale_parts = cross_grads[:, 4 * BLOCK : 4 * BLOCK + 6, :BLOCK].astype(F32)
        scale_parts = scale_parts.transpose(1, 0, 2).reshape(6, width)
        scale_sum = lax.psum_scatter(scale_parts, AXES, scatter_dimension=1, tiled=True)
        gain_grad, offset_grad = scale_sum[:3], scale_sum[3:]
        self_qkv_grad = add_up(self_grads, 0, 3 * BLOCK, BLOCK)
    return (
        result[None], tokens_grad[None], encoder_grad[None], self_qkv_grad, self_out_grad, cross_qkv_grad,
        cross_out_grad, ffn_in_grad, ffn_out_grad, gain_grad, offset_grad,
    )


def solution(mesh):
    rows, first, second = P(AXES, None, None), P(AXES, None), P(None, AXES, None)
    columns = P(None, AXES)
    in_specs = (
        rows, rows, rows, second, first, second, first, first, first, columns, columns, first, P(AXES), first,
    )
    out_specs = (rows, rows, rows, second, first, second, first, first, first, columns, columns)
    return jax.shard_map(local, mesh=mesh, in_specs=in_specs, out_specs=out_specs, check_vma=False)
```

```python
import math

import jax
import jax.numpy as jnp
from jax import lax
from jax.experimental import pallas as pl
from jax.experimental.pallas import tpu as pltpu
from jax.sharding import PartitionSpec as P

F32 = jnp.float32
BF16 = jnp.bfloat16
HEAD_DIM = 64
PAIR = 2 * HEAD_DIM
TILE = 128
BLOCK = 16
AXES = ("dp", "fsdp")
QUERY_SCALE = math.log2(math.e) / math.sqrt(HEAD_DIM)
MASK_ROWS = 32
MASKED = -1e30
WINDOWS = (2, 4, 6, 8)
SMEM = pl.BlockSpec(memory_space=pltpu.SMEM)
ANYWHERE = pl.BlockSpec(memory_space=pl.ANY)
HBM = pl.BlockSpec(memory_space=pltpu.HBM)
VMEM = pl.BlockSpec(memory_space=pltpu.VMEM)


def dot(left, right):
    return jnp.dot(left, right, preferred_element_type=F32)


def dot_tn(left, right):
    return lax.dot_general(left, right, (((0,), (0,)), ((), ())), preferred_element_type=F32)


def dot_nt(left, right):
    return lax.dot_general(left, right, (((1,), (1,)), ((), ())), preferred_element_type=F32)


def iota(shape, axis):
    return lax.broadcasted_iota(jnp.int32, shape, axis)


def part_shape(shape, index):
    if index is None:
        return shape
    index = index if isinstance(index, tuple) else (index,)
    taken = [one.stop - one.start for one in index if isinstance(one, slice)]
    return (*taken, *shape[len(index) :])


class Copies:

    def __init__(self, semaphores):
        self.semaphores = semaphores
        self.used = 0
        self.coming = {}
        self.going = {}
        self.started = []

    def start(self, source, target):
        copy = pltpu.make_async_copy(source, target, self.semaphores.at[self.used])
        self.used += 1
        copy.start()
        return copy

    def need(self, *refs):
        for ref in refs:
            if id(ref) in self.coming:
                self.coming.pop(id(ref)).wait()

    def push(self, *refs):
        for ref in refs:
            self.started.append(self.start(*self.going.pop(id(ref))))

    def push_part(self, source, target):
        self.started.append(self.start(source, target))

    def finish(self):
        for copy in self.coming.values():
            copy.wait()
        for ref, target in self.going.values():
            self.started.append(self.start(ref, target))
        for copy in self.started:
            copy.wait()


def call(body, name, outs, ins, in_smem, micros, scratch=(), out_smem=(), after=(), by_part=(), stay=(), near=(), through=(), update=(), limit=48):
    ins = [one if isinstance(one, tuple) else (one, None) for one in ins]
    indexes = [index for _, index in ins]
    ins = [array for array, _ in ins]
    through = (*through, *update)
    in_count, out_count = len(ins), len(outs)
    moved_in = [at for at in range(in_count) if at not in in_smem and at not in near]
    moved_out = [at for at in range(out_count) if at not in out_smem and at not in by_part and at not in stay]
    ins = [pltpu.with_memory_space_constraint(one, pltpu.HBM) if at in moved_in else one for at, one in enumerate(ins)]

    def ordered(*refs):
        sources, refs = list(refs[:in_count]), refs[in_count + len(after) + len(through) :]
        targets, refs = list(refs[: out_count + len(through)]), refs[out_count + len(through) :]
        updated = targets[len(targets) - len(update) :]
        targets = targets[:out_count]
        buffers_in, refs = refs[: len(moved_in)], refs[len(moved_in) :]
        buffers_out, refs = refs[: len(moved_out)], refs[len(moved_out) :]
        copies = Copies(refs[0])
        for at, buffer in zip(moved_in, buffers_in):
            source = sources[at] if indexes[at] is None else sources[at].at[indexes[at]]
            copies.coming[id(buffer)] = copies.start(source, buffer)
            sources[at] = buffer
        for at, buffer in zip(moved_out, buffers_out):
            copies.going[id(buffer)] = (buffer, targets[at])
            targets[at] = buffer
        body(copies, *sources, *targets, *updated, *refs[1:])
        copies.finish()

    return pl.pallas_call(
        ordered,
        name=name,
        out_shape=[
            jax.ShapeDtypeStruct(shape, kind) if at in out_smem else (pltpu.VMEM if at in stay else pltpu.HBM)(shape, kind)
            for at, (shape, kind) in enumerate(outs)
        ]
        + [jax.ShapeDtypeStruct(one.shape, one.dtype) for one in through[: len(through) - len(update)]]
        + [pltpu.HBM(one.shape, one.dtype) for one in update],
        in_specs=[SMEM if at in in_smem else VMEM if at in near else HBM for at in range(in_count)]
        + [ANYWHERE] * (len(after) + len(through)),
        out_specs=[SMEM if at in out_smem else VMEM if at in stay else HBM for at in range(out_count)]
        + [ANYWHERE] * len(through),
        input_output_aliases={in_count + len(after) + at: out_count + at for at in range(len(through))},
        scratch_shapes=[pltpu.VMEM(part_shape(ins[at].shape, indexes[at]), ins[at].dtype) for at in moved_in]
        + [pltpu.VMEM(*outs[at]) for at in moved_out]
        + [pltpu.SemaphoreType.DMA((len(moved_in) + len(moved_out) + 4 * len(by_part) + len(stay) + 2 * len(update) + 1,))]
        + [pltpu.VMEM(shape, kind) for shape, kind in scratch],
        compiler_params=pltpu.CompilerParams(vmem_limit_bytes=limit * 2**20),
        cost_estimate=pl.CostEstimate(flops=int(micros * 1e9), bytes_accessed=0, transcendentals=0),
    )(*ins, *after, *through)


def call_near(body, name, outs, ins, micros, after=(), through=(), stay=True):
    count, skipped = len(ins), len(ins) + len(after) + len(through)
    after = [pltpu.with_memory_space_constraint(one, pltpu.HBM) for one in after]
    results = pl.pallas_call(
        lambda *refs: body(*refs[:count], *refs[skipped : skipped + len(outs)]),
        name=name,
        out_shape=[pltpu.VMEM(shape, kind) if stay else jax.ShapeDtypeStruct(shape, kind) for shape, kind in outs]
        + [jax.ShapeDtypeStruct(one.shape, one.dtype) for one in through],
        in_specs=[VMEM] * count + [HBM] * len(after) + [ANYWHERE] * len(through),
        out_specs=[VMEM] * len(outs) + [ANYWHERE] * len(through),
        input_output_aliases={count + len(after) + at: len(outs) + at for at in range(len(through))},
        compiler_params=pltpu.CompilerParams(vmem_limit_bytes=16 * 2**20),
        cost_estimate=pl.CostEstimate(flops=int(micros * 1e9), bytes_accessed=0, transcendentals=0),
    )(*ins, *after, *through)
    return results[: len(outs)], results[len(outs) :]


def prep_body(copies, lengths, padding, src_grid, self_kaug, self_qaug, cross_kaug, cross_qaug, windows):
    copies.need(src_grid)
    rows = self_kaug.shape[0]
    count = lengths.shape[0]
    edge = rows - padding[0]
    ends, total = [], 0
    for at in range(count):
        total = total + lengths[at]
        ends.append(total)

    def labels(places):
        found = sum((places >= end).astype(jnp.int32) for end in ends)
        return jnp.where(places < edge, found, count)

    row_ids = labels(iota((8, rows), 1))[0:1]
    mask_rows = iota((MASK_ROWS, rows), 0)
    self_qaug[...] = jnp.where(row_ids != mask_rows, 1.0, 0.0).astype(BF16)
    cross_qaug[...] = jnp.where(jnp.minimum(row_ids, count - 1) != mask_rows, 1.0, 0.0).astype(BF16)
    lanes = iota((TILE, TILE), 1)
    ones_lanes = jnp.where((lanes >= MASK_ROWS) & (lanes < MASK_ROWS + 3), 1.0, 0.0)
    for tile in range(rows // TILE):
        part = slice(tile * TILE, (tile + 1) * TILE)
        column_ids = labels(iota((TILE, TILE), 0) + tile * TILE)
        self_kaug[part, :] = jnp.where(column_ids == lanes, MASKED, ones_lanes).astype(BF16)
        source_row = src_grid[tile : tile + 1, :].astype(F32)
        source_column = jnp.broadcast_to(source_row, (TILE, TILE)).T
        cross_kaug[part, :] = jnp.where(source_column == lanes.astype(F32), MASKED, ones_lanes).astype(BF16)
    copies.push(self_kaug, self_qaug, cross_kaug, cross_qaug)
    for tile in range(rows // TILE):
        first, last = tile * TILE, tile * TILE + TILE - 1
        start, stop, first_id, last_id = 0, edge, 0, 0
        for end in ends:
            start = jnp.where(end <= first, end, start)
            first_id = first_id + jnp.where(end <= first, 1, 0)
            last_id = last_id + jnp.where(end <= last, 1, 0)
        for end in reversed(ends):
            stop = jnp.where(end > last, jnp.minimum(end, edge), stop)
        start = jnp.where(first >= edge, edge, start)
        stop = jnp.where(last >= edge, rows, stop)
        first_id = jnp.where(first < edge, jnp.minimum(first_id, count - 1), count - 1)
        last_id = jnp.where(last < edge, jnp.minimum(last_id, count - 1), count - 1)
        low = start // TILE
        windows[0, tile] = low
        windows[1, tile] = (stop + TILE - 1) // TILE - low
        source = src_grid[...]
        below = jnp.sum(jnp.where(source < first_id, 1, 0))
        upto = jnp.sum(jnp.where(source <= last_id, 1, 0))
        low = below // TILE
        windows[2, tile] = low
        windows[3, tile] = (upto + TILE - 1) // TILE - low


def pair_columns(block):
    upper = iota(block.shape, 0) < HEAD_DIM
    none = jnp.zeros_like(block)
    return jnp.concatenate([jnp.where(upper, block, none), jnp.where(upper, none, block)], axis=1)


def pair_rows(block):
    left = iota(block.shape, 1) < HEAD_DIM
    none = jnp.zeros_like(block)
    return jnp.concatenate([jnp.where(left, block, none), jnp.where(left, none, block)], axis=0)


def twice(block):
    return jnp.concatenate([block, block], axis=1)


def split_three(row):
    first = row.astype(BF16).astype(F32)
    second = (row - first).astype(BF16).astype(F32)
    third = row - first - second
    at = iota((BLOCK, row.shape[1]), 0)
    none = jnp.zeros((BLOCK, row.shape[1]), F32)
    picked = jnp.where(at == 0, first, jnp.where(at == 1, second, jnp.where(at == 2, third, none)))
    return picked.astype(BF16)


def over_windows(windows, row, rows, run):
    tiles = rows // TILE

    def one_tile(tile, _):
        low, width = windows[row, tile], windows[row + 1, tile]
        before = 0
        for most in WINDOWS:
            start = jnp.minimum(low, tiles - most) * TILE

            @pl.when((width > before) & (width <= most))
            def _():
                run(pl.multiple_of(tile * TILE, TILE), pl.multiple_of(start, TILE), most * TILE)

            before = most
        return 0

    lax.fori_loop(0, tiles, one_tile, 0)


def places(pair):
    inner = (pair % 2) * PAIR
    return pair // 2, slice(inner, inner + PAIR)


def head_places(pair, head):
    inner = (pair % 2) * PAIR + head * HEAD_DIM
    return pair // 2, slice(inner, inner + HEAD_DIM), slice((pair % 2) * 2 + head, (pair % 2) * 2 + head + 1)


def attend(windows, row, queries_t, keys, values_t, kaug, qaug, mixed_t, log_mass, scores, raised):
    halves, rows, width = keys.shape
    pairs = halves * width // PAIR

    def run(query_at, key_at, key_count):
        query_part, key_part = pl.ds(query_at, TILE), pl.ds(key_at, key_count)
        mask_part = twice(qaug[:, query_part])
        empty = jnp.zeros((PAIR - MASK_ROWS, 2 * TILE), BF16)
        ones = jnp.ones((BLOCK, key_count), BF16)
        rights, found, peaks = [], [None] * pairs, [None] * pairs
        for pair in range(pairs):
            half, part = places(pair)
            rights.append(jnp.concatenate([pair_columns(queries_t[half, part, query_part]), mask_part, empty], axis=0))

        def score(pair, at):
            half, part = places(pair)
            here, span = pl.ds(key_at + at, TILE * 2), slice(at, at + TILE * 2)
            value = dot(jnp.concatenate([keys[half, here, part], kaug[here, :]], axis=1), rights[pair])
            scores[pair % 2, span, :] = value
            most = jnp.max(value.reshape(-1, 8, 2 * TILE), axis=0)
            found[pair] = most if at == 0 else jnp.maximum(found[pair], most)

        def raise_up(pair, at):
            span = slice(at, at + TILE * 2)
            if at == 0:
                peaks[pair] = jnp.max(found[pair], axis=0, keepdims=True)
            raised[pair % 2, span, :] = jnp.exp2(scores[pair % 2, span, :] - peaks[pair]).astype(BF16)

        def mix(pair):
            half, part = places(pair)
            left = jnp.concatenate([values_t[half, part, key_part], ones], axis=0)
            mixed = dot(left, raised[pair % 2, 0:key_count, :])
            mass = mixed[PAIR : PAIR + 1]
            scale = 1.0 / mass
            logs = peaks[pair] + jnp.log2(mass)
            for head in range(2):
                spot = slice(head * TILE, (head + 1) * TILE)
                inner = slice(head * HEAD_DIM, (head + 1) * HEAD_DIM)
                half, outer, at = head_places(pair, head)
                mixed_t[half, outer, query_part] = (mixed[inner, spot] * scale[:, spot]).astype(BF16)
                log_mass[half, at, query_part] = logs[:, spot]

        for step in range(pairs + 2):
            for at in range(0, key_count, TILE * 2):
                if step < pairs:
                    score(step, at)
                if 0 <= step - 1 < pairs:
                    raise_up(step - 1, at)
                if at == 0 and 0 <= step - 2 < pairs:
                    mix(step - 2)

    over_windows(windows, row, rows, run)


def attend_back(
    windows, row, queries, queries_t, keys, keys_t, values, kaug, qaug, log_mass, delta, grad, grad_t,
    query_grad_t, key_grad, value_grad,
):
    halves, rows, width = keys.shape
    key_grad[...] = jnp.zeros_like(key_grad)
    value_grad[...] = jnp.zeros_like(value_grad)

    def run(query_at, key_at, key_count):
        query_part, key_part = pl.ds(query_at, TILE), pl.ds(key_at, key_count)
        mask_part = twice(qaug[:, query_part])
        no_mask = jnp.zeros((MASK_ROWS, 2 * TILE), BF16)
        empty = jnp.zeros((PAIR - MASK_ROWS - BLOCK, 2 * TILE), BF16)
        key_mask = kaug[key_part, :]
        for pair in range(halves * width // PAIR):
            half, part = places(pair)
            heads = [head_places(pair, head) for head in range(2)]
            masses = jnp.concatenate([log_mass[half, at, query_part] for half, _, at in heads], axis=1)
            deltas = jnp.concatenate([delta[half, at, query_part] for half, _, at in heads], axis=1)
            right = jnp.concatenate(
                [pair_columns(queries_t[half, part, query_part]), mask_part, split_three(-masses), empty], axis=0
            )
            probs = jnp.exp2(dot(jnp.concatenate([keys[half, key_part, part], key_mask], axis=1), right))
            right = jnp.concatenate(
                [pair_columns(grad_t[half, part, query_part]), no_mask, split_three(-deltas), empty], axis=0
            )
            grad_probs = dot(jnp.concatenate([values[half, key_part, part], key_mask], axis=1), right)
            grad_scores = (probs * grad_probs).astype(BF16)
            value_grad[half, key_part, part] += dot(probs.astype(BF16), pair_rows(grad[half, query_part, part]))
            key_grad[half, key_part, part] += dot(grad_scores, pair_rows(queries[half, query_part, part]))
            mixed = dot(keys_t[half, part, key_part], grad_scores)
            for head, (half, outer, _) in enumerate(heads):
                spot = slice(head * TILE, (head + 1) * TILE)
                inner = slice(head * HEAD_DIM, (head + 1) * HEAD_DIM)
                query_grad_t[half, outer, query_part] = mixed[inner, spot]

    over_windows(windows, row, rows, run)


def row_deltas(mixed_t, grad_t, delta):
    halves, width, rows = mixed_t.shape
    for half in range(halves):
        for head in range(width // HEAD_DIM):
            part = slice(head * HEAD_DIM, (head + 1) * HEAD_DIM)
            product = mixed_t[half, part, :].astype(F32) * grad_t[half, part, :].astype(F32)
            delta[half, head : head + 1, :] = jnp.sum(product, axis=0, keepdims=True)


def normalize(hidden):
    center = hidden - jnp.mean(hidden, axis=-1, keepdims=True)
    spread = jnp.mean(center * center, axis=-1, keepdims=True)
    inverse = lax.rsqrt(spread + 1e-05)
    return center * inverse, inverse


def normalize_back(incoming, normal, inverse, gain):
    scaled = incoming * gain
    average = jnp.mean(scaled, axis=-1, keepdims=True)
    along = jnp.mean(scaled * normal, axis=-1, keepdims=True)
    return inverse * (scaled - average - normal * along)


def chunks(rows, step, run):
    def one(at, _):
        run(pl.ds(pl.multiple_of(at * step, step), step))
        return 0

    lax.fori_loop(0, rows // step, one, 0)


def fold_rows(block):
    return jnp.sum(block.reshape(-1, 8, block.shape[1]), axis=0)


def mirrored(number):
    return sum(((number >> bit) & 1) << (4 - bit) for bit in range(5))


def origin(spots, spot, swapped=False):
    number = mirrored(spot)
    if swapped:
        number = (number & 25) | ((number & 2) << 1) | ((number & 4) >> 1)
    return jnp.where(spots[0] == 1, number ^ spots[1], spot)


def place(spots, block):
    return jnp.where(spots[0] == 1, mirrored(block) ^ spots[2], block)


def take_blocks(spots, pieces, row, target, swapped=False, column=0):
    each = pieces[0].shape[0]
    for spot in range(each * len(pieces)):
        start = pl.multiple_of(origin(spots, spot, swapped) * BLOCK, BLOCK)
        piece = pieces[spot // each]
        target[pl.ds(start, BLOCK), column : column + piece.shape[2]] = piece[spot % each, row : row + BLOCK, :]


def put_blocks(spots, grads, first, rows_each, row, value):
    for at in range(value.shape[0] // rows_each):
        grads[place(spots, first + at), row : row + rows_each, :] = value[at * rows_each : (at + 1) * rows_each]


def hand_out(copies, grads, keep, send):
    half = keep.shape[0]
    copies.push_part(grads.at[half : 2 * half], send)
    copies.push_part(grads.at[0:half], keep)


def pack_body(copies, self_qkv, self_out, cross_qkv, cross_out, ffn_in, ffn_out, gain, offset, self_block, cross_block, ffn_block):
    copies.need(self_qkv, self_out, cross_qkv, cross_out, ffn_in, ffn_out, gain, offset)
    width = self_out.shape[1]
    own = gain.shape[1]
    for which in range(3):
        rows = slice(which * BLOCK, (which + 1) * BLOCK)
        self_block[0, rows, :] = self_qkv[which]
        cross_block[0, rows, :] = cross_qkv[which]
    cross_block[0, 3 * BLOCK : 4 * BLOCK, :] = cross_out[...]
    cross_block[0, 4 * BLOCK : 5 * BLOCK, :] = self_out[...]
    scales = jnp.concatenate([gain[...].astype(F32), offset[...].astype(F32), jnp.zeros((BLOCK - 6, own), F32)], axis=0)
    scales = jnp.concatenate([scales, jnp.zeros((BLOCK, width - own), F32)], axis=1)
    cross_block[0, 5 * BLOCK : 6 * BLOCK, :] = scales.astype(BF16)
    parts = ffn_in.shape[1] // width
    for part in range(parts):
        ffn_block[part * BLOCK : (part + 1) * BLOCK, :] = ffn_in[:, part * width : (part + 1) * width]
    ffn_block[parts * BLOCK :, :] = ffn_out[...]
    copies.push(self_block, cross_block, ffn_block)


def lay_rows(value, target, part):
    wide = target.shape[2]
    for half in range(target.shape[0]):
        target[half, part, :] = value[:, half * wide : (half + 1) * wide]


def lay_columns(value, target, part):
    wide = target.shape[1]
    turned = value.T
    for half in range(target.shape[0]):
        target[half, :, part] = turned[half * wide : (half + 1) * wide]


def mixed_product(mixed_t, part, weight):
    wide = mixed_t.shape[1]
    return sum(dot_tn(mixed_t[half, :, part], weight[half * wide : (half + 1) * wide, :]) for half in range(mixed_t.shape[0]))


def self_forward_body(
    copies, left_one, left_two, left_three, left_four, right_one, right_two, right_three, right_four, tokens, kaug, qaug, spots, windows,
    queries, queries_t, keys, keys_t, values, mixed_t, log_mass, weights,
    values_t, scores, raised,
):
    left = (left_one, left_two, left_three, left_four)
    right = (right_one, right_two, right_three, right_four)
    copies.need(*left, *right)
    for which in range(3):
        take_blocks(spots, left, which * BLOCK, weights.at[which])
        take_blocks(spots, right, which * BLOCK, weights.at[which], True, left_one.shape[2])
    copies.push(weights)
    copies.need(tokens)

    def project(part):
        rows = tokens[part, :]
        query_rows = (dot(rows, weights[0]) * QUERY_SCALE).astype(BF16)
        lay_rows(query_rows, queries, part)
        lay_columns(query_rows, queries_t, part)
        key_rows = dot(rows, weights[1]).astype(BF16)
        lay_rows(key_rows, keys, part)
        lay_columns(key_rows, keys_t, part)
        value_rows = dot(rows, weights[2]).astype(BF16)
        lay_rows(value_rows, values, part)
        lay_columns(value_rows, values_t, part)

    chunks(tokens.shape[0], 256, project)
    copies.push(queries, queries_t, keys, keys_t, values)
    copies.need(kaug, qaug)
    attend(windows, 0, queries_t, keys, values_t, kaug, qaug, mixed_t, log_mass, scores, raised)
    copies.push(mixed_t, log_mass)


def cross_forward_body(
    copies, upper_one, upper_two, upper_three, upper_four, lower_one, lower_two, lower_three, lower_four,
    tokens, self_mixed_t, encoder, kaug, qaug, spots, windows,
    hidden, hidden_two, first_low, queries, queries_t, keys, keys_t, values, mixed_t, log_mass, weights, scales,
    values_t, scores, raised, first,
):
    upper = (upper_one, upper_two, upper_three, upper_four)
    lower = (lower_one, lower_two, lower_three, lower_four)
    copies.need(*upper, *lower)
    for which in range(3):
        take_blocks(spots, upper, which * BLOCK, weights.at[which])
    for which in range(2):
        take_blocks(spots, lower, which * BLOCK, weights.at[3 + which], True)
    each = lower_one.shape[0]
    gathered = jnp.zeros(scales.shape, F32)
    for spot in range(4 * each):
        block = lower[spot // each][spot % each, 2 * BLOCK : 3 * BLOCK, :].astype(F32)
        gathered = gathered + pltpu.roll(block, origin(spots, spot, True) * BLOCK, 1)
    scales[...] = gathered
    copies.push(weights, scales)
    gain, offset = scales[0:1, :], scales[3:4, :]
    copies.need(tokens, self_mixed_t, encoder)

    def project(part):
        rows = encoder[part, :]
        key_rows = dot(rows, weights[1]).astype(BF16)
        lay_rows(key_rows, keys, part)
        lay_columns(key_rows, keys_t, part)
        value_rows = dot(rows, weights[2]).astype(BF16)
        lay_rows(value_rows, values, part)
        lay_columns(value_rows, values_t, part)
        before = tokens[part, :].astype(F32) + mixed_product(self_mixed_t, part, weights.at[4])
        hidden[part, :] = before
        normal, _ = normalize(before)
        first_rows = normal * gain + offset
        first[part, :] = first_rows
        low_rows = first_rows.astype(BF16)
        first_low[part, :] = low_rows
        query_rows = (dot(low_rows, weights[0]) * QUERY_SCALE).astype(BF16)
        lay_rows(query_rows, queries, part)
        lay_columns(query_rows, queries_t, part)

    chunks(encoder.shape[0], 256, project)
    copies.push(hidden, first_low, queries, queries_t, keys, keys_t, values)
    copies.need(kaug, qaug)
    attend(windows, 2, queries_t, keys, values_t, kaug, qaug, mixed_t, log_mass, scores, raised)
    copies.push(mixed_t, log_mass)

    def finish(part):
        hidden_two[part, :] = first[part, :] + mixed_product(mixed_t, part, weights.at[3])

    chunks(encoder.shape[0], 256, finish)
    copies.push(hidden_two)


def feed_forward_body(
    copies, gathered, hidden, out_grad, scales, cross_mixed_t, spots,
    out, grad_two, scale_grads, inner_grads, keep, send,
    inner, outer, second_low, active, slope, branch, grad_inner, cross_branch, sums, grads, grads_out,
):
    rows, width = hidden.shape
    wide = outer.shape[0]
    parts = wide // width
    each = wide // (width // BLOCK)
    copies.need(gathered)
    for block in range(width // BLOCK):
        for part in range(parts):
            inner[block * BLOCK : (block + 1) * BLOCK, part * width : (part + 1) * width] = gathered[
                block, part * BLOCK : (part + 1) * BLOCK, :
            ]
        outer[block * each : (block + 1) * each, :] = gathered[block, parts * BLOCK : parts * BLOCK + each, :]
    sums[...] = jnp.zeros_like(sums)
    root = math.sqrt(2.0 / math.pi)
    copies.need(hidden, out_grad, scales)

    def one(part):
        normal_two, inverse_two = normalize(hidden[part, :])
        second = normal_two * scales[1:2, :] + scales[4:5, :]
        low = second.astype(BF16)
        second_low[part, :] = low
        for at in range(parts):
            span = slice(at * width, (at + 1) * width)
            value = dot(low, inner[:, span])
            cubic = (0.044715 * root) * (value * value)
            share = 0.5 * jnp.tanh(value * (cubic + root)) + 0.5
            passed = value * share
            active[part, span] = passed.astype(BF16)
            slope[:, span] = share + (passed - passed * share) * (6.0 * cubic + 2.0 * root)
        normal_three, inverse_three = normalize(second + dot(active[part, :], outer[...]))
        out[part, :] = (normal_three * scales[2:3, :] + scales[5:6, :]).astype(BF16)
        incoming = out_grad[part, :].astype(F32)
        sums[2] += fold_rows(incoming * normal_three)
        sums[5] += fold_rows(incoming)
        grad_three = normalize_back(incoming, normal_three, inverse_three, scales[2:3, :])
        grad_low = grad_three.astype(BF16)
        branch[part, :] = grad_low
        for at in range(parts):
            span = slice(at * width, (at + 1) * width)
            grad_inner[part, span] = (dot_nt(grad_low, outer[span, :]) * slope[:, span]).astype(BF16)
        grad_second = grad_three + dot_nt(grad_inner[part, :], inner[...])
        sums[1] += fold_rows(grad_second * normal_two)
        sums[4] += fold_rows(grad_second)
        result = normalize_back(grad_second, normal_two, inverse_two, scales[1:2, :])
        grad_two[part, :] = result
        cross_branch[part, :] = result.astype(BF16)

    chunks(rows, 512, one)
    scale_grads[...] = jnp.sum(sums[...], axis=1)
    copies.push(out, grad_two, scale_grads)
    inside = parts * BLOCK

    def put(first, row, value):
        for at in range(value.shape[0] // BLOCK):
            block = first + at
            spot = jnp.where(spots[0] == 1, (block % 8) * 4 + block // 8, block)
            grads[spot, row : row + BLOCK, :] = value[at * BLOCK : (at + 1) * BLOCK]

    for at in range(parts):
        span = slice(at * width, (at + 1) * width)
        put(0, at * BLOCK, dot_tn(second_low[...], grad_inner[:, span]).astype(BF16))
    copies.push_part(grads.at[:, 0:inside, :], inner_grads.at[:, 0:inside, :])
    copies.need(cross_mixed_t)
    half_width = cross_mixed_t.shape[1]
    for half in range(cross_mixed_t.shape[0]):
        put(half * half_width // BLOCK, inside, dot(cross_mixed_t[half], cross_branch[...]).astype(BF16))
    copies.push_part(grads.at[:, inside : inside + BLOCK, :], inner_grads.at[:, inside : inside + BLOCK, :])
    for at in range(parts):
        span = slice(at * width, (at + 1) * width)
        value = dot_tn(active[:, span], branch[...]).astype(BF16)
        put_blocks(spots, grads_out, at * width // each, each, 0, value)
    hand_out(copies, grads_out, keep, send)


def back_projections(grad_rows, weight, grad, grad_t):
    def one(part):
        value = dot_nt(grad_rows[part, :], weight[...]).astype(BF16)
        lay_rows(value, grad, part)
        lay_columns(value, grad_t, part)

    chunks(grad.shape[1], 256, one)


def round_grads(query_grad_t, key_grad, value_grad, query_low, key_low, value_low):
    def one(part):
        for half in range(key_low.shape[0]):
            query_low[half, part, :] = (query_grad_t[half, :, part] * HEAD_DIM**-0.5).T.astype(BF16)
            key_low[half, part, :] = (key_grad[half, part, :] * math.log(2.0)).astype(BF16)
            value_low[half, part, :] = value_grad[half, part, :].astype(BF16)

    chunks(key_low.shape[1], 256, one)


def back_product(low, part, weight):
    wide = low.shape[2]
    return sum(dot_nt(low[half, part, :], weight[:, half * wide : (half + 1) * wide]) for half in range(low.shape[0]))


def weight_grad(spots, grads, row, left, low):
    wide = low.shape[2]
    for half in range(low.shape[0]):
        value = dot_tn(left[...], low[half]).astype(BF16)
        span = slice(half * wide, (half + 1) * wide)
        for at in range(value.shape[0] // BLOCK):
            grads[place(spots, at), row : row + BLOCK, span] = value[at * BLOCK : (at + 1) * BLOCK]


def cross_backward_body(
    copies, grad_two, out_weight, mixed_t, queries_t, keys, kaug, qaug, values, log_mass, queries, keys_t,
    query_weight, scales, hidden, first_low, encoder, self_mixed_t, scale_grads, windows, spots,
    grad_one, self_branch, key_low, value_low, keep, send,
    branch, query_low, grad, grad_t, delta, query_grad_t, key_grad, value_grad, sums, grads,
):
    rows, width = hidden.shape
    copies.need(grad_two, out_weight)

    def prepare(part):
        branch[part, :] = grad_two[part, :].astype(BF16)

    chunks(rows, 256, prepare)
    back_projections(branch, out_weight, grad, grad_t)
    copies.need(mixed_t)
    row_deltas(mixed_t, grad_t, delta)
    copies.need(queries_t, keys, kaug, qaug, values, log_mass, queries, keys_t)
    attend_back(
        windows, 2, queries, queries_t, keys, keys_t, values, kaug, qaug, log_mass, delta, grad, grad_t,
        query_grad_t, key_grad, value_grad,
    )
    round_grads(query_grad_t, key_grad, value_grad, query_low, key_low, value_low)
    copies.push(key_low, value_low)
    copies.need(query_weight, scales, hidden)
    sums[...] = jnp.zeros_like(sums)

    def finish(part):
        normal, inverse = normalize(hidden[part, :])
        incoming = grad_two[part, :] + back_product(query_low, part, query_weight)
        sums[0] += fold_rows(incoming * normal)
        sums[1] += fold_rows(incoming)
        result = normalize_back(incoming, normal, inverse, scales[0:1, :])
        grad_one[part, :] = result
        self_branch[part, :] = result.astype(BF16)

    chunks(rows, 256, finish)
    copies.push(self_branch, grad_one)
    copies.need(first_low, encoder, self_mixed_t, scale_grads)
    weight_grad(spots, grads, 0, first_low, query_low)
    weight_grad(spots, grads, BLOCK, encoder, key_low)
    weight_grad(spots, grads, 2 * BLOCK, encoder, value_low)
    half_width = self_mixed_t.shape[1]
    for half in range(self_mixed_t.shape[0]):
        value = dot(self_mixed_t[half], self_branch[...]).astype(BF16)
        put_blocks(spots, grads, half * half_width // BLOCK, BLOCK, 3 * BLOCK, value)
    at = iota((BLOCK, width), 0)
    own = jnp.sum(sums[...], axis=1)
    below = jnp.concatenate([scale_grads[...], jnp.zeros_like(scale_grads)], axis=0)
    every = jnp.where(at == 0, own[0:1], jnp.where(at == 3, own[1:2], below))
    for block in range(width // BLOCK):
        shift = (width - block * BLOCK) % width
        turned = every if shift == 0 else pltpu.roll(every, shift, 1)
        grads[place(spots, block), 4 * BLOCK : 5 * BLOCK, :] = turned.astype(BF16)
    hand_out(copies, grads, keep, send)


def self_backward_body(
    copies, branch, weight, mixed_t, queries_t, keys, kaug, qaug, values, log_mass, queries, keys_t, tokens, windows, spots,
    query_low, key_low, value_low, keep, send,
    grad, grad_t, delta, query_grad_t, key_grad, value_grad, grads,
):
    copies.need(branch, weight)
    back_projections(branch, weight, grad, grad_t)
    copies.need(mixed_t)
    row_deltas(mixed_t, grad_t, delta)
    copies.need(queries_t, keys, kaug, qaug, values, log_mass, queries, keys_t)
    attend_back(
        windows, 0, queries, queries_t, keys, keys_t, values, kaug, qaug, log_mass, delta, grad, grad_t,
        query_grad_t, key_grad, value_grad,
    )
    round_grads(query_grad_t, key_grad, value_grad, query_low, key_low, value_low)
    copies.push(query_low, key_low, value_low)
    copies.need(tokens)
    for which, low in enumerate((query_low, key_low, value_low)):
        weight_grad(spots, grads, which * BLOCK, tokens, low)
    hand_out(copies, grads, keep, send)


def encoder_grad_body(copies, key_low, value_low, weights, encoder_grad):
    copies.need(key_low, value_low, weights)

    def one(part):
        value = back_product(key_low, part, weights.at[0]) + back_product(value_low, part, weights.at[1])
        encoder_grad[part, :] = value.astype(BF16)

    chunks(encoder_grad.shape[0], 256, one)
    copies.push(encoder_grad)


def tokens_grad_body(copies, grad_one, weights, query_low, key_low, value_low, tokens_grad):
    copies.need(grad_one, weights, query_low, key_low, value_low)

    def one(part):
        value = grad_one[part, :]
        for which, low in enumerate((query_low, key_low, value_low)):
            value = value + back_product(low, part, weights.at[which])
        tokens_grad[part, :] = value.astype(BF16)

    chunks(grad_one.shape[0], 256, one)
    copies.push(tokens_grad)


def fold_body(groups, copies, *refs):
    count = sum(2 * len(terms) for terms, _ in groups)
    terms_refs, results = list(refs[:count]), list(refs[count:])
    for terms, axis in groups:
        keep, send = results.pop(0), results.pop(0)
        for row, column in terms:
            kept, came = terms_refs.pop(0), terms_refs.pop(0)
            copies.need(kept)
            lead, (high, wide) = kept.shape[:-2], kept.shape[-2:]
            for number in range(math.prod(lead)):
                index, left = [], number
                for size in reversed(lead):
                    index.insert(0, left % size)
                    left //= size
                value = (kept[tuple(index)].astype(F32) + came[tuple(index)].astype(F32)).astype(BF16)
                target = keep if index.pop(axis) == 0 else send
                target[(*index, slice(row, row + high), slice(column, column + wide))] = value


def order_body(copies, total, spots, keep, send):
    copies.need(total)
    near, far = (spots[1] >> 3) & 1, (spots[1] >> 4) & 1
    for block in range(2):
        keep[block] = total[near + 2 * (far ^ block)]
        send[block] = total[(1 - near) + 2 * (far ^ block)]


def inner_total_body(keep, came, ffn_in, cross_out):
    width = cross_out.shape[1]
    parts = ffn_in.shape[1] // width

    def total(first):
        return keep[first : first + BLOCK, :].astype(F32) + came[first : first + BLOCK, :].astype(F32)

    for part in range(parts):
        ffn_in[:, part * width : (part + 1) * width] = total(part * BLOCK)
    cross_out[...] = total(parts * BLOCK)


def total_body(keep, came, cross_qkv, self_out, gain, offset, self_qkv, ffn_out):
    def total(first, rows):
        return keep[first : first + rows, :].astype(F32) + came[first : first + rows, :].astype(F32)

    for which in range(3):
        cross_qkv[which] = total(which * BLOCK, BLOCK)
        self_qkv[which] = total((5 + which) * BLOCK, BLOCK)
    self_out[...] = total(3 * BLOCK, BLOCK)
    ffn_out[...] = total(8 * BLOCK, ffn_out.shape[0])
    scales = total(4 * BLOCK, BLOCK)
    gain[...] = scales[0:3, : gain.shape[1]]
    offset[...] = scales[3:6, : offset.shape[1]]


def exchange(value, bit, devices):
    with jax.named_scope("across_" + ("core", "x", "y", "z", "zz")[bit] if bit < 5 else "across"):
        return exchange_bit(value, bit, devices)


def exchange_bit(value, bit, devices):
    return lax.ppermute(value, AXES, [(at, at ^ (1 << bit)) for at in range(devices)])


def bit_count(devices):
    return devices.bit_length() - 1


def join_body(*refs):
    count = len(refs) // 3
    for at in range(count):
        first, second, target = refs[2 * at], refs[2 * at + 1], refs[2 * count + at]
        for block in range(first.shape[0]):
            target[block] = first[block]
            target[first.shape[0] + block] = second[block]


def join(name, pairs, after=(), through=()):
    outs = [((2 * first.shape[0], *first.shape[1:]), first.dtype) for first, _ in pairs]
    return call_near(join_body, name, outs, [one for pair in pairs for one in pair], 1, after, through)


def join_split_body(by_rows, *refs):
    count = len(by_rows)
    for at, rows_cut in enumerate(by_rows):
        first, second, upper, lower = refs[2 * at], refs[2 * at + 1], refs[2 * count + 2 * at], refs[2 * count + 2 * at + 1]
        rows, width = upper.shape[1:]
        for block in range(2 * first.shape[0]):
            source = first if block < first.shape[0] else second
            spot = block % first.shape[0]
            upper[block] = source[spot, 0:rows, 0:width]
            lower[block] = source[spot, rows:, :] if rows_cut else source[spot, :, width:]


def join_split(name, pairs, by_rows, after=()):
    outs = []
    for (first, _), rows_cut in zip(pairs, by_rows):
        blocks, rows, width = first.shape
        outs += [((2 * blocks, rows // 2, width) if rows_cut else (2 * blocks, rows, width // 2), BF16)] * 2
    return call_near(lambda *refs: join_split_body(by_rows, *refs), name, outs, [one for pair in pairs for one in pair], 1, after)[0]


def gather_both(self_held, cross_held, prepared, devices):
    come, cross_come = exchange(self_held, 4, devices), exchange(cross_held, 4, devices)
    (self_held,), _ = join("join_self_one", [(self_held, come)])
    come = exchange(self_held, 3, devices)
    left, right = join_split("join_self_two", [(self_held, come)], (False,), (cross_come,))
    left_come, right_come = exchange(left, 2, devices), exchange(right, 1, devices)
    (cross_held,), _ = join("join_cross", [(cross_held, cross_come)])
    cross_come = exchange(cross_held, 3, devices)
    (left, right), _ = join("join_self_three", [(left, left_come), (right, right_come)], (prepared, cross_come))
    left_come, right_come = exchange(left, 1, devices), exchange(right, 2, devices)
    upper, lower = join_split("join_split", [(cross_held, cross_come)], (True,))
    upper_come, lower_come = exchange(upper, 2, devices), exchange(lower, 1, devices)
    (upper, lower), (left_come, right_come) = join(
        "join_halves", [(upper, upper_come), (lower, lower_come)], (), (left_come, right_come)
    )
    self_pieces = [left, left_come, exchange(left, 0, devices), exchange(left_come, 0, devices)]
    self_pieces += [right, right_come, exchange(right, 0, devices), exchange(right_come, 0, devices)]
    return self_pieces, (upper, lower, exchange(upper, 1, devices), exchange(lower, 2, devices))


def gather_plain(block, per, blocks):
    every = lax.all_gather(block, AXES, axis=0, tiled=False)
    parts = every.shape[1] // per
    every = every.reshape(every.shape[0], parts, per, every.shape[2]).transpose(1, 0, 2, 3)
    every = every.reshape(parts, blocks, -1, every.shape[3]).transpose(1, 0, 2, 3)
    every = every.reshape(blocks, -1, every.shape[3])
    return [every[at : at + blocks // 4] for at in range(0, blocks, blocks // 4)]


def fold(name, groups, after=(), through=(), far=False):
    ins, outs, shapes = [], [], []
    for terms, axis in groups:
        high = max(row + kept.shape[-2] for kept, _, row, _ in terms)
        wide = max(column + kept.shape[-1] for kept, _, _, column in terms)
        lead = list(terms[0][0].shape[:-2])
        lead.pop(axis)
        for kept, came, _, _ in terms:
            ins += [kept, came]
        outs += [((*lead, high, wide), BF16)] * 2
        shapes.append(([(row, column) for _, _, row, column in terms], axis))
    after = [pltpu.with_memory_space_constraint(one, pltpu.HBM) for one in after]
    near = range(1 if far else 0, len(ins), 2 if far else 1)
    stay = range(1 if far == "both" else 0, len(outs), 2 if far == "both" else 1)
    results = call(
        lambda *refs: fold_body(shapes, *refs), name, outs, ins, (), 2, after=after, through=through, near=near, stay=stay,
        limit=16,
    )
    passed = results[len(outs) :]
    return [tuple(results[at : at + 2]) for at in range(0, len(outs), 2)] + list(passed)


def local(
    tokens, encoder, out_grad, self_qkv, self_out, cross_qkv, cross_out, ffn_in, ffn_out, ln_gain, ln_bias,
    tgt_lengths, tgt_pad, src_segments,
):
    devices = lax.axis_size("dp") * lax.axis_size("fsdp")
    me = lax.axis_index(AXES)
    token_rows, encoder_rows = tokens[0], encoder[0]
    rows, width = token_rows.shape
    wide = ffn_in.shape[1]
    own = self_out.shape[0]
    blocks = width // BLOCK
    direct = devices == blocks and devices == 32
    parts = wide // width
    each = wide // blocks
    heads = width // HEAD_DIM

    number = me.astype(jnp.int32)
    if direct:
        spots = jnp.stack([jnp.int32(1), number, mirrored(number)])
    else:
        spots = jnp.zeros((3,), jnp.int32)

    square, tall = (rows, width), (width, rows)
    self_kaug, self_qaug, cross_kaug, cross_qaug, windows = call(
        prep_body, "prep",
        [((rows, TILE), BF16), ((MASK_ROWS, rows), BF16)] * 2 + [((4, rows // TILE), jnp.int32)],
        [tgt_lengths[0], tgt_pad, src_segments[0].reshape(-1, TILE)],
        (0, 1), 2, out_smem=(4,),
    )
    if direct:
        self_block, cross_block, ffn_block = call(
            pack_body, "pack",
            [((1, 3 * BLOCK, width), BF16), ((1, 6 * BLOCK, width), BF16), ((parts * BLOCK + each, width), BF16)],
            [self_qkv, self_out, cross_qkv, cross_out, ffn_in, ffn_out, ln_gain, ln_bias], (), 1,
        )
        self_pieces, (upper, lower, upper_came, lower_came) = gather_both(self_block, cross_block, self_kaug, devices)
        ready = (upper, lower)
        ffn_all = lax.all_gather(ffn_block, AXES, axis=0, tiled=False)
    else:
        inner_rows = jnp.concatenate([ffn_in[:, at * width : (at + 1) * width] for at in range(parts)], axis=0)
        cross_block = jnp.concatenate([cross_qkv.reshape(-1, width), cross_out, self_out], axis=0)
        self_pieces = gather_plain(self_qkv.reshape(-1, width), own, blocks)
        self_pieces = [piece[:, :, : width // 2] for piece in self_pieces] + [piece[:, :, width // 2 :] for piece in self_pieces]
        ready = ()
        cross_pieces = gather_plain(cross_block, own, blocks)
        scale_all = lax.all_gather(jnp.concatenate([ln_gain, ln_bias], axis=0), AXES, axis=1, tiled=True)
        scale_all = scale_all.reshape(-1, blocks, BLOCK).transpose(1, 0, 2)
        scale_all = jnp.pad(scale_all, ((0, 0), (0, BLOCK - scale_all.shape[1]), (0, width - BLOCK)))
        lower_pieces = [
            jnp.concatenate([piece[:, 3 * BLOCK :], scale_all[at * blocks // 4 : (at + 1) * blocks // 4]], axis=1)
            for at, piece in enumerate(cross_pieces)
        ]
        cross_pieces = [piece[:, : 3 * BLOCK] for piece in cross_pieces] + lower_pieces
        inner_all = jnp.concatenate(gather_plain(inner_rows, own, blocks), axis=0)
        outer_all = jnp.concatenate(gather_plain(ffn_out, ffn_out.shape[0], blocks), axis=0)
        ffn_all = jnp.concatenate([inner_all, outer_all], axis=1)

    halves, halves_t, masses = (2, rows, width // 2), (2, width // 2, rows), (2, 8, rows)
    saved = [(halves, BF16), (halves_t, BF16), (halves, BF16), (halves_t, BF16), (halves, BF16), (halves_t, BF16), (masses, F32)]
    pipeline = [(halves_t, BF16), ((2, rows, 2 * TILE), F32), ((2, rows, 2 * TILE), BF16)]
    queries, queries_t, keys, keys_t, values, mixed_t, log_mass, weights = call(
        self_forward_body, "self_forward", saved + [((3, width, width), BF16)],
        [*self_pieces, token_rows, self_kaug, self_qaug, spots, windows],
        (len(self_pieces) + 3, len(self_pieces) + 4), 15, pipeline, after=ready, limit=30,
    )
    if direct:
        _, (upper_came, lower_came) = call_near(
            lambda: None, "gate", [], [], 1, (mixed_t,), (upper_came, lower_came)
        )
        cross_pieces = [
            upper, upper_came, exchange(upper, 0, devices), exchange(upper_came, 0, devices),
            lower, lower_came, exchange(lower, 0, devices), exchange(lower_came, 0, devices),
        ]
    (
        hidden_one, hidden_two, first_low, cross_queries, cross_queries_t, cross_keys, cross_keys_t, cross_values,
        cross_mixed_t, cross_mass, cross_weights, scales,
    ) = call(
        cross_forward_body, "cross_forward",
        [(square, F32)] * 2 + [(square, BF16)] + saved + [((5, width, width), BF16), ((BLOCK, width), F32)],
        [*cross_pieces, token_rows, mixed_t, encoder_rows, cross_kaug, cross_qaug, spots, windows],
        (13, 14), 18, pipeline + [(square, F32)], near=(3, 7) if direct else (), limit=40,
    )
    inside = parts * BLOCK + BLOCK
    result, grad_two, scale_grads, inner_grads, outer_keep, outer_send = call(
        feed_forward_body, "feed_forward",
        [(square, BF16), (square, F32), ((8, width), F32), ((blocks, inside, width), BF16)]
        + [((blocks // 2, each, width), BF16)] * 2,
        [ffn_all, hidden_two, out_grad[0], scales, cross_mixed_t, spots],
        (5,), 30,
        [
            ((width, wide), BF16), ((wide, width), BF16),
            (square, BF16), ((rows, wide), BF16), ((512, wide), F32), (square, BF16), ((rows, wide), BF16), (square, BF16),
            ((8, 8, width), F32), ((blocks, inside, width), BF16), ((blocks, each, width), BF16),
        ],
        by_part=(3, 4), stay=(5,), limit=54,
    )
    if direct:
        outer_came = exchange(outer_send, 0, devices)
        near_groups = [[8 * at + other for other in range(8)] for at in range(4)]
        inner_sum = lax.psum_scatter(inner_grads, AXES, scatter_dimension=0, axis_index_groups=near_groups, tiled=True)
    work = [(halves, BF16), (halves_t, BF16), (masses, F32), (halves_t, F32), (halves, F32), (halves, F32)]
    grad_one, self_branch, cross_key_low, cross_value_low, cross_keep, cross_send = call(
        cross_backward_body, "cross_backward",
        [(square, F32), (square, BF16)] + [(halves, BF16)] * 2 + [((blocks // 2, 5 * BLOCK, width), BF16)] * 2,
        [
            grad_two, (cross_weights, 3), cross_mixed_t, cross_queries_t, cross_keys, cross_kaug, cross_qaug, cross_values,
            cross_mass, cross_queries, cross_keys_t, (cross_weights, 0), scales, hidden_one, first_low, encoder_rows, mixed_t,
            scale_grads, windows, spots,
        ],
        (18, 19), 25,
        [(square, BF16), (halves, BF16)] + work + [((2, 8, width), F32), ((blocks, 5 * BLOCK, width), BF16)],
        by_part=(4,), stay=(5,),
    )

    grid = (2, 2, 2, 2)
    after = ()
    if direct:

        def cube(value):
            return value.reshape(grid + value.shape[1:])

        (outer_keep, outer_send), cross_send = fold(
            "fold_outer", [([(cube(outer_keep), cube(outer_came), 0, 0)], 0)], (self_branch,), (cross_send,), "both"
        )
        cross_came = exchange(cross_send, 0, devices)
        outer_came = exchange(outer_send, 1, devices)
        after = (outer_send,)
    query_low, key_low, value_low, self_keep, self_send = call(
        self_backward_body, "self_backward",
        [(halves, BF16)] * 3 + [((blocks // 2, 3 * BLOCK, width), BF16)] * 2,
        [
            self_branch, (cross_weights, 4), mixed_t, queries_t, keys, self_kaug, self_qaug, values, log_mass, queries, keys_t,
            token_rows, windows, spots,
        ],
        (12, 13), 25, work + [((blocks, 3 * BLOCK, width), BF16)], after=after, by_part=(3,), stay=(4,), limit=36,
    )
    after = ()
    if direct:
        (outer_keep, outer_send), (cross_keep, cross_send), self_send, inner_sum = fold(
            "fold_first",
            [([(outer_keep, outer_came, 0, 0)], 0), ([(cube(cross_keep), cube(cross_came), 0, 0)], 0)], (query_low,),
            (self_send, pltpu.with_memory_space_constraint(inner_sum, pltpu.HBM)), "in",
        )
        self_came = exchange(self_send, 0, devices)
        inner_keep, inner_send = call(
            order_body, "inner_order", [((2, inside, width), BF16)] * 2, [inner_sum, spots], (1,), 1, stay=(0, 1), limit=16,
        )
        inner_came = exchange(inner_send, 3, devices)
        outer_came = exchange(outer_send, 2, devices)
        cross_came = exchange(cross_send, 1, devices)
        ((self_keep, self_send),) = fold(
            "fold_self", [([(cube(self_keep), cube(self_came), 0, 0)], 1)], far="in"
        )
        self_came = exchange(self_send, 2, devices)
        after = (cross_send, self_send)
    (encoder_grad,) = call(
        encoder_grad_body, "encoder_grad", [(square, BF16)],
        [cross_key_low, cross_value_low, (cross_weights, slice(1, 3))], (), 4, after=after, limit=16,
    )
    if direct:
        (inner_keep, inner_send), (cross_keep, cross_send), (self_keep, self_send) = fold(
            "fold_second",
            [
                ([(inner_keep, inner_came, 0, 0)], 0), ([(cross_keep, cross_came, 0, 0)], 0),
                ([(self_keep, self_came, 0, 0)], 0),
            ],
            (encoder_grad,),
        )
        inner_came = exchange(inner_send, 4, devices)
        cross_came = exchange(cross_send, 2, devices)
        self_came = exchange(self_send, 1, devices)
        after = (cross_send, self_send)
    (tokens_grad,) = call(
        tokens_grad_body, "tokens_grad", [(square, BF16)], [grad_one, weights, query_low, key_low, value_low], (), 5,
        after=after, limit=20,
    )
    if direct:
        (ffn_in_grad, cross_out_grad), _ = call_near(
            inner_total_body, "inner_total", [((own, wide), F32), ((own, width), F32)], [inner_keep, inner_came], 1,
            stay=False,
        )
        ((rest_keep, rest_send),) = fold(
            "fold_third",
            [
                ([(cross_keep, cross_came, 0, 0), (self_keep, self_came, 5 * BLOCK, 0), (outer_keep, outer_came, 8 * BLOCK, 0)], 0),
            ],
            (tokens_grad, ffn_in_grad),
        )
        rest_came = exchange(rest_send, 3, devices)
        ((rest_keep, rest_send),) = fold("fold_fourth", [([(rest_keep, rest_came, 0, 0)], 0)])
        rest_came = exchange(rest_send, 4, devices)
        (cross_qkv_grad, self_out_grad, gain_grad, offset_grad, self_qkv_grad, ffn_out_grad), _ = call_near(
            total_body, "total",
            [
                ((3, own, width), F32), ((own, width), F32), ((3, own), F32), ((3, own), F32), ((3, own, width), F32),
                ((each, width), F32),
            ],
            [rest_keep, rest_came], 1, stay=False,
        )
    else:

        def add_up(grads, first, last, per):
            piece = grads[:, first:last].reshape(blocks, -1, per, width).transpose(1, 0, 2, 3)
            piece = piece.reshape(piece.shape[0], blocks * per, width)
            return lax.psum_scatter(piece.astype(F32), AXES, scatter_dimension=1, tiled=True)

        cross_grads = jnp.concatenate([cross_keep, cross_send], axis=0)
        self_grads = jnp.concatenate([self_keep, self_send], axis=0)
        inner_sum = add_up(inner_grads, 0, parts * BLOCK, BLOCK)
        ffn_in_grad = inner_sum.transpose(1, 0, 2).reshape(own, wide)
        ffn_out_grad = add_up(jnp.concatenate([outer_keep, outer_send], axis=0), 0, each, each)[0]
        cross_out_grad = add_up(inner_grads, parts * BLOCK, inside, BLOCK)[0]
        cross_qkv_grad = add_up(cross_grads, 0, 3 * BLOCK, BLOCK)
        self_out_grad = add_up(cross_grads, 3 * BLOCK, 4 * BLOCK, BLOCK)[0]
        scale_parts = cross_grads[:, 4 * BLOCK : 4 * BLOCK + 6, :BLOCK].astype(F32)
        scale_parts = scale_parts.transpose(1, 0, 2).reshape(6, width)
        scale_sum = lax.psum_scatter(scale_parts, AXES, scatter_dimension=1, tiled=True)
        gain_grad, offset_grad = scale_sum[:3], scale_sum[3:]
        self_qkv_grad = add_up(self_grads, 0, 3 * BLOCK, BLOCK)
    return (
        result[None], tokens_grad[None], encoder_grad[None], self_qkv_grad, self_out_grad, cross_qkv_grad,
        cross_out_grad, ffn_in_grad, ffn_out_grad, gain_grad, offset_grad,
    )


def solution(mesh):
    rows, first, second = P(AXES, None, None), P(AXES, None), P(None, AXES, None)
    columns = P(None, AXES)
    in_specs = (
        rows, rows, rows, second, first, second, first, first, first, columns, columns, first, P(AXES), first,
    )
    out_specs = (rows, rows, rows, second, first, second, first, first, first, columns, columns)
    return jax.shard_map(local, mesh=mesh, in_specs=in_specs, out_specs=out_specs, check_vma=False)
```

```python
import math

import jax
import jax.numpy as jnp
from jax import lax
from jax.experimental import pallas as pl
from jax.experimental.pallas import tpu as pltpu
from jax.sharding import PartitionSpec as P

F32 = jnp.float32
BF16 = jnp.bfloat16
HEAD_DIM = 64
PAIR = 2 * HEAD_DIM
TILE = 128
BLOCK = 16
AXES = ("dp", "fsdp")
QUERY_SCALE = math.log2(math.e) / math.sqrt(HEAD_DIM)
MASK_ROWS = 32
MASKED = -1e30
STEP = 64
WINDOWS = (2, 4, 6, 8, 10, 11, 12, 14, 16)
SMEM = pl.BlockSpec(memory_space=pltpu.SMEM)
ANYWHERE = pl.BlockSpec(memory_space=pl.ANY)
HBM = pl.BlockSpec(memory_space=pltpu.HBM)
VMEM = pl.BlockSpec(memory_space=pltpu.VMEM)


def dot(left, right):
    return jnp.dot(left, right, preferred_element_type=F32)


def dot_tn(left, right):
    return lax.dot_general(left, right, (((0,), (0,)), ((), ())), preferred_element_type=F32)


def dot_nt(left, right):
    return lax.dot_general(left, right, (((1,), (1,)), ((), ())), preferred_element_type=F32)


def iota(shape, axis):
    return lax.broadcasted_iota(jnp.int32, shape, axis)


def part_shape(shape, index):
    if index is None:
        return shape
    index = index if isinstance(index, tuple) else (index,)
    taken = [one.stop - one.start for one in index if isinstance(one, slice)]
    return (*taken, *shape[len(index) :])


class Copies:

    def __init__(self, semaphores):
        self.semaphores = semaphores
        self.used = 0
        self.coming = {}
        self.going = {}
        self.started = []

    def start(self, source, target):
        copy = pltpu.make_async_copy(source, target, self.semaphores.at[self.used])
        self.used += 1
        copy.start()
        return copy

    def need(self, *refs):
        for ref in refs:
            if id(ref) in self.coming:
                self.coming.pop(id(ref)).wait()

    def push(self, *refs):
        for ref in refs:
            self.started.append(self.start(*self.going.pop(id(ref))))

    def push_part(self, source, target):
        self.started.append(self.start(source, target))

    def finish(self):
        for copy in self.coming.values():
            copy.wait()
        for ref, target in self.going.values():
            self.started.append(self.start(ref, target))
        for copy in self.started:
            copy.wait()


def call(body, name, outs, ins, in_smem, micros, scratch=(), out_smem=(), after=(), by_part=(), stay=(), near=(), through=(), update=(), carry=(), limit=48):
    ins = [one if isinstance(one, tuple) else (one, None) for one in ins]
    indexes = [index for _, index in ins]
    ins = [array for array, _ in ins]
    outs = [*outs, *[(one.shape, one.dtype) for one in carry]]
    stay = (*stay, *range(len(outs) - len(carry), len(outs)))
    after = (*after, *[pltpu.with_memory_space_constraint(one, pltpu.HBM) for one in carry])
    through = (*through, *update)
    in_count, out_count = len(ins), len(outs)
    moved_in = [at for at in range(in_count) if at not in in_smem and at not in near]
    moved_out = [at for at in range(out_count) if at not in out_smem and at not in by_part and at not in stay]
    ins = [pltpu.with_memory_space_constraint(one, pltpu.HBM) if at in moved_in else one for at, one in enumerate(ins)]

    def ordered(*refs):
        carried = refs[in_count + len(after) - len(carry) : in_count + len(after)]
        sources, refs = list(refs[:in_count]), refs[in_count + len(after) + len(through) :]
        targets, refs = list(refs[: out_count + len(through)]), refs[out_count + len(through) :]
        updated = targets[len(targets) - len(update) :]
        targets = targets[:out_count]
        carried = list(zip(carried, targets[out_count - len(carry) :]))
        targets = targets[: out_count - len(carry)]
        buffers_in, refs = refs[: len(moved_in)], refs[len(moved_in) :]
        buffers_out, refs = refs[: len(moved_out)], refs[len(moved_out) :]
        copies = Copies(refs[0])
        for at, buffer in zip(moved_in, buffers_in):
            source = sources[at] if indexes[at] is None else sources[at].at[indexes[at]]
            copies.coming[id(buffer)] = copies.start(source, buffer)
            sources[at] = buffer
        for at, buffer in zip(moved_out, buffers_out):
            copies.going[id(buffer)] = (buffer, targets[at])
            targets[at] = buffer
        for source, target in carried:
            copies.push_part(source, target)
        body(copies, *sources, *targets, *updated, *refs[1:])
        copies.finish()

    return pl.pallas_call(
        ordered,
        name=name,
        out_shape=[
            jax.ShapeDtypeStruct(shape, kind) if at in out_smem else (pltpu.VMEM if at in stay else pltpu.HBM)(shape, kind)
            for at, (shape, kind) in enumerate(outs)
        ]
        + [jax.ShapeDtypeStruct(one.shape, one.dtype) for one in through[: len(through) - len(update)]]
        + [pltpu.HBM(one.shape, one.dtype) for one in update],
        in_specs=[SMEM if at in in_smem else VMEM if at in near else HBM for at in range(in_count)]
        + [ANYWHERE] * (len(after) + len(through)),
        out_specs=[SMEM if at in out_smem else VMEM if at in stay else HBM for at in range(out_count)]
        + [ANYWHERE] * len(through),
        input_output_aliases={in_count + len(after) + at: out_count + at for at in range(len(through))},
        scratch_shapes=[pltpu.VMEM(part_shape(ins[at].shape, indexes[at]), ins[at].dtype) for at in moved_in]
        + [pltpu.VMEM(*outs[at]) for at in moved_out]
        + [pltpu.SemaphoreType.DMA((len(moved_in) + len(moved_out) + 4 * len(by_part) + len(stay) + 2 * len(update) + 1,))]
        + [pltpu.VMEM(shape, kind) for shape, kind in scratch],
        compiler_params=pltpu.CompilerParams(vmem_limit_bytes=limit * 2**20),
        cost_estimate=pl.CostEstimate(flops=int(micros * 1e9), bytes_accessed=0, transcendentals=0),
    )(*ins, *after, *through)


def call_near(body, name, outs, ins, micros, after=(), through=(), stay=True):
    count, skipped = len(ins), len(ins) + len(after) + len(through)
    after = [pltpu.with_memory_space_constraint(one, pltpu.HBM) for one in after]
    results = pl.pallas_call(
        lambda *refs: body(*refs[:count], *refs[skipped : skipped + len(outs)]),
        name=name,
        out_shape=[pltpu.VMEM(shape, kind) if stay else jax.ShapeDtypeStruct(shape, kind) for shape, kind in outs]
        + [jax.ShapeDtypeStruct(one.shape, one.dtype) for one in through],
        in_specs=[VMEM] * count + [HBM] * len(after) + [ANYWHERE] * len(through),
        out_specs=[VMEM] * len(outs) + [ANYWHERE] * len(through),
        input_output_aliases={count + len(after) + at: len(outs) + at for at in range(len(through))},
        compiler_params=pltpu.CompilerParams(vmem_limit_bytes=16 * 2**20),
        cost_estimate=pl.CostEstimate(flops=int(micros * 1e9), bytes_accessed=0, transcendentals=0),
    )(*ins, *after, *through)
    return results[: len(outs)], results[len(outs) :]


def prep_body(copies, lengths, padding, src_grid, self_kaug, self_qaug, cross_kaug, cross_qaug, windows):
    copies.need(src_grid)
    rows = self_kaug.shape[0]
    count = lengths.shape[0]
    edge = rows - padding[0]
    ends, total = [], 0
    for at in range(count):
        total = total + lengths[at]
        ends.append(total)

    def labels(places):
        found = sum((places >= end).astype(jnp.int32) for end in ends)
        return jnp.where(places < edge, found, count)

    row_ids = labels(iota((8, rows), 1))[0:1]
    mask_rows = iota((MASK_ROWS, rows), 0)
    self_qaug[...] = jnp.where(row_ids != mask_rows, 1.0, 0.0).astype(BF16)
    cross_qaug[...] = jnp.where(jnp.minimum(row_ids, count - 1) != mask_rows, 1.0, 0.0).astype(BF16)
    lanes = iota((TILE, TILE), 1)
    ones_lanes = jnp.where((lanes >= MASK_ROWS) & (lanes < MASK_ROWS + 3), 1.0, 0.0)
    for tile in range(rows // TILE):
        part = slice(tile * TILE, (tile + 1) * TILE)
        column_ids = labels(iota((TILE, TILE), 0) + tile * TILE)
        self_kaug[part, :] = jnp.where(column_ids == lanes, MASKED, ones_lanes).astype(BF16)
        source_row = src_grid[tile : tile + 1, :].astype(F32)
        source_column = jnp.broadcast_to(source_row, (TILE, TILE)).T
        cross_kaug[part, :] = jnp.where(source_column == lanes.astype(F32), MASKED, ones_lanes).astype(BF16)
    copies.push(self_kaug, self_qaug, cross_kaug, cross_qaug)
    for tile in range(rows // TILE):
        first, last = tile * TILE, tile * TILE + TILE - 1
        start, stop, first_id, last_id = 0, edge, 0, 0
        for end in ends:
            start = jnp.where(end <= first, end, start)
            first_id = first_id + jnp.where(end <= first, 1, 0)
            last_id = last_id + jnp.where(end <= last, 1, 0)
        for end in reversed(ends):
            stop = jnp.where(end > last, jnp.minimum(end, edge), stop)
        start = jnp.where(first >= edge, edge, start)
        stop = jnp.where(last >= edge, rows, stop)
        first_id = jnp.where(first < edge, jnp.minimum(first_id, count - 1), count - 1)
        last_id = jnp.where(last < edge, jnp.minimum(last_id, count - 1), count - 1)
        low = start // STEP
        windows[0, tile] = low
        windows[1, tile] = (stop + STEP - 1) // STEP - low
        source = src_grid[...]
        below = jnp.sum(jnp.where(source < first_id, 1, 0))
        upto = jnp.sum(jnp.where(source <= last_id, 1, 0))
        low = below // STEP
        windows[2, tile] = low
        windows[3, tile] = (upto + STEP - 1) // STEP - low


def pair_columns(block):
    upper = iota(block.shape, 0) < HEAD_DIM
    none = jnp.zeros_like(block)
    return jnp.concatenate([jnp.where(upper, block, none), jnp.where(upper, none, block)], axis=1)


def pair_rows(block):
    left = iota(block.shape, 1) < HEAD_DIM
    none = jnp.zeros_like(block)
    return jnp.concatenate([jnp.where(left, block, none), jnp.where(left, none, block)], axis=0)


def twice(block):
    return jnp.concatenate([block, block], axis=1)


def split_three(row):
    first = row.astype(BF16).astype(F32)
    second = (row - first).astype(BF16).astype(F32)
    third = row - first - second
    at = iota((BLOCK, row.shape[1]), 0)
    none = jnp.zeros((BLOCK, row.shape[1]), F32)
    picked = jnp.where(at == 0, first, jnp.where(at == 1, second, jnp.where(at == 2, third, none)))
    return picked.astype(BF16)


def over_windows(windows, row, rows, run):
    tiles, steps = rows // TILE, rows // STEP

    def one_tile(tile, _):
        low, width = windows[row, tile], windows[row + 1, tile]
        before = 0
        for most in WINDOWS:
            start = jnp.minimum(low, steps - most)

            @pl.when((width > before) & (width <= most))
            def _():
                run(pl.multiple_of(tile * TILE, TILE), start, most * STEP)

            before = most
        return 0

    lax.fori_loop(0, tiles, one_tile, 0)


def add_shifted(both):
    for half in range(both.shape[1]):
        value = both[0, half]
        both[1, half] = jnp.concatenate([value[:, STEP:], value[:, :STEP]], axis=1)


def shifted(start, count):
    return start % 2, pl.ds(pl.multiple_of(start // 2 * TILE, TILE), count)


def places(pair):
    inner = (pair % 2) * PAIR
    return pair // 2, slice(inner, inner + PAIR)


def head_places(pair, head):
    inner = (pair % 2) * PAIR + head * HEAD_DIM
    return pair // 2, slice(inner, inner + HEAD_DIM), slice((pair % 2) * 2 + head, (pair % 2) * 2 + head + 1)


def attend(windows, row, queries_t, keys, values_t, kaug, qaug, mixed_t, log_mass, scores, raised):
    halves, rows, width = keys.shape
    pairs = halves * width // PAIR

    def run(query_at, key_start, key_count):
        key_at = pl.multiple_of(key_start * STEP, STEP)
        side, columns = shifted(key_start, key_count)
        query_part = pl.ds(query_at, TILE)
        mask_part = twice(qaug[:, query_part])
        empty = jnp.zeros((PAIR - MASK_ROWS, 2 * TILE), BF16)
        ones = jnp.ones((BLOCK, key_count), BF16)
        rights, found, peaks = [], [None] * pairs, [None] * pairs
        for pair in range(pairs):
            half, part = places(pair)
            rights.append(jnp.concatenate([pair_columns(queries_t[half, part, query_part]), mask_part, empty], axis=0))

        def score(pair, at):
            half, part = places(pair)
            size = min(TILE * 2, key_count - at)
            here, span = pl.ds(key_at + at, size), slice(at, at + size)
            value = dot(jnp.concatenate([keys[half, here, part], kaug[here, :]], axis=1), rights[pair])
            scores[pair % 2, span, :] = value
            most = jnp.max(value.reshape(-1, 8, 2 * TILE), axis=0)
            found[pair] = most if at == 0 else jnp.maximum(found[pair], most)

        def raise_up(pair, at):
            span = slice(at, min(at + TILE * 2, key_count))
            if at == 0:
                peaks[pair] = jnp.max(found[pair], axis=0, keepdims=True)
            raised[pair % 2, span, :] = jnp.exp2(scores[pair % 2, span, :] - peaks[pair]).astype(BF16)

        def mix(pair):
            half, part = places(pair)
            left = jnp.concatenate([values_t[side, half, part, columns], ones], axis=0)
            mixed = dot(left, raised[pair % 2, 0:key_count, :])
            mass = mixed[PAIR : PAIR + 1]
            scale = 1.0 / mass
            logs = peaks[pair] + jnp.log2(mass)
            for head in range(2):
                spot = slice(head * TILE, (head + 1) * TILE)
                inner = slice(head * HEAD_DIM, (head + 1) * HEAD_DIM)
                half, outer, at = head_places(pair, head)
                mixed_t[half, outer, query_part] = (mixed[inner, spot] * scale[:, spot]).astype(BF16)
                log_mass[half, at, query_part] = logs[:, spot]

        for step in range(pairs + 2):
            for at in range(0, key_count, TILE * 2):
                if step < pairs:
                    score(step, at)
                if 0 <= step - 1 < pairs:
                    raise_up(step - 1, at)
                if at == 0 and 0 <= step - 2 < pairs:
                    mix(step - 2)

    over_windows(windows, row, rows, run)


def attend_back(
    windows, row, queries, queries_t, keys, keys_t, values, kaug, qaug, log_mass, delta, grad, grad_t,
    query_grad_t, key_grad, value_grad,
):
    halves, rows, width = keys.shape
    key_grad[...] = jnp.zeros_like(key_grad)
    value_grad[...] = jnp.zeros_like(value_grad)

    def run(query_at, key_start, key_count):
        side, columns = shifted(key_start, key_count)
        query_part, key_part = pl.ds(query_at, TILE), pl.ds(pl.multiple_of(key_start * STEP, STEP), key_count)
        mask_part = twice(qaug[:, query_part])
        no_mask = jnp.zeros((MASK_ROWS, 2 * TILE), BF16)
        empty = jnp.zeros((PAIR - MASK_ROWS - BLOCK, 2 * TILE), BF16)
        key_mask = kaug[key_part, :]
        for pair in range(halves * width // PAIR):
            half, part = places(pair)
            heads = [head_places(pair, head) for head in range(2)]
            masses = jnp.concatenate([log_mass[half, at, query_part] for half, _, at in heads], axis=1)
            deltas = jnp.concatenate([delta[half, at, query_part] for half, _, at in heads], axis=1)
            right = jnp.concatenate(
                [pair_columns(queries_t[half, part, query_part]), mask_part, split_three(-masses), empty], axis=0
            )
            probs = jnp.exp2(dot(jnp.concatenate([keys[half, key_part, part], key_mask], axis=1), right))
            right = jnp.concatenate(
                [pair_columns(grad_t[half, part, query_part]), no_mask, split_three(-deltas), empty], axis=0
            )
            grad_probs = dot(jnp.concatenate([values[half, key_part, part], key_mask], axis=1), right)
            grad_scores = (probs * grad_probs).astype(BF16)
            value_grad[half, key_part, part] += dot(probs.astype(BF16), pair_rows(grad[half, query_part, part]))
            key_grad[half, key_part, part] += dot(grad_scores, pair_rows(queries[half, query_part, part]))
            mixed = dot(keys_t[side, half, part, columns], grad_scores)
            for head, (half, outer, _) in enumerate(heads):
                spot = slice(head * TILE, (head + 1) * TILE)
                inner = slice(head * HEAD_DIM, (head + 1) * HEAD_DIM)
                query_grad_t[half, outer, query_part] = mixed[inner, spot]

    over_windows(windows, row, rows, run)


def row_deltas(mixed_t, grad_t, delta):
    halves, width, rows = mixed_t.shape
    for half in range(halves):
        for head in range(width // HEAD_DIM):
            part = slice(head * HEAD_DIM, (head + 1) * HEAD_DIM)
            product = mixed_t[half, part, :].astype(F32) * grad_t[half, part, :].astype(F32)
            delta[half, head : head + 1, :] = jnp.sum(product, axis=0, keepdims=True)


def normalize(hidden):
    center = hidden - jnp.mean(hidden, axis=-1, keepdims=True)
    spread = jnp.mean(center * center, axis=-1, keepdims=True)
    inverse = lax.rsqrt(spread + 1e-05)
    return center * inverse, inverse


def normalize_back(incoming, normal, inverse, gain):
    scaled = incoming * gain
    average = jnp.mean(scaled, axis=-1, keepdims=True)
    along = jnp.mean(scaled * normal, axis=-1, keepdims=True)
    return inverse * (scaled - average - normal * along)


def chunks(rows, step, run):
    def one(at, _):
        run(pl.ds(pl.multiple_of(at * step, step), step))
        return 0

    lax.fori_loop(0, rows // step, one, 0)


def fold_rows(block):
    return jnp.sum(block.reshape(-1, 8, block.shape[1]), axis=0)


def mirrored(number):
    return sum(((number >> bit) & 1) << (4 - bit) for bit in range(5))


def origin(spots, spot, swapped=False):
    number = mirrored(spot)
    if swapped:
        number = (number & 25) | ((number & 2) << 1) | ((number & 4) >> 1)
    return jnp.where(spots[0] == 1, number ^ spots[1], spot)


def place(spots, block):
    return jnp.where(spots[0] == 1, mirrored(block) ^ spots[2], block)


def take_blocks(spots, pieces, row, target, swapped=False, column=0):
    each = pieces[0].shape[0]
    for spot in range(each * len(pieces)):
        start = pl.multiple_of(origin(spots, spot, swapped) * BLOCK, BLOCK)
        piece = pieces[spot // each]
        target[pl.ds(start, BLOCK), column : column + piece.shape[2]] = piece[spot % each, row : row + BLOCK, :]


def put_blocks(spots, grads, first, rows_each, row, value):
    for at in range(value.shape[0] // rows_each):
        grads[place(spots, first + at), row : row + rows_each, :] = value[at * rows_each : (at + 1) * rows_each]


def hand_out(copies, grads, keep, send):
    half = keep.shape[0]
    copies.push_part(grads.at[half : 2 * half], send)
    copies.push_part(grads.at[0:half], keep)


def pack_body(copies, self_qkv, self_out, cross_qkv, cross_out, ffn_in, ffn_out, gain, offset, self_block, cross_block, ffn_block):
    copies.need(self_qkv, self_out, cross_qkv, cross_out, ffn_in, ffn_out, gain, offset)
    width = self_out.shape[1]
    own = gain.shape[1]
    for which in range(3):
        rows = slice(which * BLOCK, (which + 1) * BLOCK)
        self_block[0, rows, :] = self_qkv[which]
        cross_block[0, rows, :] = cross_qkv[which]
    cross_block[0, 3 * BLOCK : 4 * BLOCK, :] = cross_out[...]
    cross_block[0, 4 * BLOCK : 5 * BLOCK, :] = self_out[...]
    scales = jnp.concatenate([gain[...].astype(F32), offset[...].astype(F32), jnp.zeros((BLOCK - 6, own), F32)], axis=0)
    scales = jnp.concatenate([scales, jnp.zeros((BLOCK, width - own), F32)], axis=1)
    cross_block[0, 5 * BLOCK : 6 * BLOCK, :] = scales.astype(BF16)
    parts = ffn_in.shape[1] // width
    for part in range(parts):
        ffn_block[part * BLOCK : (part + 1) * BLOCK, :] = ffn_in[:, part * width : (part + 1) * width]
    ffn_block[parts * BLOCK :, :] = ffn_out[...]
    copies.push(self_block, cross_block, ffn_block)


def lay_rows(value, target, part):
    wide = target.shape[2]
    for half in range(target.shape[0]):
        target[half, part, :] = value[:, half * wide : (half + 1) * wide]


def lay_columns(value, target, part):
    wide = target.shape[1]
    turned = value.T
    for half in range(target.shape[0]):
        target[half, :, part] = turned[half * wide : (half + 1) * wide]


def mixed_product(mixed_t, part, weight):
    wide = mixed_t.shape[1]
    return sum(dot_tn(mixed_t[half, :, part], weight[half * wide : (half + 1) * wide, :]) for half in range(mixed_t.shape[0]))


def self_forward_body(
    copies, left_one, left_two, left_three, left_four, right_one, right_two, right_three, right_four, tokens, kaug, qaug, spots, windows,
    queries, queries_t, keys, keys_t, values, mixed_t, log_mass, weights,
    values_t, scores, raised,
):
    left = (left_one, left_two, left_three, left_four)
    right = (right_one, right_two, right_three, right_four)
    copies.need(*left, *right)
    for which in range(3):
        take_blocks(spots, left, which * BLOCK, weights.at[which])
        take_blocks(spots, right, which * BLOCK, weights.at[which], True, left_one.shape[2])
    copies.push(weights)
    copies.need(tokens)

    def project(part):
        rows = tokens[part, :]
        query_rows = (dot(rows, weights[0]) * QUERY_SCALE).astype(BF16)
        lay_rows(query_rows, queries, part)
        lay_columns(query_rows, queries_t, part)
        key_rows = dot(rows, weights[1]).astype(BF16)
        lay_rows(key_rows, keys, part)
        lay_columns(key_rows, keys_t, part)
        value_rows = dot(rows, weights[2]).astype(BF16)
        lay_rows(value_rows, values, part)
        lay_columns(value_rows, values_t.at[0], part)

    chunks(tokens.shape[0], 256, project)
    copies.push(queries, queries_t, keys, keys_t, values)
    add_shifted(values_t)
    copies.need(kaug, qaug)
    attend(windows, 0, queries_t, keys, values_t, kaug, qaug, mixed_t, log_mass, scores, raised)
    copies.push(mixed_t, log_mass)


def cross_forward_body(
    copies, upper_one, upper_two, upper_three, upper_four, lower_one, lower_two, lower_three, lower_four,
    tokens, self_mixed_t, encoder, kaug, qaug, spots, windows,
    hidden, hidden_two, first_low, queries, queries_t, keys, keys_t, values, mixed_t, log_mass, weights, scales,
    values_t, scores, raised, first,
):
    upper = (upper_one, upper_two, upper_three, upper_four)
    lower = (lower_one, lower_two, lower_three, lower_four)
    copies.need(*upper, *lower)
    for which in range(3):
        take_blocks(spots, upper, which * BLOCK, weights.at[which])
    for which in range(2):
        take_blocks(spots, lower, which * BLOCK, weights.at[3 + which], True)
    each = lower_one.shape[0]
    gathered = jnp.zeros(scales.shape, F32)
    for spot in range(4 * each):
        block = lower[spot // each][spot % each, 2 * BLOCK : 3 * BLOCK, :].astype(F32)
        gathered = gathered + pltpu.roll(block, origin(spots, spot, True) * BLOCK, 1)
    scales[...] = gathered
    copies.push(weights, scales)
    gain, offset = scales[0:1, :], scales[3:4, :]
    copies.need(tokens, self_mixed_t, encoder)

    def project(part):
        rows = encoder[part, :]
        key_rows = dot(rows, weights[1]).astype(BF16)
        lay_rows(key_rows, keys, part)
        lay_columns(key_rows, keys_t, part)
        value_rows = dot(rows, weights[2]).astype(BF16)
        lay_rows(value_rows, values, part)
        lay_columns(value_rows, values_t.at[0], part)
        before = tokens[part, :].astype(F32) + mixed_product(self_mixed_t, part, weights.at[4])
        hidden[part, :] = before
        normal, _ = normalize(before)
        first_rows = normal * gain + offset
        first[part, :] = first_rows
        low_rows = first_rows.astype(BF16)
        first_low[part, :] = low_rows
        query_rows = (dot(low_rows, weights[0]) * QUERY_SCALE).astype(BF16)
        lay_rows(query_rows, queries, part)
        lay_columns(query_rows, queries_t, part)

    chunks(encoder.shape[0], 256, project)
    copies.push(hidden, first_low, queries, queries_t, keys, keys_t, values)
    add_shifted(values_t)
    copies.need(kaug, qaug)
    attend(windows, 2, queries_t, keys, values_t, kaug, qaug, mixed_t, log_mass, scores, raised)
    copies.push(mixed_t, log_mass)

    def finish(part):
        hidden_two[part, :] = first[part, :] + mixed_product(mixed_t, part, weights.at[3])

    chunks(encoder.shape[0], 256, finish)
    copies.push(hidden_two)


def feed_forward_body(
    copies, gathered, hidden, out_grad, scales, cross_mixed_t, spots,
    out, grad_two, scale_grads, inner_grads, keep, send,
    inner, outer, second_low, active, slope, branch, grad_inner, cross_branch, sums, grads, grads_out,
):
    rows, width = hidden.shape
    wide = outer.shape[0]
    parts = wide // width
    each = wide // (width // BLOCK)
    copies.need(gathered)
    for block in range(width // BLOCK):
        for part in range(parts):
            inner[block * BLOCK : (block + 1) * BLOCK, part * width : (part + 1) * width] = gathered[
                block, part * BLOCK : (part + 1) * BLOCK, :
            ]
        outer[block * each : (block + 1) * each, :] = gathered[block, parts * BLOCK : parts * BLOCK + each, :]
    sums[...] = jnp.zeros_like(sums)
    root = math.sqrt(2.0 / math.pi)
    copies.need(hidden, out_grad, scales)

    def one(part):
        normal_two, inverse_two = normalize(hidden[part, :])
        second = normal_two * scales[1:2, :] + scales[4:5, :]
        low = second.astype(BF16)
        second_low[part, :] = low
        for at in range(parts):
            span = slice(at * width, (at + 1) * width)
            value = dot(low, inner[:, span])
            cubic = (0.044715 * root) * (value * value)
            share = 0.5 * jnp.tanh(value * (cubic + root)) + 0.5
            passed = value * share
            active[part, span] = passed.astype(BF16)
            slope[:, span] = share + (passed - passed * share) * (6.0 * cubic + 2.0 * root)
        normal_three, inverse_three = normalize(second + dot(active[part, :], outer[...]))
        out[part, :] = (normal_three * scales[2:3, :] + scales[5:6, :]).astype(BF16)
        incoming = out_grad[part, :].astype(F32)
        sums[2] += fold_rows(incoming * normal_three)
        sums[5] += fold_rows(incoming)
        grad_three = normalize_back(incoming, normal_three, inverse_three, scales[2:3, :])
        grad_low = grad_three.astype(BF16)
        branch[part, :] = grad_low
        for at in range(parts):
            span = slice(at * width, (at + 1) * width)
            grad_inner[part, span] = (dot_nt(grad_low, outer[span, :]) * slope[:, span]).astype(BF16)
        grad_second = grad_three + dot_nt(grad_inner[part, :], inner[...])
        sums[1] += fold_rows(grad_second * normal_two)
        sums[4] += fold_rows(grad_second)
        result = normalize_back(grad_second, normal_two, inverse_two, scales[1:2, :])
        grad_two[part, :] = result
        cross_branch[part, :] = result.astype(BF16)

    chunks(rows, 512, one)
    scale_grads[...] = jnp.sum(sums[...], axis=1)
    copies.push(out, grad_two, scale_grads)
    inside = parts * BLOCK

    def put(first, row, value):
        for at in range(value.shape[0] // BLOCK):
            block = first + at
            spot = jnp.where(spots[0] == 1, (block % 8) * 4 + block // 8, block)
            grads[spot, row : row + BLOCK, :] = value[at * BLOCK : (at + 1) * BLOCK]

    for at in range(parts):
        span = slice(at * width, (at + 1) * width)
        put(0, at * BLOCK, dot_tn(second_low[...], grad_inner[:, span]).astype(BF16))
    copies.push_part(grads.at[:, 0:inside, :], inner_grads.at[:, 0:inside, :])
    copies.need(cross_mixed_t)
    half_width = cross_mixed_t.shape[1]
    for half in range(cross_mixed_t.shape[0]):
        put(half * half_width // BLOCK, inside, dot(cross_mixed_t[half], cross_branch[...]).astype(BF16))
    copies.push_part(grads.at[:, inside : inside + BLOCK, :], inner_grads.at[:, inside : inside + BLOCK, :])
    for at in range(parts):
        span = slice(at * width, (at + 1) * width)
        value = dot_tn(active[:, span], branch[...]).astype(BF16)
        put_blocks(spots, grads_out, at * width // each, each, 0, value)
    hand_out(copies, grads_out, keep, send)


def back_projections(grad_rows, weight, grad, grad_t):
    def one(part):
        value = dot_nt(grad_rows[part, :], weight[...]).astype(BF16)
        lay_rows(value, grad, part)
        lay_columns(value, grad_t, part)

    chunks(grad.shape[1], 256, one)


def round_grads(query_grad_t, key_grad, value_grad, query_low, key_low, value_low):
    def one(part):
        for half in range(key_low.shape[0]):
            query_low[half, part, :] = (query_grad_t[half, :, part] * HEAD_DIM**-0.5).T.astype(BF16)
            key_low[half, part, :] = (key_grad[half, part, :] * math.log(2.0)).astype(BF16)
            value_low[half, part, :] = value_grad[half, part, :].astype(BF16)

    chunks(key_low.shape[1], 256, one)


def back_product(low, part, weight):
    wide = low.shape[2]
    return sum(dot_nt(low[half, part, :], weight[:, half * wide : (half + 1) * wide]) for half in range(low.shape[0]))


def weight_grad(spots, grads, row, left, low):
    wide = low.shape[2]
    for half in range(low.shape[0]):
        value = dot_tn(left[...], low[half]).astype(BF16)
        span = slice(half * wide, (half + 1) * wide)
        for at in range(value.shape[0] // BLOCK):
            grads[place(spots, at), row : row + BLOCK, span] = value[at * BLOCK : (at + 1) * BLOCK]


def cross_backward_body(
    copies, grad_two, out_weight, mixed_t, queries_t, keys, kaug, qaug, values, log_mass, queries, keys_t,
    query_weight, scales, hidden, first_low, encoder, self_mixed_t, scale_grads, windows, spots,
    grad_one, self_branch, key_low, value_low, keep, send,
    branch, query_low, keys_both, grad, grad_t, delta, query_grad_t, key_grad, value_grad, sums, grads,
):
    rows, width = hidden.shape
    copies.need(grad_two, out_weight)

    def prepare(part):
        branch[part, :] = grad_two[part, :].astype(BF16)

    chunks(rows, 256, prepare)
    back_projections(branch, out_weight, grad, grad_t)
    copies.need(mixed_t)
    row_deltas(mixed_t, grad_t, delta)
    copies.need(queries_t, keys, kaug, qaug, values, log_mass, queries, keys_t)
    keys_both[0] = keys_t[...]
    add_shifted(keys_both)
    attend_back(
        windows, 2, queries, queries_t, keys, keys_both, values, kaug, qaug, log_mass, delta, grad, grad_t,
        query_grad_t, key_grad, value_grad,
    )
    round_grads(query_grad_t, key_grad, value_grad, query_low, key_low, value_low)
    copies.push(key_low, value_low)
    copies.need(query_weight, scales, hidden)
    sums[...] = jnp.zeros_like(sums)

    def finish(part):
        normal, inverse = normalize(hidden[part, :])
        incoming = grad_two[part, :] + back_product(query_low, part, query_weight)
        sums[0] += fold_rows(incoming * normal)
        sums[1] += fold_rows(incoming)
        result = normalize_back(incoming, normal, inverse, scales[0:1, :])
        grad_one[part, :] = result
        self_branch[part, :] = result.astype(BF16)

    chunks(rows, 256, finish)
    copies.push(self_branch, grad_one)
    copies.need(first_low, encoder, self_mixed_t, scale_grads)
    weight_grad(spots, grads, 0, first_low, query_low)
    weight_grad(spots, grads, BLOCK, encoder, key_low)
    weight_grad(spots, grads, 2 * BLOCK, encoder, value_low)
    half_width = self_mixed_t.shape[1]
    for half in range(self_mixed_t.shape[0]):
        value = dot(self_mixed_t[half], self_branch[...]).astype(BF16)
        put_blocks(spots, grads, half * half_width // BLOCK, BLOCK, 3 * BLOCK, value)
    at = iota((BLOCK, width), 0)
    own = jnp.sum(sums[...], axis=1)
    below = jnp.concatenate([scale_grads[...], jnp.zeros_like(scale_grads)], axis=0)
    every = jnp.where(at == 0, own[0:1], jnp.where(at == 3, own[1:2], below))
    for block in range(width // BLOCK):
        shift = (width - block * BLOCK) % width
        turned = every if shift == 0 else pltpu.roll(every, shift, 1)
        grads[place(spots, block), 4 * BLOCK : 5 * BLOCK, :] = turned.astype(BF16)
    hand_out(copies, grads, keep, send)


def self_backward_body(
    copies, branch, weight, mixed_t, queries_t, keys, kaug, qaug, values, log_mass, queries, keys_t, tokens, windows, spots,
    query_low, key_low, value_low, keep, send,
    keys_both, grad, grad_t, delta, query_grad_t, key_grad, value_grad, grads,
):
    copies.need(branch, weight)
    back_projections(branch, weight, grad, grad_t)
    copies.need(mixed_t)
    row_deltas(mixed_t, grad_t, delta)
    copies.need(queries_t, keys, kaug, qaug, values, log_mass, queries, keys_t)
    keys_both[0] = keys_t[...]
    add_shifted(keys_both)
    attend_back(
        windows, 0, queries, queries_t, keys, keys_both, values, kaug, qaug, log_mass, delta, grad, grad_t,
        query_grad_t, key_grad, value_grad,
    )
    round_grads(query_grad_t, key_grad, value_grad, query_low, key_low, value_low)
    copies.push(query_low, key_low, value_low)
    copies.need(tokens)
    for which, low in enumerate((query_low, key_low, value_low)):
        weight_grad(spots, grads, which * BLOCK, tokens, low)
    hand_out(copies, grads, keep, send)


def encoder_grad_body(copies, key_low, value_low, weights, encoder_grad):
    copies.need(key_low, value_low, weights)

    def one(part):
        value = back_product(key_low, part, weights.at[0]) + back_product(value_low, part, weights.at[1])
        encoder_grad[part, :] = value.astype(BF16)

    chunks(encoder_grad.shape[0], 256, one)
    copies.push(encoder_grad)


def tokens_grad_body(copies, grad_one, weights, query_low, key_low, value_low, tokens_grad):
    copies.need(grad_one, weights, query_low, key_low, value_low)

    def one(part):
        value = grad_one[part, :]
        for which, low in enumerate((query_low, key_low, value_low)):
            value = value + back_product(low, part, weights.at[which])
        tokens_grad[part, :] = value.astype(BF16)

    chunks(grad_one.shape[0], 256, one)
    copies.push(tokens_grad)


def fold_body(groups, copies, *refs):
    count = sum(2 * len(terms) for terms, _ in groups)
    terms_refs, results = list(refs[:count]), list(refs[count:])
    for terms, axis in groups:
        keep, send = results.pop(0), results.pop(0)
        for row, column in terms:
            kept, came = terms_refs.pop(0), terms_refs.pop(0)
            copies.need(kept)
            lead, (high, wide) = kept.shape[:-2], kept.shape[-2:]
            for number in range(math.prod(lead)):
                index, left = [], number
                for size in reversed(lead):
                    index.insert(0, left % size)
                    left //= size
                value = (kept[tuple(index)].astype(F32) + came[tuple(index)].astype(F32)).astype(BF16)
                target = keep if index.pop(axis) == 0 else send
                target[(*index, slice(row, row + high), slice(column, column + wide))] = value


def order_body(copies, total, spots, keep, send):
    copies.need(total)
    near, far = (spots[1] >> 3) & 1, (spots[1] >> 4) & 1
    for block in range(2):
        keep[block] = total[near + 2 * (far ^ block)]
        send[block] = total[(1 - near) + 2 * (far ^ block)]


def inner_total_body(keep, came, ffn_in, cross_out):
    width = cross_out.shape[1]
    parts = ffn_in.shape[1] // width

    def total(first):
        return keep[first : first + BLOCK, :].astype(F32) + came[first : first + BLOCK, :].astype(F32)

    for part in range(parts):
        ffn_in[:, part * width : (part + 1) * width] = total(part * BLOCK)
    cross_out[...] = total(parts * BLOCK)


def total_body(keep, came, cross_qkv, self_out, gain, offset, self_qkv, ffn_out):
    def total(first, rows):
        return keep[first : first + rows, :].astype(F32) + came[first : first + rows, :].astype(F32)

    for which in range(3):
        cross_qkv[which] = total(which * BLOCK, BLOCK)
        self_qkv[which] = total((5 + which) * BLOCK, BLOCK)
    self_out[...] = total(3 * BLOCK, BLOCK)
    ffn_out[...] = total(8 * BLOCK, ffn_out.shape[0])
    scales = total(4 * BLOCK, BLOCK)
    gain[...] = scales[0:3, : gain.shape[1]]
    offset[...] = scales[3:6, : offset.shape[1]]


def exchange(value, bit, devices):
    with jax.named_scope("across_" + ("core", "x", "y", "z", "zz")[bit] if bit < 5 else "across"):
        return exchange_bit(value, bit, devices)


def exchange_bit(value, bit, devices):
    return lax.ppermute(value, AXES, [(at, at ^ (1 << bit)) for at in range(devices)])


def bit_count(devices):
    return devices.bit_length() - 1


def join_body(*refs):
    count = len(refs) // 3
    for at in range(count):
        first, second, target = refs[2 * at], refs[2 * at + 1], refs[2 * count + at]
        for block in range(first.shape[0]):
            target[block] = first[block]
            target[first.shape[0] + block] = second[block]


def join(name, pairs, after=(), through=()):
    outs = [((2 * first.shape[0], *first.shape[1:]), first.dtype) for first, _ in pairs]
    return call_near(join_body, name, outs, [one for pair in pairs for one in pair], 1, after, through)


def join_split_body(by_rows, *refs):
    count = len(by_rows)
    for at, rows_cut in enumerate(by_rows):
        first, second, upper, lower = refs[2 * at], refs[2 * at + 1], refs[2 * count + 2 * at], refs[2 * count + 2 * at + 1]
        rows, width = upper.shape[1:]
        for block in range(2 * first.shape[0]):
            source = first if block < first.shape[0] else second
            spot = block % first.shape[0]
            upper[block] = source[spot, 0:rows, 0:width]
            lower[block] = source[spot, rows:, :] if rows_cut else source[spot, :, width:]


def join_split(name, pairs, by_rows, after=()):
    outs = []
    for (first, _), rows_cut in zip(pairs, by_rows):
        blocks, rows, width = first.shape
        outs += [((2 * blocks, rows // 2, width) if rows_cut else (2 * blocks, rows, width // 2), BF16)] * 2
    return call_near(lambda *refs: join_split_body(by_rows, *refs), name, outs, [one for pair in pairs for one in pair], 1, after)[0]


def gather_both(self_held, cross_held, prepared, devices):
    come, cross_come = exchange(self_held, 4, devices), exchange(cross_held, 4, devices)
    (self_held,), _ = join("join_self_one", [(self_held, come)])
    come = exchange(self_held, 3, devices)
    left, right = join_split("join_self_two", [(self_held, come)], (False,), (cross_come,))
    left_come, right_come = exchange(left, 2, devices), exchange(right, 1, devices)
    (cross_held,), _ = join("join_cross", [(cross_held, cross_come)])
    cross_come = exchange(cross_held, 3, devices)
    (left, right), _ = join("join_self_three", [(left, left_come), (right, right_come)], (prepared, cross_come))
    left_come, right_come = exchange(left, 1, devices), exchange(right, 2, devices)
    upper, lower = join_split("join_split", [(cross_held, cross_come)], (True,))
    upper_come, lower_come = exchange(upper, 2, devices), exchange(lower, 1, devices)
    (upper, lower), (left_come, right_come) = join(
        "join_halves", [(upper, upper_come), (lower, lower_come)], (), (left_come, right_come)
    )
    self_pieces = [left, left_come, exchange(left, 0, devices), exchange(left_come, 0, devices)]
    self_pieces += [right, right_come, exchange(right, 0, devices), exchange(right_come, 0, devices)]
    return self_pieces, (upper, lower, exchange(upper, 1, devices), exchange(lower, 2, devices))


def gather_plain(block, per, blocks):
    every = lax.all_gather(block, AXES, axis=0, tiled=False)
    parts = every.shape[1] // per
    every = every.reshape(every.shape[0], parts, per, every.shape[2]).transpose(1, 0, 2, 3)
    every = every.reshape(parts, blocks, -1, every.shape[3]).transpose(1, 0, 2, 3)
    every = every.reshape(blocks, -1, every.shape[3])
    return [every[at : at + blocks // 4] for at in range(0, blocks, blocks // 4)]


def fold(name, groups, after=(), through=(), far=False, from_far=False):
    ins, outs, shapes = [], [], []
    for terms, axis in groups:
        high = max(row + kept.shape[-2] for kept, _, row, _ in terms)
        wide = max(column + kept.shape[-1] for kept, _, _, column in terms)
        lead = list(terms[0][0].shape[:-2])
        lead.pop(axis)
        for kept, came, _, _ in terms:
            ins += [kept, came]
        outs += [((*lead, high, wide), BF16)] * 2
        shapes.append(([(row, column) for _, _, row, column in terms], axis))
    after = [pltpu.with_memory_space_constraint(one, pltpu.HBM) for one in after]
    near = range(1 if from_far else 0, len(ins), 2 if from_far else 1)
    stay = range(1 if far else 0, len(outs), 2 if far else 1)
    results = call(
        lambda *refs: fold_body(shapes, *refs), name, outs, ins, (), 2, after=after, through=through, near=near, stay=stay,
        limit=16,
    )
    passed = results[len(outs) :]
    return [tuple(results[at : at + 2]) for at in range(0, len(outs), 2)] + list(passed)


def local(
    tokens, encoder, out_grad, self_qkv, self_out, cross_qkv, cross_out, ffn_in, ffn_out, ln_gain, ln_bias,
    tgt_lengths, tgt_pad, src_segments,
):
    devices = lax.axis_size("dp") * lax.axis_size("fsdp")
    me = lax.axis_index(AXES)
    token_rows, encoder_rows = tokens[0], encoder[0]
    rows, width = token_rows.shape
    wide = ffn_in.shape[1]
    own = self_out.shape[0]
    blocks = width // BLOCK
    direct = devices == blocks and devices == 32
    parts = wide // width
    each = wide // blocks
    heads = width // HEAD_DIM

    number = me.astype(jnp.int32)
    if direct:
        spots = jnp.stack([jnp.int32(1), number, mirrored(number)])
    else:
        spots = jnp.zeros((3,), jnp.int32)

    square, tall = (rows, width), (width, rows)
    self_kaug, self_qaug, cross_kaug, cross_qaug, windows = call(
        prep_body, "prep",
        [((rows, TILE), BF16), ((MASK_ROWS, rows), BF16)] * 2 + [((4, rows // TILE), jnp.int32)],
        [tgt_lengths[0], tgt_pad, src_segments[0].reshape(-1, TILE)],
        (0, 1), 2, out_smem=(4,),
    )
    if direct:
        self_block, cross_block, ffn_block = call(
            pack_body, "pack",
            [((1, 3 * BLOCK, width), BF16), ((1, 6 * BLOCK, width), BF16), ((parts * BLOCK + each, width), BF16)],
            [self_qkv, self_out, cross_qkv, cross_out, ffn_in, ffn_out, ln_gain, ln_bias], (), 1,
        )
        self_pieces, (upper, lower, upper_came, lower_came) = gather_both(self_block, cross_block, self_kaug, devices)
        ready = (upper, lower)
        ffn_all = lax.all_gather(ffn_block, AXES, axis=0, tiled=False)
    else:
        inner_rows = jnp.concatenate([ffn_in[:, at * width : (at + 1) * width] for at in range(parts)], axis=0)
        cross_block = jnp.concatenate([cross_qkv.reshape(-1, width), cross_out, self_out], axis=0)
        self_pieces = gather_plain(self_qkv.reshape(-1, width), own, blocks)
        self_pieces = [piece[:, :, : width // 2] for piece in self_pieces] + [piece[:, :, width // 2 :] for piece in self_pieces]
        ready = ()
        cross_pieces = gather_plain(cross_block, own, blocks)
        scale_all = lax.all_gather(jnp.concatenate([ln_gain, ln_bias], axis=0), AXES, axis=1, tiled=True)
        scale_all = scale_all.reshape(-1, blocks, BLOCK).transpose(1, 0, 2)
        scale_all = jnp.pad(scale_all, ((0, 0), (0, BLOCK - scale_all.shape[1]), (0, width - BLOCK)))
        lower_pieces = [
            jnp.concatenate([piece[:, 3 * BLOCK :], scale_all[at * blocks // 4 : (at + 1) * blocks // 4]], axis=1)
            for at, piece in enumerate(cross_pieces)
        ]
        cross_pieces = [piece[:, : 3 * BLOCK] for piece in cross_pieces] + lower_pieces
        inner_all = jnp.concatenate(gather_plain(inner_rows, own, blocks), axis=0)
        outer_all = jnp.concatenate(gather_plain(ffn_out, ffn_out.shape[0], blocks), axis=0)
        ffn_all = jnp.concatenate([inner_all, outer_all], axis=1)

    halves, halves_t, masses = (2, rows, width // 2), (2, width // 2, rows), (2, 8, rows)
    saved = [(halves, BF16), (halves_t, BF16), (halves, BF16), (halves_t, BF16), (halves, BF16), (halves_t, BF16), (masses, F32)]
    both_t = (2, *halves_t)
    pipeline = [(both_t, BF16), ((2, rows, 2 * TILE), F32), ((2, rows, 2 * TILE), BF16)]
    queries, queries_t, keys, keys_t, values, mixed_t, log_mass, weights = call(
        self_forward_body, "self_forward", saved + [((3, width, width), BF16)],
        [*self_pieces, token_rows, self_kaug, self_qaug, spots, windows],
        (len(self_pieces) + 3, len(self_pieces) + 4), 15, pipeline, after=ready, limit=30,
    )
    if direct:
        _, (upper_came, lower_came) = call_near(
            lambda: None, "gate", [], [], 1, (mixed_t,), (upper_came, lower_came)
        )
        cross_pieces = [
            upper, upper_came, exchange(upper, 0, devices), exchange(upper_came, 0, devices),
            lower, lower_came, exchange(lower, 0, devices), exchange(lower_came, 0, devices),
        ]
    (
        hidden_one, hidden_two, first_low, cross_queries, cross_queries_t, cross_keys, cross_keys_t, cross_values,
        cross_mixed_t, cross_mass, cross_weights, scales,
    ) = call(
        cross_forward_body, "cross_forward",
        [(square, F32)] * 2 + [(square, BF16)] + saved + [((5, width, width), BF16), ((BLOCK, width), F32)],
        [*cross_pieces, token_rows, mixed_t, encoder_rows, cross_kaug, cross_qaug, spots, windows],
        (13, 14), 18, pipeline + [(square, F32)], near=(3, 7) if direct else (), limit=40,
    )
    inside = parts * BLOCK + BLOCK
    result, grad_two, scale_grads, inner_grads, outer_keep, outer_send = call(
        feed_forward_body, "feed_forward",
        [(square, BF16), (square, F32), ((8, width), F32), ((blocks, inside, width), BF16)]
        + [((blocks // 2, each, width), BF16)] * 2,
        [ffn_all, hidden_two, out_grad[0], scales, cross_mixed_t, spots],
        (5,), 30,
        [
            ((width, wide), BF16), ((wide, width), BF16),
            (square, BF16), ((rows, wide), BF16), ((512, wide), F32), (square, BF16), ((rows, wide), BF16), (square, BF16),
            ((8, 8, width), F32), ((blocks, inside, width), BF16), ((blocks, each, width), BF16),
        ],
        by_part=(3, 4), stay=(5,), limit=54,
    )
    if direct:
        outer_came = exchange(outer_send, 0, devices)
        near_groups = [[8 * at + other for other in range(8)] for at in range(4)]
        inner_sum = lax.psum_scatter(inner_grads, AXES, scatter_dimension=0, axis_index_groups=near_groups, tiled=True)
    work = [(both_t, BF16), (halves, BF16), (halves_t, BF16), (masses, F32), (halves_t, F32), (halves, F32), (halves, F32)]
    grad_one, self_branch, cross_key_low, cross_value_low, cross_keep, cross_send, *carried = call(
        cross_backward_body, "cross_backward",
        [(square, F32), (square, BF16)] + [(halves, BF16)] * 2 + [((blocks // 2, 5 * BLOCK, width), BF16)] * 2,
        [
            grad_two, (cross_weights, 3), cross_mixed_t, cross_queries_t, cross_keys, cross_kaug, cross_qaug, cross_values,
            cross_mass, cross_queries, cross_keys_t, (cross_weights, 0), scales, hidden_one, first_low, encoder_rows, mixed_t,
            scale_grads, windows, spots,
        ],
        (18, 19), 25,
        [(square, BF16), (halves, BF16)] + work + [((2, 8, width), F32), ((blocks, 5 * BLOCK, width), BF16)],
        by_part=(4,), stay=(5,), carry=(outer_keep,) if direct else (),
    )

    grid = (2, 2, 2, 2)
    after = ()
    if direct:

        def cube(value):
            return value.reshape(grid + value.shape[1:])

        (outer_keep,) = carried
        (outer_keep, outer_send), cross_send = fold(
            "fold_outer", [([(cube(outer_keep), cube(outer_came), 0, 0)], 0)], (self_branch,), (cross_send,), True
        )
        cross_came = exchange(cross_send, 0, devices)
        outer_came = exchange(outer_send, 1, devices)
        after = (outer_send,)
    query_low, key_low, value_low, self_keep, self_send = call(
        self_backward_body, "self_backward",
        [(halves, BF16)] * 3 + [((blocks // 2, 3 * BLOCK, width), BF16)] * 2,
        [
            self_branch, (cross_weights, 4), mixed_t, queries_t, keys, self_kaug, self_qaug, values, log_mass, queries, keys_t,
            token_rows, windows, spots,
        ],
        (12, 13), 25, work + [((blocks, 3 * BLOCK, width), BF16)], after=after, stay=(3, 4), limit=36,
    )
    after = ()
    if direct:
        (outer_keep, outer_send), (cross_keep, cross_send), self_send = fold(
            "fold_first",
            [([(outer_keep, outer_came, 0, 0)], 0), ([(cube(cross_keep), cube(cross_came), 0, 0)], 0)], (query_low,),
            (self_send,), from_far=True,
        )
        self_came = exchange(self_send, 0, devices)
        inner_keep, inner_send = call(
            order_body, "inner_order", [((2, inside, width), BF16)] * 2, [inner_sum, spots], (1,), 1, stay=(0, 1), limit=16,
        )
        inner_came = exchange(inner_send, 3, devices)
        outer_came = exchange(outer_send, 2, devices)
        cross_came = exchange(cross_send, 1, devices)
        (self_keep, self_send), inner_sum = fold(
            "fold_self", [([(cube(self_keep), cube(self_came), 0, 0)], 1)], (),
            (pltpu.with_memory_space_constraint(inner_sum, pltpu.HBM),),
        )
        self_came = exchange(self_send, 2, devices)
        after = (cross_send, self_send)
    (encoder_grad,) = call(
        encoder_grad_body, "encoder_grad", [(square, BF16)],
        [cross_key_low, cross_value_low, (cross_weights, slice(1, 3))], (), 4, after=after, limit=16,
    )
    if direct:
        (inner_keep, inner_send), (cross_keep, cross_send), (self_keep, self_send) = fold(
            "fold_second",
            [
                ([(inner_keep, inner_came, 0, 0)], 0), ([(cross_keep, cross_came, 0, 0)], 0),
                ([(self_keep, self_came, 0, 0)], 0),
            ],
            (encoder_grad,),
        )
        inner_came = exchange(inner_send, 4, devices)
        cross_came = exchange(cross_send, 2, devices)
        self_came = exchange(self_send, 1, devices)
        after = (cross_send, self_send)
    (tokens_grad,) = call(
        tokens_grad_body, "tokens_grad", [(square, BF16)], [grad_one, weights, query_low, key_low, value_low], (), 5,
        after=after, limit=20,
    )
    if direct:
        (ffn_in_grad, cross_out_grad), _ = call_near(
            inner_total_body, "inner_total", [((own, wide), F32), ((own, width), F32)], [inner_keep, inner_came], 1,
            stay=False,
        )
        ((rest_keep, rest_send),) = fold(
            "fold_third",
            [
                ([(cross_keep, cross_came, 0, 0), (self_keep, self_came, 5 * BLOCK, 0), (outer_keep, outer_came, 8 * BLOCK, 0)], 0),
            ],
            (tokens_grad, ffn_in_grad),
        )
        rest_came = exchange(rest_send, 3, devices)
        ((rest_keep, rest_send),) = fold("fold_fourth", [([(rest_keep, rest_came, 0, 0)], 0)])
        rest_came = exchange(rest_send, 4, devices)
        (cross_qkv_grad, self_out_grad, gain_grad, offset_grad, self_qkv_grad, ffn_out_grad), _ = call_near(
            total_body, "total",
            [
                ((3, own, width), F32), ((own, width), F32), ((3, own), F32), ((3, own), F32), ((3, own, width), F32),
                ((each, width), F32),
            ],
            [rest_keep, rest_came], 1, stay=False,
        )
    else:

        def add_up(grads, first, last, per):
            piece = grads[:, first:last].reshape(blocks, -1, per, width).transpose(1, 0, 2, 3)
            piece = piece.reshape(piece.shape[0], blocks * per, width)
            return lax.psum_scatter(piece.astype(F32), AXES, scatter_dimension=1, tiled=True)

        cross_grads = jnp.concatenate([cross_keep, cross_send], axis=0)
        self_grads = jnp.concatenate([self_keep, self_send], axis=0)
        inner_sum = add_up(inner_grads, 0, parts * BLOCK, BLOCK)
        ffn_in_grad = inner_sum.transpose(1, 0, 2).reshape(own, wide)
        ffn_out_grad = add_up(jnp.concatenate([outer_keep, outer_send], axis=0), 0, each, each)[0]
        cross_out_grad = add_up(inner_grads, parts * BLOCK, inside, BLOCK)[0]
        cross_qkv_grad = add_up(cross_grads, 0, 3 * BLOCK, BLOCK)
        self_out_grad = add_up(cross_grads, 3 * BLOCK, 4 * BLOCK, BLOCK)[0]
        scale_parts = cross_grads[:, 4 * BLOCK : 4 * BLOCK + 6, :BLOCK].astype(F32)
        scale_parts = scale_parts.transpose(1, 0, 2).reshape(6, width)
        scale_sum = lax.psum_scatter(scale_parts, AXES, scatter_dimension=1, tiled=True)
        gain_grad, offset_grad = scale_sum[:3], scale_sum[3:]
        self_qkv_grad = add_up(self_grads, 0, 3 * BLOCK, BLOCK)
    return (
        result[None], tokens_grad[None], encoder_grad[None], self_qkv_grad, self_out_grad, cross_qkv_grad,
        cross_out_grad, ffn_in_grad, ffn_out_grad, gain_grad, offset_grad,
    )


def solution(mesh):
    rows, first, second = P(AXES, None, None), P(AXES, None), P(None, AXES, None)
    columns = P(None, AXES)
    in_specs = (
        rows, rows, rows, second, first, second, first, first, first, columns, columns, first, P(AXES), first,
    )
    out_specs = (rows, rows, rows, second, first, second, first, first, first, columns, columns)
    return jax.shard_map(local, mesh=mesh, in_specs=in_specs, out_specs=out_specs, check_vma=False)
```

```python
import math

import jax
import jax.numpy as jnp
from jax import lax
from jax.experimental import pallas as pl
from jax.experimental.pallas import tpu as pltpu
from jax.sharding import PartitionSpec as P

F32 = jnp.float32
BF16 = jnp.bfloat16
HEAD_DIM = 64
PAIR = 2 * HEAD_DIM
TILE = 128
BLOCK = 16
AXES = ("dp", "fsdp")
QUERY_SCALE = math.log2(math.e) / math.sqrt(HEAD_DIM)
MASK_ROWS = 32
MASKED = -1e30
STEP = 64
WINDOWS = (2, 4, 6, 8, 10, 11, 12, 14, 16)
SMEM = pl.BlockSpec(memory_space=pltpu.SMEM)
ANYWHERE = pl.BlockSpec(memory_space=pl.ANY)
HBM = pl.BlockSpec(memory_space=pltpu.HBM)
VMEM = pl.BlockSpec(memory_space=pltpu.VMEM)


def dot(left, right):
    return jnp.dot(left, right, preferred_element_type=F32)


def dot_tn(left, right):
    return lax.dot_general(left, right, (((0,), (0,)), ((), ())), preferred_element_type=F32)


def dot_nt(left, right):
    return lax.dot_general(left, right, (((1,), (1,)), ((), ())), preferred_element_type=F32)


def iota(shape, axis):
    return lax.broadcasted_iota(jnp.int32, shape, axis)


def part_shape(shape, index):
    if index is None:
        return shape
    index = index if isinstance(index, tuple) else (index,)
    taken = [one.stop - one.start for one in index if isinstance(one, slice)]
    return (*taken, *shape[len(index) :])


class Copies:

    def __init__(self, semaphores):
        self.semaphores = semaphores
        self.used = 0
        self.coming = {}
        self.going = {}
        self.started = []

    def start(self, source, target):
        copy = pltpu.make_async_copy(source, target, self.semaphores.at[self.used])
        self.used += 1
        copy.start()
        return copy

    def need(self, *refs):
        for ref in refs:
            if id(ref) in self.coming:
                self.coming.pop(id(ref)).wait()

    def push(self, *refs):
        for ref in refs:
            self.started.append(self.start(*self.going.pop(id(ref))))

    def push_part(self, source, target):
        self.started.append(self.start(source, target))

    def finish(self):
        for copy in self.coming.values():
            copy.wait()
        for ref, target in self.going.values():
            self.started.append(self.start(ref, target))
        for copy in self.started:
            copy.wait()


def call(body, name, outs, ins, in_smem, micros, scratch=(), out_smem=(), after=(), by_part=(), stay=(), near=(), through=(), update=(), carry=(), far=(), limit=48):
    ins = [one if isinstance(one, tuple) else (one, None) for one in ins]
    indexes = [index for _, index in ins]
    ins = [array for array, _ in ins]
    outs = [*outs, *[(one.shape, one.dtype) for one in carry]]
    stay = (*stay, *range(len(outs) - len(carry), len(outs)))
    after = (*after, *[pltpu.with_memory_space_constraint(one, pltpu.HBM) for one in carry])
    through = (*through, *update)
    in_count, out_count = len(ins), len(outs)
    moved_in = [at for at in range(in_count) if at not in in_smem and at not in near and at not in far]
    moved_out = [at for at in range(out_count) if at not in out_smem and at not in by_part and at not in stay]
    ins = [pltpu.with_memory_space_constraint(one, pltpu.HBM) if at in moved_in or at in far else one for at, one in enumerate(ins)]

    def ordered(*refs):
        carried = refs[in_count + len(after) - len(carry) : in_count + len(after)]
        sources, refs = list(refs[:in_count]), refs[in_count + len(after) + len(through) :]
        targets, refs = list(refs[: out_count + len(through)]), refs[out_count + len(through) :]
        updated = targets[len(targets) - len(update) :]
        targets = targets[:out_count]
        carried = list(zip(carried, targets[out_count - len(carry) :]))
        targets = targets[: out_count - len(carry)]
        buffers_in, refs = refs[: len(moved_in)], refs[len(moved_in) :]
        buffers_out, refs = refs[: len(moved_out)], refs[len(moved_out) :]
        copies = Copies(refs[0])
        for at, buffer in zip(moved_in, buffers_in):
            source = sources[at] if indexes[at] is None else sources[at].at[indexes[at]]
            copies.coming[id(buffer)] = copies.start(source, buffer)
            sources[at] = buffer
        for at, buffer in zip(moved_out, buffers_out):
            copies.going[id(buffer)] = (buffer, targets[at])
            targets[at] = buffer
        for source, target in carried:
            copies.push_part(source, target)
        body(copies, *sources, *targets, *updated, *refs[1:])
        copies.finish()

    return pl.pallas_call(
        ordered,
        name=name,
        out_shape=[
            jax.ShapeDtypeStruct(shape, kind) if at in out_smem else (pltpu.VMEM if at in stay else pltpu.HBM)(shape, kind)
            for at, (shape, kind) in enumerate(outs)
        ]
        + [jax.ShapeDtypeStruct(one.shape, one.dtype) for one in through[: len(through) - len(update)]]
        + [pltpu.HBM(one.shape, one.dtype) for one in update],
        in_specs=[SMEM if at in in_smem else VMEM if at in near else HBM for at in range(in_count)]
        + [ANYWHERE] * (len(after) + len(through)),
        out_specs=[SMEM if at in out_smem else VMEM if at in stay else HBM for at in range(out_count)]
        + [ANYWHERE] * len(through),
        input_output_aliases={in_count + len(after) + at: out_count + at for at in range(len(through))},
        scratch_shapes=[pltpu.VMEM(part_shape(ins[at].shape, indexes[at]), ins[at].dtype) for at in moved_in]
        + [pltpu.VMEM(*outs[at]) for at in moved_out]
        + [pltpu.SemaphoreType.DMA((len(moved_in) + len(moved_out) + 4 * len(by_part) + len(stay) + 2 * len(update) + len(far) + 1,))]
        + [pltpu.VMEM(shape, kind) for shape, kind in scratch],
        compiler_params=pltpu.CompilerParams(vmem_limit_bytes=limit * 2**20),
        cost_estimate=pl.CostEstimate(flops=int(micros * 1e9), bytes_accessed=0, transcendentals=0),
    )(*ins, *after, *through)


def call_near(body, name, outs, ins, micros, after=(), through=(), stay=True):
    count, skipped = len(ins), len(ins) + len(after) + len(through)
    after = [pltpu.with_memory_space_constraint(one, pltpu.HBM) for one in after]
    results = pl.pallas_call(
        lambda *refs: body(*refs[:count], *refs[skipped : skipped + len(outs)]),
        name=name,
        out_shape=[pltpu.VMEM(shape, kind) if stay else jax.ShapeDtypeStruct(shape, kind) for shape, kind in outs]
        + [jax.ShapeDtypeStruct(one.shape, one.dtype) for one in through],
        in_specs=[VMEM] * count + [HBM] * len(after) + [ANYWHERE] * len(through),
        out_specs=[VMEM] * len(outs) + [ANYWHERE] * len(through),
        input_output_aliases={count + len(after) + at: len(outs) + at for at in range(len(through))},
        compiler_params=pltpu.CompilerParams(vmem_limit_bytes=16 * 2**20),
        cost_estimate=pl.CostEstimate(flops=int(micros * 1e9), bytes_accessed=0, transcendentals=0),
    )(*ins, *after, *through)
    return results[: len(outs)], results[len(outs) :]


def prep_body(copies, lengths, padding, src_grid, self_kaug, self_qaug, cross_kaug, cross_qaug, windows):
    copies.need(src_grid)
    rows = self_kaug.shape[0]
    count = lengths.shape[0]
    edge = rows - padding[0]
    ends, total = [], 0
    for at in range(count):
        total = total + lengths[at]
        ends.append(total)

    def labels(places):
        found = sum((places >= end).astype(jnp.int32) for end in ends)
        return jnp.where(places < edge, found, count)

    row_ids = labels(iota((8, rows), 1))[0:1]
    mask_rows = iota((MASK_ROWS, rows), 0)
    self_qaug[...] = jnp.where(row_ids != mask_rows, 1.0, 0.0).astype(BF16)
    cross_qaug[...] = jnp.where(jnp.minimum(row_ids, count - 1) != mask_rows, 1.0, 0.0).astype(BF16)
    lanes = iota((TILE, TILE), 1)
    ones_lanes = jnp.where((lanes >= MASK_ROWS) & (lanes < MASK_ROWS + 3), 1.0, 0.0)
    places = lanes.astype(F32)

    def columns(row):
        return jnp.broadcast_to(row, (TILE, TILE)).T

    for tile in range(rows // TILE):
        part = slice(tile * TILE, (tile + 1) * TILE)
        target_row = row_ids[:, part].astype(F32)
        self_kaug[part, :] = jnp.where(columns(target_row) == places, MASKED, ones_lanes).astype(BF16)
        source_row = src_grid[tile : tile + 1, :].astype(F32)
        cross_kaug[part, :] = jnp.where(columns(source_row) == places, MASKED, ones_lanes).astype(BF16)
    copies.push(self_kaug, self_qaug, cross_kaug, cross_qaug)
    for tile in range(rows // TILE):
        first, last = tile * TILE, tile * TILE + TILE - 1
        start, stop, first_id, last_id = 0, edge, 0, 0
        for end in ends:
            start = jnp.where(end <= first, end, start)
            first_id = first_id + jnp.where(end <= first, 1, 0)
            last_id = last_id + jnp.where(end <= last, 1, 0)
        for end in reversed(ends):
            stop = jnp.where(end > last, jnp.minimum(end, edge), stop)
        start = jnp.where(first >= edge, edge, start)
        stop = jnp.where(last >= edge, rows, stop)
        first_id = jnp.where(first < edge, jnp.minimum(first_id, count - 1), count - 1)
        last_id = jnp.where(last < edge, jnp.minimum(last_id, count - 1), count - 1)
        low = start // STEP
        windows[0, tile] = low
        windows[1, tile] = (stop + STEP - 1) // STEP - low
        source = src_grid[...]
        below = jnp.sum(jnp.where(source < first_id, 1, 0))
        upto = jnp.sum(jnp.where(source <= last_id, 1, 0))
        low = below // STEP
        windows[2, tile] = low
        windows[3, tile] = (upto + STEP - 1) // STEP - low


def pair_columns(block):
    upper = iota(block.shape, 0) < HEAD_DIM
    none = jnp.zeros_like(block)
    return jnp.concatenate([jnp.where(upper, block, none), jnp.where(upper, none, block)], axis=1)


def pair_rows(block):
    left = iota(block.shape, 1) < HEAD_DIM
    none = jnp.zeros_like(block)
    return jnp.concatenate([jnp.where(left, block, none), jnp.where(left, none, block)], axis=0)


def twice(block):
    return jnp.concatenate([block, block], axis=1)


def split_three(row):
    first = row.astype(BF16).astype(F32)
    second = (row - first).astype(BF16).astype(F32)
    third = row - first - second
    at = iota((BLOCK, row.shape[1]), 0)
    none = jnp.zeros((BLOCK, row.shape[1]), F32)
    picked = jnp.where(at == 0, first, jnp.where(at == 1, second, jnp.where(at == 2, third, none)))
    return picked.astype(BF16)


def over_windows(windows, row, rows, run):
    tiles, steps = rows // TILE, rows // STEP

    def one_tile(tile, _):
        low, width = windows[row, tile], windows[row + 1, tile]
        before = 0
        for most in WINDOWS:
            start = jnp.minimum(low, steps - most)

            @pl.when((width > before) & (width <= most))
            def _():
                run(pl.multiple_of(tile * TILE, TILE), start, most * STEP)

            before = most
        return 0

    lax.fori_loop(0, tiles, one_tile, 0)


def add_shifted(both):
    for half in range(both.shape[1]):
        value = both[0, half]
        both[1, half] = jnp.concatenate([value[:, STEP:], value[:, :STEP]], axis=1)


def shifted(start, count):
    return start % 2, pl.ds(pl.multiple_of(start // 2 * TILE, TILE), count)


def places(pair):
    inner = (pair % 2) * PAIR
    return pair // 2, slice(inner, inner + PAIR)


def head_places(pair, head):
    inner = (pair % 2) * PAIR + head * HEAD_DIM
    return pair // 2, slice(inner, inner + HEAD_DIM), slice((pair % 2) * 2 + head, (pair % 2) * 2 + head + 1)


def attend(windows, row, queries_t, keys, values_t, kaug, qaug, mixed_t, log_mass, scores, raised):
    halves, rows, width = keys.shape
    pairs = halves * width // PAIR

    def run(query_at, key_start, key_count):
        key_at = pl.multiple_of(key_start * STEP, STEP)
        side, columns = shifted(key_start, key_count)
        query_part = pl.ds(query_at, TILE)
        mask_part = twice(qaug[:, query_part])
        ones = jnp.ones((BLOCK, key_count), BF16)
        rights, found, peaks = [], [None] * pairs, [None] * pairs
        for pair in range(pairs):
            half, part = places(pair)
            rights.append(jnp.concatenate([pair_columns(queries_t[half, part, query_part]), mask_part], axis=0))

        def score(pair, at):
            half, part = places(pair)
            size = min(TILE * 2, key_count - at)
            here, span = pl.ds(key_at + at, size), slice(at, at + size)
            value = dot(jnp.concatenate([keys[half, here, part], kaug[here, :MASK_ROWS]], axis=1), rights[pair])
            scores[pair % 2, span, :] = value
            most = jnp.max(value.reshape(-1, 8, 2 * TILE), axis=0)
            found[pair] = most if at == 0 else jnp.maximum(found[pair], most)

        def raise_up(pair, at):
            span = slice(at, min(at + TILE * 2, key_count))
            if at == 0:
                peaks[pair] = jnp.max(found[pair], axis=0, keepdims=True)
            raised[pair % 2, span, :] = jnp.exp2(scores[pair % 2, span, :] - peaks[pair]).astype(BF16)

        def mix(pair):
            half, part = places(pair)
            left = jnp.concatenate([values_t[side, half, part, columns], ones], axis=0)
            mixed = dot(left, raised[pair % 2, 0:key_count, :])
            mass = mixed[PAIR : PAIR + 1]
            scale = 1.0 / mass
            logs = peaks[pair] + jnp.log2(mass)
            for head in range(2):
                spot = slice(head * TILE, (head + 1) * TILE)
                inner = slice(head * HEAD_DIM, (head + 1) * HEAD_DIM)
                half, outer, at = head_places(pair, head)
                mixed_t[half, outer, query_part] = (mixed[inner, spot] * scale[:, spot]).astype(BF16)
                log_mass[half, at, query_part] = logs[:, spot]

        for step in range(pairs + 2):
            for at in range(0, key_count, TILE * 2):
                if step < pairs:
                    score(step, at)
                if 0 <= step - 1 < pairs:
                    raise_up(step - 1, at)
                if at == 0 and 0 <= step - 2 < pairs:
                    mix(step - 2)

    over_windows(windows, row, rows, run)


def attend_back(
    windows, row, queries, queries_t, keys, keys_t, values, kaug, qaug, log_mass, delta, grad, grad_t,
    query_grad_t, key_grad, value_grad,
):
    halves, rows, width = keys.shape
    key_grad[...] = jnp.zeros_like(key_grad)
    value_grad[...] = jnp.zeros_like(value_grad)

    def run(query_at, key_start, key_count):
        side, columns = shifted(key_start, key_count)
        query_part, key_part = pl.ds(query_at, TILE), pl.ds(pl.multiple_of(key_start * STEP, STEP), key_count)
        mask_part = twice(qaug[:, query_part])
        no_mask = jnp.zeros((MASK_ROWS, 2 * TILE), BF16)
        key_mask = kaug[key_part, : MASK_ROWS + BLOCK]
        for pair in range(halves * width // PAIR):
            half, part = places(pair)
            heads = [head_places(pair, head) for head in range(2)]
            masses = jnp.concatenate([log_mass[half, at, query_part] for half, _, at in heads], axis=1)
            deltas = jnp.concatenate([delta[half, at, query_part] for half, _, at in heads], axis=1)
            right = jnp.concatenate(
                [pair_columns(queries_t[half, part, query_part]), mask_part, split_three(-masses)], axis=0
            )
            probs = jnp.exp2(dot(jnp.concatenate([keys[half, key_part, part], key_mask], axis=1), right))
            right = jnp.concatenate(
                [pair_columns(grad_t[half, part, query_part]), no_mask, split_three(-deltas)], axis=0
            )
            grad_probs = dot(jnp.concatenate([values[half, key_part, part], key_mask], axis=1), right)
            grad_scores = (probs * grad_probs).astype(BF16)
            value_grad[half, key_part, part] += dot(probs.astype(BF16), pair_rows(grad[half, query_part, part]))
            key_grad[half, key_part, part] += dot(grad_scores, pair_rows(queries[half, query_part, part]))
            mixed = dot(keys_t[side, half, part, columns], grad_scores)
            for head, (half, outer, _) in enumerate(heads):
                spot = slice(head * TILE, (head + 1) * TILE)
                inner = slice(head * HEAD_DIM, (head + 1) * HEAD_DIM)
                query_grad_t[half, outer, query_part] = mixed[inner, spot]

    over_windows(windows, row, rows, run)


def row_deltas(mixed_t, grad_t, delta):
    halves, width, rows = mixed_t.shape
    for half in range(halves):
        for head in range(width // HEAD_DIM):
            part = slice(head * HEAD_DIM, (head + 1) * HEAD_DIM)
            product = mixed_t[half, part, :].astype(F32) * grad_t[half, part, :].astype(F32)
            delta[half, head : head + 1, :] = jnp.sum(product, axis=0, keepdims=True)


def normalize(hidden):
    center = hidden - jnp.mean(hidden, axis=-1, keepdims=True)
    spread = jnp.mean(center * center, axis=-1, keepdims=True)
    inverse = lax.rsqrt(spread + 1e-05)
    return center * inverse, inverse


def normalize_back(incoming, normal, inverse, gain):
    scaled = incoming * gain
    average = jnp.mean(scaled, axis=-1, keepdims=True)
    along = jnp.mean(scaled * normal, axis=-1, keepdims=True)
    return inverse * (scaled - average - normal * along)


def chunks(rows, step, run):
    def one(at, _):
        run(pl.ds(pl.multiple_of(at * step, step), step))
        return 0

    lax.fori_loop(0, rows // step, one, 0)


def fold_rows(block):
    return jnp.sum(block.reshape(-1, 8, block.shape[1]), axis=0)


def mirrored(number):
    return sum(((number >> bit) & 1) << (4 - bit) for bit in range(5))


def origin(spots, spot, swapped=False):
    number = mirrored(spot)
    if swapped:
        number = (number & 25) | ((number & 2) << 1) | ((number & 4) >> 1)
    return jnp.where(spots[0] == 1, number ^ spots[1], spot)


def place(spots, block):
    return jnp.where(spots[0] == 1, mirrored(block) ^ spots[2], block)


def take_blocks(spots, pieces, row, target, swapped=False, column=0):
    each = pieces[0].shape[0]
    for spot in range(each * len(pieces)):
        start = pl.multiple_of(origin(spots, spot, swapped) * BLOCK, BLOCK)
        piece = pieces[spot // each]
        target[pl.ds(start, BLOCK), column : column + piece.shape[2]] = piece[spot % each, row : row + BLOCK, :]


def put_blocks(spots, grads, first, rows_each, row, value):
    for at in range(value.shape[0] // rows_each):
        grads[place(spots, first + at), row : row + rows_each, :] = value[at * rows_each : (at + 1) * rows_each]


def hand_out(copies, grads, keep, send):
    half = keep.shape[0]
    copies.push_part(grads.at[half : 2 * half], send)
    copies.push_part(grads.at[0:half], keep)


def pack_body(copies, self_qkv, self_out, cross_qkv, cross_out, ffn_in, ffn_out, gain, offset, self_block, cross_block, ffn_block):
    copies.need(self_qkv, self_out, cross_qkv, cross_out, ffn_in, ffn_out, gain, offset)
    width = self_out.shape[1]
    own = gain.shape[1]
    for which in range(3):
        rows = slice(which * BLOCK, (which + 1) * BLOCK)
        self_block[0, rows, :] = self_qkv[which]
        cross_block[0, rows, :] = cross_qkv[which]
    cross_block[0, 3 * BLOCK : 4 * BLOCK, :] = cross_out[...]
    cross_block[0, 4 * BLOCK : 5 * BLOCK, :] = self_out[...]
    scales = jnp.concatenate([gain[...].astype(F32), offset[...].astype(F32), jnp.zeros((BLOCK - 6, own), F32)], axis=0)
    scales = jnp.concatenate([scales, jnp.zeros((BLOCK, width - own), F32)], axis=1)
    cross_block[0, 5 * BLOCK : 6 * BLOCK, :] = scales.astype(BF16)
    parts = ffn_in.shape[1] // width
    for part in range(parts):
        ffn_block[part * BLOCK : (part + 1) * BLOCK, :] = ffn_in[:, part * width : (part + 1) * width]
    ffn_block[parts * BLOCK :, :] = ffn_out[...]
    copies.push(self_block, cross_block, ffn_block)


def lay_rows(value, target, part):
    wide = target.shape[2]
    for half in range(target.shape[0]):
        target[half, part, :] = value[:, half * wide : (half + 1) * wide]


def lay_columns(value, target, part):
    wide = target.shape[1]
    turned = value.T
    for half in range(target.shape[0]):
        target[half, :, part] = turned[half * wide : (half + 1) * wide]


def mixed_product(mixed_t, part, weight):
    wide = mixed_t.shape[1]
    return sum(dot_tn(mixed_t[half, :, part], weight[half * wide : (half + 1) * wide, :]) for half in range(mixed_t.shape[0]))


def self_forward_body(
    copies, left_one, left_two, left_three, left_four, right_one, right_two, right_three, right_four, tokens, kaug, qaug, spots, windows,
    queries, queries_t, keys, keys_t, values, mixed_t, log_mass, weights,
    values_t, scores, raised,
):
    left = (left_one, left_two, left_three, left_four)
    right = (right_one, right_two, right_three, right_four)
    copies.need(*left, *right)
    for which in range(3):
        take_blocks(spots, left, which * BLOCK, weights.at[which])
        take_blocks(spots, right, which * BLOCK, weights.at[which], True, left_one.shape[2])
    copies.push(weights)
    copies.need(tokens)

    def project(part):
        rows = tokens[part, :]
        query_rows = (dot(rows, weights[0]) * QUERY_SCALE).astype(BF16)
        lay_rows(query_rows, queries, part)
        lay_columns(query_rows, queries_t, part)
        key_rows = dot(rows, weights[1]).astype(BF16)
        lay_rows(key_rows, keys, part)
        lay_columns(key_rows, keys_t, part)
        value_rows = dot(rows, weights[2]).astype(BF16)
        lay_rows(value_rows, values, part)
        lay_columns(value_rows, values_t.at[0], part)

    chunks(tokens.shape[0], 1024, project)
    copies.push(queries, queries_t, keys, keys_t, values)
    add_shifted(values_t)
    copies.need(kaug, qaug)
    attend(windows, 0, queries_t, keys, values_t, kaug, qaug, mixed_t, log_mass, scores, raised)
    copies.push(mixed_t, log_mass)


def cross_forward_body(
    copies, upper_one, upper_two, upper_three, upper_four, lower_one, lower_two, lower_three, lower_four,
    tokens, self_mixed_t, encoder, kaug, qaug, spots, windows,
    hidden, hidden_two, first_low, queries, queries_t, keys, keys_t, values, mixed_t, log_mass, weights, scales,
    values_t, scores, raised, first,
):
    upper = (upper_one, upper_two, upper_three, upper_four)
    lower = (lower_one, lower_two, lower_three, lower_four)
    copies.need(*upper, *lower)
    for which in range(3):
        take_blocks(spots, upper, which * BLOCK, weights.at[which])
    for which in range(2):
        take_blocks(spots, lower, which * BLOCK, weights.at[3 + which], True)
    each = lower_one.shape[0]
    gathered = jnp.zeros(scales.shape, F32)
    for spot in range(4 * each):
        block = lower[spot // each][spot % each, 2 * BLOCK : 3 * BLOCK, :].astype(F32)
        gathered = gathered + pltpu.roll(block, origin(spots, spot, True) * BLOCK, 1)
    scales[...] = gathered
    copies.push(weights, scales)
    gain, offset = scales[0:1, :], scales[3:4, :]
    copies.need(tokens, self_mixed_t, encoder)

    def project(part):
        rows = encoder[part, :]
        key_rows = dot(rows, weights[1]).astype(BF16)
        lay_rows(key_rows, keys, part)
        lay_columns(key_rows, keys_t, part)
        value_rows = dot(rows, weights[2]).astype(BF16)
        lay_rows(value_rows, values, part)
        lay_columns(value_rows, values_t.at[0], part)
        before = tokens[part, :].astype(F32) + mixed_product(self_mixed_t, part, weights.at[4])
        hidden[part, :] = before
        normal, _ = normalize(before)
        first_rows = normal * gain + offset
        first[part, :] = first_rows
        low_rows = first_rows.astype(BF16)
        first_low[part, :] = low_rows
        query_rows = (dot(low_rows, weights[0]) * QUERY_SCALE).astype(BF16)
        lay_rows(query_rows, queries, part)
        lay_columns(query_rows, queries_t, part)

    chunks(encoder.shape[0], 512, project)
    copies.push(hidden, first_low, queries, queries_t, keys, keys_t, values)
    add_shifted(values_t)
    copies.need(kaug, qaug)
    attend(windows, 2, queries_t, keys, values_t, kaug, qaug, mixed_t, log_mass, scores, raised)
    copies.push(mixed_t, log_mass)

    def finish(part):
        hidden_two[part, :] = first[part, :] + mixed_product(mixed_t, part, weights.at[3])

    chunks(encoder.shape[0], 1024, finish)
    copies.push(hidden_two)


def feed_forward_body(
    copies, gathered, hidden, out_grad, scales, cross_mixed_t, spots,
    out, grad_two, scale_grads, inner_grads, keep, send,
    second_low, active, slope, branch, grad_inner, cross_branch, sums, grads, grads_out,
):
    rows, width = hidden.shape
    wide = active.shape[1]
    parts = wide // width
    each = wide // (width // BLOCK)
    copies.need(gathered)

    def inner(part):
        return gathered[:, part * BLOCK : (part + 1) * BLOCK, :].reshape(width, width)

    def outer(first, last):
        return gathered[first // each : last // each, parts * BLOCK :, :].reshape(last - first, width)

    sums[...] = jnp.zeros_like(sums)
    root = math.sqrt(2.0 / math.pi)
    copies.need(hidden, out_grad, scales)

    def one(part):
        normal_two, inverse_two = normalize(hidden[part, :])
        second = normal_two * scales[1:2, :] + scales[4:5, :]
        low = second.astype(BF16)
        second_low[part, :] = low
        for at in range(parts):
            span = slice(at * width, (at + 1) * width)
            value = dot(low, inner(at))
            cubic = (0.044715 * root) * (value * value)
            share = 0.5 * jnp.tanh(value * (cubic + root)) + 0.5
            passed = value * share
            active[part, span] = passed.astype(BF16)
            slope[:, span] = share + (passed - passed * share) * (6.0 * cubic + 2.0 * root)
        normal_three, inverse_three = normalize(second + dot(active[part, :], outer(0, wide)))
        out[part, :] = (normal_three * scales[2:3, :] + scales[5:6, :]).astype(BF16)
        incoming = out_grad[part, :].astype(F32)
        sums[2] += fold_rows(incoming * normal_three)
        sums[5] += fold_rows(incoming)
        grad_three = normalize_back(incoming, normal_three, inverse_three, scales[2:3, :])
        grad_low = grad_three.astype(BF16)
        branch[part, :] = grad_low
        for at in range(parts):
            span = slice(at * width, (at + 1) * width)
            grad_inner[part, span] = (dot_nt(grad_low, outer(at * width, (at + 1) * width)) * slope[:, span]).astype(BF16)
        whole = jnp.concatenate([inner(at) for at in range(parts)], axis=1)
        grad_second = grad_three + dot_nt(grad_inner[part, :], whole)
        sums[1] += fold_rows(grad_second * normal_two)
        sums[4] += fold_rows(grad_second)
        result = normalize_back(grad_second, normal_two, inverse_two, scales[1:2, :])
        grad_two[part, :] = result
        cross_branch[part, :] = result.astype(BF16)

    chunks(rows, 512, one)
    scale_grads[...] = jnp.sum(sums[...], axis=1)
    copies.push(out, grad_two, scale_grads)
    inside = parts * BLOCK

    def put(first, row, value):
        for at in range(value.shape[0] // BLOCK):
            block = first + at
            spot = jnp.where(spots[0] == 1, (block % 8) * 4 + block // 8, block)
            grads[spot, row : row + BLOCK, :] = value[at * BLOCK : (at + 1) * BLOCK]

    for at in range(parts):
        span = slice(at * width, (at + 1) * width)
        put(0, at * BLOCK, dot_tn(second_low[...], grad_inner[:, span]).astype(BF16))
    copies.push_part(grads.at[:, 0:inside, :], inner_grads.at[:, 0:inside, :])
    copies.need(cross_mixed_t)
    half_width = cross_mixed_t.shape[1]
    for half in range(cross_mixed_t.shape[0]):
        put(half * half_width // BLOCK, inside, dot(cross_mixed_t[half], cross_branch[...]).astype(BF16))
    copies.push_part(grads.at[:, inside : inside + BLOCK, :], inner_grads.at[:, inside : inside + BLOCK, :])
    for at in range(parts):
        span = slice(at * width, (at + 1) * width)
        value = dot_tn(active[:, span], branch[...]).astype(BF16)
        put_blocks(spots, grads_out, at * width // each, each, 0, value)
    hand_out(copies, grads_out, keep, send)


def back_projections(grad_rows, weight, grad, grad_t):
    def one(part):
        value = dot_nt(grad_rows[part, :], weight[...]).astype(BF16)
        lay_rows(value, grad, part)
        lay_columns(value, grad_t, part)

    chunks(grad.shape[1], 1024, one)


def round_grads(query_grad_t, key_grad, value_grad, query_low, key_low, value_low):
    def one(part):
        for half in range(key_low.shape[0]):
            query_low[half, part, :] = (query_grad_t[half, :, part] * HEAD_DIM**-0.5).T.astype(BF16)
            key_low[half, part, :] = (key_grad[half, part, :] * math.log(2.0)).astype(BF16)
            value_low[half, part, :] = value_grad[half, part, :].astype(BF16)

    chunks(key_low.shape[1], 512, one)


def back_product(low, part, weight):
    wide = low.shape[2]
    return sum(dot_nt(low[half, part, :], weight[:, half * wide : (half + 1) * wide]) for half in range(low.shape[0]))


def weight_grad(spots, grads, row, left, low):
    wide = low.shape[2]
    for half in range(low.shape[0]):
        value = dot_tn(left[...], low[half]).astype(BF16)
        span = slice(half * wide, (half + 1) * wide)
        for at in range(value.shape[0] // BLOCK):
            grads[place(spots, at), row : row + BLOCK, span] = value[at * BLOCK : (at + 1) * BLOCK]


def cross_backward_body(
    copies, grad_two, out_weight, mixed_t, queries_t, keys, kaug, qaug, values, log_mass, queries, keys_t,
    query_weight, scales, hidden, first_low, encoder, self_mixed_t, scale_grads, windows, spots,
    grad_one, self_branch, key_low, value_low, keep, send,
    branch, query_low, keys_both, grad, grad_t, delta, query_grad_t, key_grad, value_grad, sums, grads,
):
    rows, width = hidden.shape
    copies.need(grad_two, out_weight)

    def prepare(part):
        branch[part, :] = grad_two[part, :].astype(BF16)

    chunks(rows, 512, prepare)
    back_projections(branch, out_weight, grad, grad_t)
    copies.need(mixed_t)
    row_deltas(mixed_t, grad_t, delta)
    copies.need(queries_t, keys, kaug, qaug, values, log_mass, queries, keys_t)
    keys_both[0] = keys_t[...]
    add_shifted(keys_both)
    attend_back(
        windows, 2, queries, queries_t, keys, keys_both, values, kaug, qaug, log_mass, delta, grad, grad_t,
        query_grad_t, key_grad, value_grad,
    )
    round_grads(query_grad_t, key_grad, value_grad, query_low, key_low, value_low)
    copies.push(key_low, value_low)
    copies.need(query_weight, scales, hidden)
    sums[...] = jnp.zeros_like(sums)

    def finish(part):
        normal, inverse = normalize(hidden[part, :])
        incoming = grad_two[part, :] + back_product(query_low, part, query_weight)
        sums[0] += fold_rows(incoming * normal)
        sums[1] += fold_rows(incoming)
        result = normalize_back(incoming, normal, inverse, scales[0:1, :])
        grad_one[part, :] = result
        self_branch[part, :] = result.astype(BF16)

    chunks(rows, 512, finish)
    copies.push(self_branch, grad_one)
    copies.need(first_low, encoder, self_mixed_t, scale_grads)
    weight_grad(spots, grads, 0, first_low, query_low)
    weight_grad(spots, grads, BLOCK, encoder, key_low)
    weight_grad(spots, grads, 2 * BLOCK, encoder, value_low)
    half_width = self_mixed_t.shape[1]
    for half in range(self_mixed_t.shape[0]):
        value = dot(self_mixed_t[half], self_branch[...]).astype(BF16)
        put_blocks(spots, grads, half * half_width // BLOCK, BLOCK, 3 * BLOCK, value)
    at = iota((BLOCK, width), 0)
    own = jnp.sum(sums[...], axis=1)
    below = jnp.concatenate([scale_grads[...], jnp.zeros_like(scale_grads)], axis=0)
    every = jnp.where(at == 0, own[0:1], jnp.where(at == 3, own[1:2], below))
    for block in range(width // BLOCK):
        shift = (width - block * BLOCK) % width
        turned = every if shift == 0 else pltpu.roll(every, shift, 1)
        grads[place(spots, block), 4 * BLOCK : 5 * BLOCK, :] = turned.astype(BF16)
    hand_out(copies, grads, keep, send)


def self_backward_body(
    copies, branch, weight, mixed_t, queries_t, keys, kaug, qaug, values, log_mass, queries, keys_t, tokens, windows, spots,
    query_low, key_low, value_low, keep, send,
    keys_both, grad, grad_t, delta, query_grad_t, key_grad, value_grad, grads,
):
    copies.need(branch, weight)
    back_projections(branch, weight, grad, grad_t)
    copies.need(mixed_t)
    row_deltas(mixed_t, grad_t, delta)
    copies.need(queries_t, keys, kaug, qaug, values, log_mass, queries, keys_t)
    keys_both[0] = keys_t[...]
    add_shifted(keys_both)
    attend_back(
        windows, 0, queries, queries_t, keys, keys_both, values, kaug, qaug, log_mass, delta, grad, grad_t,
        query_grad_t, key_grad, value_grad,
    )
    round_grads(query_grad_t, key_grad, value_grad, query_low, key_low, value_low)
    copies.push(query_low, key_low, value_low)
    copies.need(tokens)
    for which, low in enumerate((query_low, key_low, value_low)):
        weight_grad(spots, grads, which * BLOCK, tokens, low)
    hand_out(copies, grads, keep, send)


def encoder_grad_body(copies, key_low, value_low, weights, encoder_grad):
    copies.need(key_low, value_low, weights)

    def one(part):
        value = back_product(key_low, part, weights.at[0]) + back_product(value_low, part, weights.at[1])
        encoder_grad[part, :] = value.astype(BF16)

    chunks(encoder_grad.shape[0], 1024, one)
    copies.push(encoder_grad)


def tokens_grad_body(copies, grad_one, weights, query_low, key_low, value_low, tokens_grad):
    copies.need(grad_one, weights, query_low, key_low, value_low)

    def one(part):
        value = grad_one[part, :]
        for which, low in enumerate((query_low, key_low, value_low)):
            value = value + back_product(low, part, weights.at[which])
        tokens_grad[part, :] = value.astype(BF16)

    chunks(grad_one.shape[0], 1024, one)
    copies.push(tokens_grad)


def fold_body(groups, copies, *refs):
    count = sum(2 * len(terms) for terms, _ in groups)
    terms_refs, results = list(refs[:count]), list(refs[count:])
    for terms, axis in groups:
        keep, send = results.pop(0), results.pop(0)
        for row, column in terms:
            kept, came = terms_refs.pop(0), terms_refs.pop(0)
            copies.need(kept)
            lead, (high, wide) = kept.shape[:-2], kept.shape[-2:]
            for number in range(math.prod(lead)):
                index, left = [], number
                for size in reversed(lead):
                    index.insert(0, left % size)
                    left //= size
                value = (kept[tuple(index)].astype(F32) + came[tuple(index)].astype(F32)).astype(BF16)
                target = keep if index.pop(axis) == 0 else send
                target[(*index, slice(row, row + high), slice(column, column + wide))] = value


def order_body(copies, total, spots, keep, send):
    copies.need(total)
    near, far = (spots[1] >> 3) & 1, (spots[1] >> 4) & 1
    for block in range(2):
        keep[block] = total[near + 2 * (far ^ block)]
        send[block] = total[(1 - near) + 2 * (far ^ block)]


def inner_total_body(keep, came, ffn_in, cross_out):
    width = cross_out.shape[1]
    parts = ffn_in.shape[1] // width

    def total(first):
        return keep[first : first + BLOCK, :].astype(F32) + came[first : first + BLOCK, :].astype(F32)

    for part in range(parts):
        ffn_in[:, part * width : (part + 1) * width] = total(part * BLOCK)
    cross_out[...] = total(parts * BLOCK)


def total_body(keep, came, cross_qkv, self_out, gain, offset, self_qkv, ffn_out):
    def total(first, rows):
        return keep[first : first + rows, :].astype(F32) + came[first : first + rows, :].astype(F32)

    for which in range(3):
        cross_qkv[which] = total(which * BLOCK, BLOCK)
        self_qkv[which] = total((5 + which) * BLOCK, BLOCK)
    self_out[...] = total(3 * BLOCK, BLOCK)
    ffn_out[...] = total(8 * BLOCK, ffn_out.shape[0])
    scales = total(4 * BLOCK, BLOCK)
    gain[...] = scales[0:3, : gain.shape[1]]
    offset[...] = scales[3:6, : offset.shape[1]]


def exchange(value, bit, devices):
    with jax.named_scope("across_" + ("core", "x", "y", "z", "zz")[bit] if bit < 5 else "across"):
        return exchange_bit(value, bit, devices)


def exchange_bit(value, bit, devices):
    return lax.ppermute(value, AXES, [(at, at ^ (1 << bit)) for at in range(devices)])


def bit_count(devices):
    return devices.bit_length() - 1


def join_body(*refs):
    count = len(refs) // 3
    for at in range(count):
        first, second, target = refs[2 * at], refs[2 * at + 1], refs[2 * count + at]
        for block in range(first.shape[0]):
            target[block] = first[block]
            target[first.shape[0] + block] = second[block]


def join(name, pairs, after=(), through=()):
    outs = [((2 * first.shape[0], *first.shape[1:]), first.dtype) for first, _ in pairs]
    return call_near(join_body, name, outs, [one for pair in pairs for one in pair], 1, after, through)


def join_split_body(by_rows, *refs):
    count = len(by_rows)
    for at, rows_cut in enumerate(by_rows):
        first, second, upper, lower = refs[2 * at], refs[2 * at + 1], refs[2 * count + 2 * at], refs[2 * count + 2 * at + 1]
        rows, width = upper.shape[1:]
        for block in range(2 * first.shape[0]):
            source = first if block < first.shape[0] else second
            spot = block % first.shape[0]
            upper[block] = source[spot, 0:rows, 0:width]
            lower[block] = source[spot, rows:, :] if rows_cut else source[spot, :, width:]


def join_split(name, pairs, by_rows, after=()):
    outs = []
    for (first, _), rows_cut in zip(pairs, by_rows):
        blocks, rows, width = first.shape
        outs += [((2 * blocks, rows // 2, width) if rows_cut else (2 * blocks, rows, width // 2), BF16)] * 2
    return call_near(lambda *refs: join_split_body(by_rows, *refs), name, outs, [one for pair in pairs for one in pair], 1, after)[0]


def gather_both(self_held, cross_held, prepared, devices):
    come, cross_come = exchange(self_held, 4, devices), exchange(cross_held, 4, devices)
    (self_held,), _ = join("join_self_one", [(self_held, come)])
    come = exchange(self_held, 3, devices)
    left, right = join_split("join_self_two", [(self_held, come)], (False,), (cross_come,))
    left_come, right_come = exchange(left, 2, devices), exchange(right, 1, devices)
    (cross_held,), _ = join("join_cross", [(cross_held, cross_come)])
    cross_come = exchange(cross_held, 3, devices)
    (left, right), _ = join("join_self_three", [(left, left_come), (right, right_come)], (prepared, cross_come))
    left_come, right_come = exchange(left, 1, devices), exchange(right, 2, devices)
    upper, lower = join_split("join_split", [(cross_held, cross_come)], (True,))
    upper_come, lower_come = exchange(upper, 2, devices), exchange(lower, 1, devices)
    (upper, lower), (left_come, right_come) = join(
        "join_halves", [(upper, upper_come), (lower, lower_come)], (), (left_come, right_come)
    )
    self_pieces = [left, left_come, exchange(left, 0, devices), exchange(left_come, 0, devices)]
    self_pieces += [right, right_come, exchange(right, 0, devices), exchange(right_come, 0, devices)]
    return self_pieces, (upper, lower, exchange(upper, 1, devices), exchange(lower, 2, devices))


def gather_plain(block, per, blocks):
    every = lax.all_gather(block, AXES, axis=0, tiled=False)
    parts = every.shape[1] // per
    every = every.reshape(every.shape[0], parts, per, every.shape[2]).transpose(1, 0, 2, 3)
    every = every.reshape(parts, blocks, -1, every.shape[3]).transpose(1, 0, 2, 3)
    every = every.reshape(blocks, -1, every.shape[3])
    return [every[at : at + blocks // 4] for at in range(0, blocks, blocks // 4)]


def fold(name, groups, after=(), through=(), far=False, from_far=False):
    ins, outs, shapes = [], [], []
    for terms, axis in groups:
        high = max(row + kept.shape[-2] for kept, _, row, _ in terms)
        wide = max(column + kept.shape[-1] for kept, _, _, column in terms)
        lead = list(terms[0][0].shape[:-2])
        lead.pop(axis)
        for kept, came, _, _ in terms:
            ins += [kept, came]
        outs += [((*lead, high, wide), BF16)] * 2
        shapes.append(([(row, column) for _, _, row, column in terms], axis))
    after = [pltpu.with_memory_space_constraint(one, pltpu.HBM) for one in after]
    near = range(1 if from_far else 0, len(ins), 2 if from_far else 1)
    stay = range(1 if far else 0, len(outs), 2 if far else 1)
    results = call(
        lambda *refs: fold_body(shapes, *refs), name, outs, ins, (), 2, after=after, through=through, near=near, stay=stay,
        limit=16,
    )
    passed = results[len(outs) :]
    return [tuple(results[at : at + 2]) for at in range(0, len(outs), 2)] + list(passed)


def local(
    tokens, encoder, out_grad, self_qkv, self_out, cross_qkv, cross_out, ffn_in, ffn_out, ln_gain, ln_bias,
    tgt_lengths, tgt_pad, src_segments,
):
    devices = lax.axis_size("dp") * lax.axis_size("fsdp")
    me = lax.axis_index(AXES)
    token_rows, encoder_rows = tokens[0], encoder[0]
    rows, width = token_rows.shape
    wide = ffn_in.shape[1]
    own = self_out.shape[0]
    blocks = width // BLOCK
    direct = devices == blocks and devices == 32
    parts = wide // width
    each = wide // blocks
    heads = width // HEAD_DIM

    number = me.astype(jnp.int32)
    if direct:
        spots = jnp.stack([jnp.int32(1), number, mirrored(number)])
    else:
        spots = jnp.zeros((3,), jnp.int32)

    square, tall = (rows, width), (width, rows)
    self_kaug, self_qaug, cross_kaug, cross_qaug, windows = call(
        prep_body, "prep",
        [((rows, TILE), BF16), ((MASK_ROWS, rows), BF16)] * 2 + [((4, rows // TILE), jnp.int32)],
        [tgt_lengths[0], tgt_pad, src_segments[0].reshape(-1, TILE)],
        (0, 1), 2, out_smem=(4,),
    )
    if direct:
        self_block, cross_block, ffn_block = call(
            pack_body, "pack",
            [((1, 3 * BLOCK, width), BF16), ((1, 6 * BLOCK, width), BF16), ((parts * BLOCK + each, width), BF16)],
            [self_qkv, self_out, cross_qkv, cross_out, ffn_in, ffn_out, ln_gain, ln_bias], (), 1,
        )
        self_pieces, (upper, lower, upper_came, lower_came) = gather_both(self_block, cross_block, self_kaug, devices)
        ready = (upper, lower)
        ffn_all = lax.all_gather(ffn_block, AXES, axis=0, tiled=False)
    else:
        inner_rows = jnp.concatenate([ffn_in[:, at * width : (at + 1) * width] for at in range(parts)], axis=0)
        cross_block = jnp.concatenate([cross_qkv.reshape(-1, width), cross_out, self_out], axis=0)
        self_pieces = gather_plain(self_qkv.reshape(-1, width), own, blocks)
        self_pieces = [piece[:, :, : width // 2] for piece in self_pieces] + [piece[:, :, width // 2 :] for piece in self_pieces]
        ready = ()
        cross_pieces = gather_plain(cross_block, own, blocks)
        scale_all = lax.all_gather(jnp.concatenate([ln_gain, ln_bias], axis=0), AXES, axis=1, tiled=True)
        scale_all = scale_all.reshape(-1, blocks, BLOCK).transpose(1, 0, 2)
        scale_all = jnp.pad(scale_all, ((0, 0), (0, BLOCK - scale_all.shape[1]), (0, width - BLOCK)))
        lower_pieces = [
            jnp.concatenate([piece[:, 3 * BLOCK :], scale_all[at * blocks // 4 : (at + 1) * blocks // 4]], axis=1)
            for at, piece in enumerate(cross_pieces)
        ]
        cross_pieces = [piece[:, : 3 * BLOCK] for piece in cross_pieces] + lower_pieces
        inner_all = jnp.concatenate(gather_plain(inner_rows, own, blocks), axis=0)
        outer_all = jnp.concatenate(gather_plain(ffn_out, ffn_out.shape[0], blocks), axis=0)
        ffn_all = jnp.concatenate([inner_all, outer_all], axis=1)

    halves, halves_t, masses = (2, rows, width // 2), (2, width // 2, rows), (2, 8, rows)
    saved = [(halves, BF16), (halves_t, BF16), (halves, BF16), (halves_t, BF16), (halves, BF16), (halves_t, BF16), (masses, F32)]
    both_t = (2, *halves_t)
    pipeline = [(both_t, BF16), ((2, rows, 2 * TILE), F32), ((2, rows, 2 * TILE), BF16)]
    queries, queries_t, keys, keys_t, values, mixed_t, log_mass, weights = call(
        self_forward_body, "self_forward", saved + [((3, width, width), BF16)],
        [*self_pieces, token_rows, self_kaug, self_qaug, spots, windows],
        (len(self_pieces) + 3, len(self_pieces) + 4), 15, pipeline, after=ready, limit=30,
    )
    if direct:
        _, (upper_came, lower_came) = call_near(
            lambda: None, "gate", [], [], 1, (mixed_t,), (upper_came, lower_came)
        )
        cross_pieces = [
            upper, upper_came, exchange(upper, 0, devices), exchange(upper_came, 0, devices),
            lower, lower_came, exchange(lower, 0, devices), exchange(lower_came, 0, devices),
        ]
    (
        hidden_one, hidden_two, first_low, cross_queries, cross_queries_t, cross_keys, cross_keys_t, cross_values,
        cross_mixed_t, cross_mass, cross_weights, scales,
    ) = call(
        cross_forward_body, "cross_forward",
        [(square, F32)] * 2 + [(square, BF16)] + saved + [((5, width, width), BF16), ((BLOCK, width), F32)],
        [*cross_pieces, token_rows, mixed_t, encoder_rows, cross_kaug, cross_qaug, spots, windows],
        (13, 14), 18, pipeline + [(square, F32)], near=(3, 7) if direct else (), limit=40,
    )
    inside = parts * BLOCK + BLOCK
    result, grad_two, scale_grads, inner_grads, outer_keep, outer_send = call(
        feed_forward_body, "feed_forward",
        [(square, BF16), (square, F32), ((8, width), F32), ((blocks, inside, width), BF16)]
        + [((blocks // 2, each, width), BF16)] * 2,
        [ffn_all, hidden_two, out_grad[0], scales, cross_mixed_t, spots],
        (5,), 30,
        [
            (square, BF16), ((rows, wide), BF16), ((512, wide), F32), (square, BF16), ((rows, wide), BF16), (square, BF16),
            ((8, 8, width), F32), ((blocks, inside, width), BF16), ((blocks, each, width), BF16),
        ],
        by_part=(3, 4), stay=(5,), limit=54,
    )
    if direct:
        outer_came = exchange(outer_send, 0, devices)
        near_groups = [[8 * at + other for other in range(8)] for at in range(4)]
        inner_sum = lax.psum_scatter(inner_grads, AXES, scatter_dimension=0, axis_index_groups=near_groups, tiled=True)
    work = [(both_t, BF16), (halves, BF16), (halves_t, BF16), (masses, F32), (halves_t, F32), (halves, F32), (halves, F32)]
    grad_one, self_branch, cross_key_low, cross_value_low, cross_keep, cross_send, *carried = call(
        cross_backward_body, "cross_backward",
        [(square, F32), (square, BF16)] + [(halves, BF16)] * 2 + [((blocks // 2, 5 * BLOCK, width), BF16)] * 2,
        [
            grad_two, (cross_weights, 3), cross_mixed_t, cross_queries_t, cross_keys, cross_kaug, cross_qaug, cross_values,
            cross_mass, cross_queries, cross_keys_t, (cross_weights, 0), scales, hidden_one, first_low, encoder_rows, mixed_t,
            scale_grads, windows, spots,
        ],
        (18, 19), 25,
        [(square, BF16), (halves, BF16)] + work + [((2, 8, width), F32), ((blocks, 5 * BLOCK, width), BF16)],
        by_part=(4,), stay=(5,), carry=(outer_keep,) if direct else (),
    )

    grid = (2, 2, 2, 2)
    after = ()
    if direct:

        def cube(value):
            return value.reshape(grid + value.shape[1:])

        (outer_keep,) = carried
        (outer_keep, outer_send), cross_send = fold(
            "fold_outer", [([(cube(outer_keep), cube(outer_came), 0, 0)], 0)], (self_branch,), (cross_send,), True
        )
        cross_came = exchange(cross_send, 0, devices)
        outer_came = exchange(outer_send, 1, devices)
        after = (outer_send,)
    query_low, key_low, value_low, self_keep, self_send = call(
        self_backward_body, "self_backward",
        [(halves, BF16)] * 3 + [((blocks // 2, 3 * BLOCK, width), BF16)] * 2,
        [
            self_branch, (cross_weights, 4), mixed_t, queries_t, keys, self_kaug, self_qaug, values, log_mass, queries, keys_t,
            token_rows, windows, spots,
        ],
        (12, 13), 25, work + [((blocks, 3 * BLOCK, width), BF16)], after=after, stay=(3, 4), limit=36,
    )
    after = ()
    if direct:
        (outer_keep, outer_send), (cross_keep, cross_send), self_send = fold(
            "fold_first",
            [([(outer_keep, outer_came, 0, 0)], 0), ([(cube(cross_keep), cube(cross_came), 0, 0)], 0)], (query_low,),
            (self_send,), from_far=True,
        )
        self_came = exchange(self_send, 0, devices)
        inner_keep, inner_send = call(
            order_body, "inner_order", [((2, inside, width), BF16)] * 2, [inner_sum, spots], (1,), 1, stay=(0, 1), limit=16,
        )
        inner_came = exchange(inner_send, 3, devices)
        outer_came = exchange(outer_send, 2, devices)
        cross_came = exchange(cross_send, 1, devices)
        (self_keep, self_send), inner_sum = fold(
            "fold_self", [([(cube(self_keep), cube(self_came), 0, 0)], 1)], (),
            (pltpu.with_memory_space_constraint(inner_sum, pltpu.HBM),),
        )
        self_came = exchange(self_send, 2, devices)
        after = (cross_send, self_send)
    (encoder_grad,) = call(
        encoder_grad_body, "encoder_grad", [(square, BF16)],
        [cross_key_low, cross_value_low, (cross_weights, slice(1, 3))], (), 4, after=after, limit=16,
    )
    if direct:
        (inner_keep, inner_send), (cross_keep, cross_send), (self_keep, self_send) = fold(
            "fold_second",
            [
                ([(inner_keep, inner_came, 0, 0)], 0), ([(cross_keep, cross_came, 0, 0)], 0),
                ([(self_keep, self_came, 0, 0)], 0),
            ],
            (encoder_grad,),
        )
        inner_came = exchange(inner_send, 4, devices)
        cross_came = exchange(cross_send, 2, devices)
        self_came = exchange(self_send, 1, devices)
        after = (cross_send, self_send)
    (tokens_grad,) = call(
        tokens_grad_body, "tokens_grad", [(square, BF16)], [grad_one, weights, query_low, key_low, value_low], (), 5,
        after=after, limit=20,
    )
    if direct:
        (ffn_in_grad, cross_out_grad), _ = call_near(
            inner_total_body, "inner_total", [((own, wide), F32), ((own, width), F32)], [inner_keep, inner_came], 1,
            stay=False,
        )
        ((rest_keep, rest_send),) = fold(
            "fold_third",
            [
                ([(cross_keep, cross_came, 0, 0), (self_keep, self_came, 5 * BLOCK, 0), (outer_keep, outer_came, 8 * BLOCK, 0)], 0),
            ],
            (tokens_grad, ffn_in_grad),
        )
        rest_came = exchange(rest_send, 3, devices)
        ((rest_keep, rest_send),) = fold("fold_fourth", [([(rest_keep, rest_came, 0, 0)], 0)])
        rest_came = exchange(rest_send, 4, devices)
        (cross_qkv_grad, self_out_grad, gain_grad, offset_grad, self_qkv_grad, ffn_out_grad), _ = call_near(
            total_body, "total",
            [
                ((3, own, width), F32), ((own, width), F32), ((3, own), F32), ((3, own), F32), ((3, own, width), F32),
                ((each, width), F32),
            ],
            [rest_keep, rest_came], 1, stay=False,
        )
    else:

        def add_up(grads, first, last, per):
            piece = grads[:, first:last].reshape(blocks, -1, per, width).transpose(1, 0, 2, 3)
            piece = piece.reshape(piece.shape[0], blocks * per, width)
            return lax.psum_scatter(piece.astype(F32), AXES, scatter_dimension=1, tiled=True)

        cross_grads = jnp.concatenate([cross_keep, cross_send], axis=0)
        self_grads = jnp.concatenate([self_keep, self_send], axis=0)
        inner_sum = add_up(inner_grads, 0, parts * BLOCK, BLOCK)
        ffn_in_grad = inner_sum.transpose(1, 0, 2).reshape(own, wide)
        ffn_out_grad = add_up(jnp.concatenate([outer_keep, outer_send], axis=0), 0, each, each)[0]
        cross_out_grad = add_up(inner_grads, parts * BLOCK, inside, BLOCK)[0]
        cross_qkv_grad = add_up(cross_grads, 0, 3 * BLOCK, BLOCK)
        self_out_grad = add_up(cross_grads, 3 * BLOCK, 4 * BLOCK, BLOCK)[0]
        scale_parts = cross_grads[:, 4 * BLOCK : 4 * BLOCK + 6, :BLOCK].astype(F32)
        scale_parts = scale_parts.transpose(1, 0, 2).reshape(6, width)
        scale_sum = lax.psum_scatter(scale_parts, AXES, scatter_dimension=1, tiled=True)
        gain_grad, offset_grad = scale_sum[:3], scale_sum[3:]
        self_qkv_grad = add_up(self_grads, 0, 3 * BLOCK, BLOCK)
    return (
        result[None], tokens_grad[None], encoder_grad[None], self_qkv_grad, self_out_grad, cross_qkv_grad,
        cross_out_grad, ffn_in_grad, ffn_out_grad, gain_grad, offset_grad,
    )


def solution(mesh):
    rows, first, second = P(AXES, None, None), P(AXES, None), P(None, AXES, None)
    columns = P(None, AXES)
    in_specs = (
        rows, rows, rows, second, first, second, first, first, first, columns, columns, first, P(AXES), first,
    )
    out_specs = (rows, rows, rows, second, first, second, first, first, first, columns, columns)
    return jax.shard_map(local, mesh=mesh, in_specs=in_specs, out_specs=out_specs, check_vma=False)
```

```python
import math

import jax
import jax.numpy as jnp
from jax import lax
from jax.experimental import pallas as pl
from jax.experimental.pallas import tpu as pltpu
from jax.sharding import PartitionSpec as P

F32 = jnp.float32
BF16 = jnp.bfloat16
HEAD_DIM = 64
PAIR = 2 * HEAD_DIM
TILE = 128
BLOCK = 16
AXES = ("dp", "fsdp")
QUERY_SCALE = math.log2(math.e) / math.sqrt(HEAD_DIM)
MASK_ROWS = 32
MASKED = -1e30
STEP = 64
WINDOWS = (2, 4, 6, 8, 10, 11, 12, 14, 16)
SMEM = pl.BlockSpec(memory_space=pltpu.SMEM)
ANYWHERE = pl.BlockSpec(memory_space=pl.ANY)
HBM = pl.BlockSpec(memory_space=pltpu.HBM)
VMEM = pl.BlockSpec(memory_space=pltpu.VMEM)


def dot(left, right):
    return jnp.dot(left, right, preferred_element_type=F32)


def dot_tn(left, right):
    return lax.dot_general(left, right, (((0,), (0,)), ((), ())), preferred_element_type=F32)


def dot_nt(left, right):
    return lax.dot_general(left, right, (((1,), (1,)), ((), ())), preferred_element_type=F32)


def iota(shape, axis):
    return lax.broadcasted_iota(jnp.int32, shape, axis)


def part_shape(shape, index):
    if index is None:
        return shape
    index = index if isinstance(index, tuple) else (index,)
    taken = [one.stop - one.start for one in index if isinstance(one, slice)]
    return (*taken, *shape[len(index) :])


class Copies:

    def __init__(self, semaphores):
        self.semaphores = semaphores
        self.used = 0
        self.coming = {}
        self.going = {}
        self.started = []

    def start(self, source, target):
        copy = pltpu.make_async_copy(source, target, self.semaphores.at[self.used])
        self.used += 1
        copy.start()
        return copy

    def need(self, *refs):
        for ref in refs:
            if id(ref) in self.coming:
                self.coming.pop(id(ref)).wait()

    def push(self, *refs):
        for ref in refs:
            self.started.append(self.start(*self.going.pop(id(ref))))

    def push_part(self, source, target):
        self.started.append(self.start(source, target))

    def finish(self):
        for copy in self.coming.values():
            copy.wait()
        for ref, target in self.going.values():
            self.started.append(self.start(ref, target))
        for copy in self.started:
            copy.wait()


def call(body, name, outs, ins, in_smem, micros, scratch=(), out_smem=(), after=(), by_part=(), stay=(), near=(), through=(), update=(), carry=(), far=(), limit=48):
    ins = [one if isinstance(one, tuple) else (one, None) for one in ins]
    indexes = [index for _, index in ins]
    ins = [array for array, _ in ins]
    outs = [*outs, *[(one.shape, one.dtype) for one in carry]]
    stay = (*stay, *range(len(outs) - len(carry), len(outs)))
    after = (*after, *[pltpu.with_memory_space_constraint(one, pltpu.HBM) for one in carry])
    through = (*through, *update)
    in_count, out_count = len(ins), len(outs)
    moved_in = [at for at in range(in_count) if at not in in_smem and at not in near and at not in far]
    moved_out = [at for at in range(out_count) if at not in out_smem and at not in by_part and at not in stay]
    ins = [pltpu.with_memory_space_constraint(one, pltpu.HBM) if at in moved_in or at in far else one for at, one in enumerate(ins)]

    def ordered(*refs):
        carried = refs[in_count + len(after) - len(carry) : in_count + len(after)]
        sources, refs = list(refs[:in_count]), refs[in_count + len(after) + len(through) :]
        targets, refs = list(refs[: out_count + len(through)]), refs[out_count + len(through) :]
        updated = targets[len(targets) - len(update) :]
        targets = targets[:out_count]
        carried = list(zip(carried, targets[out_count - len(carry) :]))
        targets = targets[: out_count - len(carry)]
        buffers_in, refs = refs[: len(moved_in)], refs[len(moved_in) :]
        buffers_out, refs = refs[: len(moved_out)], refs[len(moved_out) :]
        copies = Copies(refs[0])
        for at, buffer in zip(moved_in, buffers_in):
            source = sources[at] if indexes[at] is None else sources[at].at[indexes[at]]
            copies.coming[id(buffer)] = copies.start(source, buffer)
            sources[at] = buffer
        for at, buffer in zip(moved_out, buffers_out):
            copies.going[id(buffer)] = (buffer, targets[at])
            targets[at] = buffer
        for source, target in carried:
            copies.push_part(source, target)
        body(copies, *sources, *targets, *updated, *refs[1:])
        copies.finish()

    return pl.pallas_call(
        ordered,
        name=name,
        out_shape=[
            jax.ShapeDtypeStruct(shape, kind) if at in out_smem else (pltpu.VMEM if at in stay else pltpu.HBM)(shape, kind)
            for at, (shape, kind) in enumerate(outs)
        ]
        + [jax.ShapeDtypeStruct(one.shape, one.dtype) for one in through[: len(through) - len(update)]]
        + [pltpu.HBM(one.shape, one.dtype) for one in update],
        in_specs=[SMEM if at in in_smem else VMEM if at in near else HBM for at in range(in_count)]
        + [ANYWHERE] * (len(after) + len(through)),
        out_specs=[SMEM if at in out_smem else VMEM if at in stay else HBM for at in range(out_count)]
        + [ANYWHERE] * len(through),
        input_output_aliases={in_count + len(after) + at: out_count + at for at in range(len(through))},
        scratch_shapes=[pltpu.VMEM(part_shape(ins[at].shape, indexes[at]), ins[at].dtype) for at in moved_in]
        + [pltpu.VMEM(*outs[at]) for at in moved_out]
        + [pltpu.SemaphoreType.DMA((len(moved_in) + len(moved_out) + 4 * len(by_part) + len(stay) + 2 * len(update) + len(far) + 1,))]
        + [pltpu.VMEM(shape, kind) for shape, kind in scratch],
        compiler_params=pltpu.CompilerParams(vmem_limit_bytes=limit * 2**20),
        cost_estimate=pl.CostEstimate(flops=int(micros * 1e9), bytes_accessed=0, transcendentals=0),
    )(*ins, *after, *through)


def call_near(body, name, outs, ins, micros, after=(), through=(), stay=True):
    count, skipped = len(ins), len(ins) + len(after) + len(through)
    after = [pltpu.with_memory_space_constraint(one, pltpu.HBM) for one in after]
    results = pl.pallas_call(
        lambda *refs: body(*refs[:count], *refs[skipped : skipped + len(outs)]),
        name=name,
        out_shape=[pltpu.VMEM(shape, kind) if stay else jax.ShapeDtypeStruct(shape, kind) for shape, kind in outs]
        + [jax.ShapeDtypeStruct(one.shape, one.dtype) for one in through],
        in_specs=[VMEM] * count + [HBM] * len(after) + [ANYWHERE] * len(through),
        out_specs=[VMEM] * len(outs) + [ANYWHERE] * len(through),
        input_output_aliases={count + len(after) + at: len(outs) + at for at in range(len(through))},
        compiler_params=pltpu.CompilerParams(vmem_limit_bytes=16 * 2**20),
        cost_estimate=pl.CostEstimate(flops=int(micros * 1e9), bytes_accessed=0, transcendentals=0),
    )(*ins, *after, *through)
    return results[: len(outs)], results[len(outs) :]


def prep_body(copies, lengths, padding, src_grid, self_kaug, self_qaug, cross_kaug, cross_qaug, windows):
    copies.need(src_grid)
    rows = self_kaug.shape[0]
    count = lengths.shape[0]
    edge = rows - padding[0]
    ends, total = [], 0
    for at in range(count):
        total = total + lengths[at]
        ends.append(total)

    def labels(places):
        found = sum((places >= end).astype(jnp.int32) for end in ends)
        return jnp.where(places < edge, found, count)

    row_ids = labels(iota((8, rows), 1))[0:1]
    mask_rows = iota((MASK_ROWS, rows), 0)
    self_qaug[...] = jnp.where(row_ids != mask_rows, 1.0, 0.0).astype(BF16)
    cross_qaug[...] = jnp.where(jnp.minimum(row_ids, count - 1) != mask_rows, 1.0, 0.0).astype(BF16)
    lanes = iota((TILE, TILE), 1)
    ones_lanes = jnp.where((lanes >= MASK_ROWS) & (lanes < MASK_ROWS + 3), 1.0, 0.0)
    places = lanes.astype(F32)

    def columns(row):
        return jnp.broadcast_to(row, (TILE, TILE)).T

    for tile in range(rows // TILE):
        part = slice(tile * TILE, (tile + 1) * TILE)
        target_row = row_ids[:, part].astype(F32)
        self_kaug[part, :] = jnp.where(columns(target_row) == places, MASKED, ones_lanes).astype(BF16)
        source_row = src_grid[tile : tile + 1, :].astype(F32)
        cross_kaug[part, :] = jnp.where(columns(source_row) == places, MASKED, ones_lanes).astype(BF16)
    copies.push(self_kaug, self_qaug, cross_kaug, cross_qaug)
    for tile in range(rows // TILE):
        first, last = tile * TILE, tile * TILE + TILE - 1
        start, stop, first_id, last_id = 0, edge, 0, 0
        for end in ends:
            start = jnp.where(end <= first, end, start)
            first_id = first_id + jnp.where(end <= first, 1, 0)
            last_id = last_id + jnp.where(end <= last, 1, 0)
        for end in reversed(ends):
            stop = jnp.where(end > last, jnp.minimum(end, edge), stop)
        start = jnp.where(first >= edge, edge, start)
        stop = jnp.where(last >= edge, rows, stop)
        first_id = jnp.where(first < edge, jnp.minimum(first_id, count - 1), count - 1)
        last_id = jnp.where(last < edge, jnp.minimum(last_id, count - 1), count - 1)
        low = start // STEP
        windows[0, tile] = low
        windows[1, tile] = (stop + STEP - 1) // STEP - low
        source = src_grid[...]
        below = jnp.sum(jnp.where(source < first_id, 1, 0))
        upto = jnp.sum(jnp.where(source <= last_id, 1, 0))
        low = below // STEP
        windows[2, tile] = low
        windows[3, tile] = (upto + STEP - 1) // STEP - low


def pair_columns(block):
    upper = iota(block.shape, 0) < HEAD_DIM
    none = jnp.zeros_like(block)
    return jnp.concatenate([jnp.where(upper, block, none), jnp.where(upper, none, block)], axis=1)


def pair_rows(block):
    left = iota(block.shape, 1) < HEAD_DIM
    none = jnp.zeros_like(block)
    return jnp.concatenate([jnp.where(left, block, none), jnp.where(left, none, block)], axis=0)


def twice(block):
    return jnp.concatenate([block, block], axis=1)


def split_three(row):
    first = row.astype(BF16).astype(F32)
    second = (row - first).astype(BF16).astype(F32)
    third = row - first - second
    at = iota((BLOCK, row.shape[1]), 0)
    none = jnp.zeros((BLOCK, row.shape[1]), F32)
    picked = jnp.where(at == 0, first, jnp.where(at == 1, second, jnp.where(at == 2, third, none)))
    return picked.astype(BF16)


def over_windows(windows, row, rows, run):
    tiles, steps = rows // TILE, rows // STEP

    def one_tile(tile, _):
        low, width = windows[row, tile], windows[row + 1, tile]
        before = 0
        for most in WINDOWS:
            start = jnp.minimum(low, steps - most)

            @pl.when((width > before) & (width <= most))
            def _():
                run(pl.multiple_of(tile * TILE, TILE), start, most * STEP)

            before = most
        return 0

    lax.fori_loop(0, tiles, one_tile, 0)


def add_shifted(both):
    for half in range(both.shape[1]):
        value = both[0, half]
        both[1, half] = jnp.concatenate([value[:, STEP:], value[:, :STEP]], axis=1)


def shifted(start, count):
    return start % 2, pl.ds(pl.multiple_of(start // 2 * TILE, TILE), count)


def places(pair):
    inner = (pair % 2) * PAIR
    return pair // 2, slice(inner, inner + PAIR)


def head_places(pair, head):
    inner = (pair % 2) * PAIR + head * HEAD_DIM
    return pair // 2, slice(inner, inner + HEAD_DIM), slice((pair % 2) * 2 + head, (pair % 2) * 2 + head + 1)


def attend(windows, row, queries_t, keys, values_t, kaug, qaug, mixed_t, log_mass, scores, raised):
    halves, rows, width = keys.shape
    pairs = halves * width // PAIR

    def run(query_at, key_start, key_count):
        key_at = pl.multiple_of(key_start * STEP, STEP)
        side, columns = shifted(key_start, key_count)
        query_part = pl.ds(query_at, TILE)
        mask_part = twice(qaug[:, query_part])
        ones = jnp.ones((BLOCK, key_count), BF16)
        rights, found, peaks = [], [None] * pairs, [None] * pairs
        for pair in range(pairs):
            half, part = places(pair)
            rights.append(jnp.concatenate([pair_columns(queries_t[half, part, query_part]), mask_part], axis=0))

        def score(pair, at):
            half, part = places(pair)
            size = min(TILE * 2, key_count - at)
            here, span = pl.ds(key_at + at, size), slice(at, at + size)
            value = dot(jnp.concatenate([keys[half, here, part], kaug[here, :MASK_ROWS]], axis=1), rights[pair])
            scores[pair % 2, span, :] = value
            most = jnp.max(value.reshape(-1, 8, 2 * TILE), axis=0)
            found[pair] = most if at == 0 else jnp.maximum(found[pair], most)

        def raise_up(pair, at):
            span = slice(at, min(at + TILE * 2, key_count))
            if at == 0:
                peaks[pair] = jnp.max(found[pair], axis=0, keepdims=True)
            raised[pair % 2, span, :] = jnp.exp2(scores[pair % 2, span, :] - peaks[pair]).astype(BF16)

        def mix(pair):
            half, part = places(pair)
            left = jnp.concatenate([values_t[side, half, part, columns], ones], axis=0)
            mixed = dot(left, raised[pair % 2, 0:key_count, :])
            mass = mixed[PAIR : PAIR + 1]
            scale = 1.0 / mass
            logs = peaks[pair] + jnp.log2(mass)
            for head in range(2):
                spot = slice(head * TILE, (head + 1) * TILE)
                inner = slice(head * HEAD_DIM, (head + 1) * HEAD_DIM)
                half, outer, at = head_places(pair, head)
                mixed_t[half, outer, query_part] = (mixed[inner, spot] * scale[:, spot]).astype(BF16)
                log_mass[half, at, query_part] = logs[:, spot]

        for step in range(pairs + 2):
            for at in range(0, key_count, TILE * 2):
                if step < pairs:
                    score(step, at)
                if 0 <= step - 1 < pairs:
                    raise_up(step - 1, at)
                if at == 0 and 0 <= step - 2 < pairs:
                    mix(step - 2)

    over_windows(windows, row, rows, run)


def attend_back(
    windows, row, queries, queries_t, keys, keys_t, values, kaug, qaug, log_mass, delta, grad, grad_t,
    query_grad_t, key_grad, value_grad,
):
    halves, rows, width = keys.shape
    key_grad[...] = jnp.zeros_like(key_grad)
    value_grad[...] = jnp.zeros_like(value_grad)

    def run(query_at, key_start, key_count):
        side, columns = shifted(key_start, key_count)
        query_part, key_part = pl.ds(query_at, TILE), pl.ds(pl.multiple_of(key_start * STEP, STEP), key_count)
        mask_part = twice(qaug[:, query_part])
        no_mask = jnp.zeros((MASK_ROWS, 2 * TILE), BF16)
        key_mask = kaug[key_part, : MASK_ROWS + BLOCK]
        for pair in range(halves * width // PAIR):
            half, part = places(pair)
            heads = [head_places(pair, head) for head in range(2)]
            masses = jnp.concatenate([log_mass[half, at, query_part] for half, _, at in heads], axis=1)
            deltas = jnp.concatenate([delta[half, at, query_part] for half, _, at in heads], axis=1)
            right = jnp.concatenate(
                [pair_columns(queries_t[half, part, query_part]), mask_part, split_three(-masses)], axis=0
            )
            probs = jnp.exp2(dot(jnp.concatenate([keys[half, key_part, part], key_mask], axis=1), right))
            right = jnp.concatenate(
                [pair_columns(grad_t[half, part, query_part]), no_mask, split_three(-deltas)], axis=0
            )
            grad_probs = dot(jnp.concatenate([values[half, key_part, part], key_mask], axis=1), right)
            grad_scores = (probs * grad_probs).astype(BF16)
            value_grad[half, key_part, part] += dot(probs.astype(BF16), pair_rows(grad[half, query_part, part]))
            key_grad[half, key_part, part] += dot(grad_scores, pair_rows(queries[half, query_part, part]))
            mixed = dot(keys_t[side, half, part, columns], grad_scores)
            for head, (half, outer, _) in enumerate(heads):
                spot = slice(head * TILE, (head + 1) * TILE)
                inner = slice(head * HEAD_DIM, (head + 1) * HEAD_DIM)
                query_grad_t[half, outer, query_part] = mixed[inner, spot]

    over_windows(windows, row, rows, run)


def row_deltas(mixed_t, grad_t, delta):
    halves, width, rows = mixed_t.shape
    for half in range(halves):
        for head in range(width // HEAD_DIM):
            part = slice(head * HEAD_DIM, (head + 1) * HEAD_DIM)
            product = mixed_t[half, part, :].astype(F32) * grad_t[half, part, :].astype(F32)
            delta[half, head : head + 1, :] = jnp.sum(product, axis=0, keepdims=True)


def normalize(hidden):
    center = hidden - jnp.mean(hidden, axis=-1, keepdims=True)
    spread = jnp.mean(center * center, axis=-1, keepdims=True)
    inverse = lax.rsqrt(spread + 1e-05)
    return center * inverse, inverse


def normalize_back(incoming, normal, inverse, gain):
    scaled = incoming * gain
    average = jnp.mean(scaled, axis=-1, keepdims=True)
    along = jnp.mean(scaled * normal, axis=-1, keepdims=True)
    return inverse * (scaled - average - normal * along)


def chunks(rows, step, run):
    def one(at, _):
        run(pl.ds(pl.multiple_of(at * step, step), step))
        return 0

    lax.fori_loop(0, rows // step, one, 0)


def fold_rows(block):
    return jnp.sum(block.reshape(-1, 8, block.shape[1]), axis=0)


def mirrored(number):
    return sum(((number >> bit) & 1) << (4 - bit) for bit in range(5))


def origin(spots, spot, swapped=False):
    number = mirrored(spot)
    if swapped:
        number = (number & 25) | ((number & 2) << 1) | ((number & 4) >> 1)
    return jnp.where(spots[0] == 1, number ^ spots[1], spot)


def place(spots, block):
    return jnp.where(spots[0] == 1, mirrored(block) ^ spots[2], block)


def take_blocks(spots, pieces, row, target, swapped=False, column=0):
    each = pieces[0].shape[0]
    for spot in range(each * len(pieces)):
        start = pl.multiple_of(origin(spots, spot, swapped) * BLOCK, BLOCK)
        piece = pieces[spot // each]
        target[pl.ds(start, BLOCK), column : column + piece.shape[2]] = piece[spot % each, row : row + BLOCK, :]


def put_blocks(spots, grads, first, rows_each, row, value):
    for at in range(value.shape[0] // rows_each):
        grads[place(spots, first + at), row : row + rows_each, :] = value[at * rows_each : (at + 1) * rows_each]


def hand_out(copies, grads, keep, send):
    half = keep.shape[0]
    copies.push_part(grads.at[half : 2 * half], send)
    copies.push_part(grads.at[0:half], keep)


def pack_body(copies, self_qkv, self_out, cross_qkv, cross_out, ffn_in, ffn_out, gain, offset, self_block, cross_block, ffn_block):
    copies.need(self_qkv, self_out, cross_qkv, cross_out, ffn_in, ffn_out, gain, offset)
    width = self_out.shape[1]
    own = gain.shape[1]
    for which in range(3):
        rows = slice(which * BLOCK, (which + 1) * BLOCK)
        self_block[0, rows, :] = self_qkv[which]
        cross_block[0, rows, :] = cross_qkv[which]
    cross_block[0, 3 * BLOCK : 4 * BLOCK, :] = cross_out[...]
    cross_block[0, 4 * BLOCK : 5 * BLOCK, :] = self_out[...]
    scales = jnp.concatenate([gain[...].astype(F32), offset[...].astype(F32), jnp.zeros((BLOCK - 6, own), F32)], axis=0)
    scales = jnp.concatenate([scales, jnp.zeros((BLOCK, width - own), F32)], axis=1)
    cross_block[0, 5 * BLOCK : 6 * BLOCK, :] = scales.astype(BF16)
    parts = ffn_in.shape[1] // width
    for part in range(parts):
        ffn_block[part * BLOCK : (part + 1) * BLOCK, :] = ffn_in[:, part * width : (part + 1) * width]
    ffn_block[parts * BLOCK :, :] = ffn_out[...]
    copies.push(self_block, cross_block, ffn_block)


def lay_rows(value, target, part):
    wide = target.shape[2]
    for half in range(target.shape[0]):
        target[half, part, :] = value[:, half * wide : (half + 1) * wide]


def lay_columns(value, target, part):
    wide = target.shape[1]
    turned = value.T
    for half in range(target.shape[0]):
        target[half, :, part] = turned[half * wide : (half + 1) * wide]


def mixed_product(mixed_t, part, weight):
    wide = mixed_t.shape[1]
    return sum(dot_tn(mixed_t[half, :, part], weight[half * wide : (half + 1) * wide, :]) for half in range(mixed_t.shape[0]))


def self_forward_body(
    copies, left_one, left_two, left_three, left_four, right_one, right_two, right_three, right_four, tokens, kaug, qaug, spots, windows,
    queries, queries_t, keys, keys_t, values, mixed_t, log_mass, weights,
    values_t, scores, raised,
):
    left = (left_one, left_two, left_three, left_four)
    right = (right_one, right_two, right_three, right_four)
    copies.need(*left, *right)
    for which in range(3):
        take_blocks(spots, left, which * BLOCK, weights.at[which])
        take_blocks(spots, right, which * BLOCK, weights.at[which], True, left_one.shape[2])
    copies.push(weights)
    copies.need(tokens)

    def project(part):
        rows = tokens[part, :]
        query_rows = (dot(rows, weights[0]) * QUERY_SCALE).astype(BF16)
        lay_rows(query_rows, queries, part)
        lay_columns(query_rows, queries_t, part)
        key_rows = dot(rows, weights[1]).astype(BF16)
        lay_rows(key_rows, keys, part)
        lay_columns(key_rows, keys_t, part)
        value_rows = dot(rows, weights[2]).astype(BF16)
        lay_rows(value_rows, values, part)
        lay_columns(value_rows, values_t.at[0], part)

    chunks(tokens.shape[0], 1024, project)
    copies.push(queries, queries_t, keys, keys_t, values)
    add_shifted(values_t)
    copies.need(kaug, qaug)
    attend(windows, 0, queries_t, keys, values_t, kaug, qaug, mixed_t, log_mass, scores, raised)
    copies.push(mixed_t, log_mass)


def cross_forward_body(
    copies, upper_one, upper_two, upper_three, upper_four, lower_one, lower_two, lower_three, lower_four,
    tokens, self_mixed_t, encoder, kaug, qaug, spots, windows,
    hidden, hidden_two, queries, queries_t, keys, keys_t, values, mixed_t, log_mass, weights, scales,
    values_t, scores, raised, first,
):
    upper = (upper_one, upper_two, upper_three, upper_four)
    lower = (lower_one, lower_two, lower_three, lower_four)
    copies.need(*upper, *lower)
    for which in range(3):
        take_blocks(spots, upper, which * BLOCK, weights.at[which])
    for which in range(2):
        take_blocks(spots, lower, which * BLOCK, weights.at[3 + which], True)
    each = lower_one.shape[0]
    gathered = jnp.zeros(scales.shape, F32)
    for spot in range(4 * each):
        block = lower[spot // each][spot % each, 2 * BLOCK : 3 * BLOCK, :].astype(F32)
        gathered = gathered + pltpu.roll(block, origin(spots, spot, True) * BLOCK, 1)
    scales[...] = gathered
    copies.push(weights, scales)
    gain, offset = scales[0:1, :], scales[3:4, :]
    copies.need(tokens, self_mixed_t, encoder)

    def project(part):
        rows = encoder[part, :]
        key_rows = dot(rows, weights[1]).astype(BF16)
        lay_rows(key_rows, keys, part)
        lay_columns(key_rows, keys_t, part)
        value_rows = dot(rows, weights[2]).astype(BF16)
        lay_rows(value_rows, values, part)
        lay_columns(value_rows, values_t.at[0], part)
        before = tokens[part, :].astype(F32) + mixed_product(self_mixed_t, part, weights.at[4])
        hidden[part, :] = before
        normal, _ = normalize(before)
        first_rows = normal * gain + offset
        first[part, :] = first_rows
        query_rows = (dot(first_rows.astype(BF16), weights[0]) * QUERY_SCALE).astype(BF16)
        lay_rows(query_rows, queries, part)
        lay_columns(query_rows, queries_t, part)

    chunks(encoder.shape[0], 512, project)
    copies.push(hidden, queries, queries_t, keys, keys_t, values)
    add_shifted(values_t)
    copies.need(kaug, qaug)
    attend(windows, 2, queries_t, keys, values_t, kaug, qaug, mixed_t, log_mass, scores, raised)
    copies.push(mixed_t, log_mass)

    def finish(part):
        hidden_two[part, :] = first[part, :] + mixed_product(mixed_t, part, weights.at[3])

    chunks(encoder.shape[0], 1024, finish)
    copies.push(hidden_two)


def feed_forward_body(
    copies, gathered, hidden, out_grad, scales, cross_mixed_t, spots,
    out, grad_two, scale_grads, inner_grads, keep, send,
    second_low, active, slope, branch, grad_inner, cross_branch, sums, grads, grads_out,
):
    rows, width = hidden.shape
    wide = active.shape[1]
    parts = wide // width
    each = wide // (width // BLOCK)
    copies.need(gathered)

    def inner(part):
        return gathered[:, part * BLOCK : (part + 1) * BLOCK, :].reshape(width, width)

    def outer(first, last):
        return gathered[first // each : last // each, parts * BLOCK :, :].reshape(last - first, width)

    sums[...] = jnp.zeros_like(sums)
    root = math.sqrt(2.0 / math.pi)
    copies.need(hidden, out_grad, scales)

    def one(part):
        normal_two, inverse_two = normalize(hidden[part, :])
        second = normal_two * scales[1:2, :] + scales[4:5, :]
        low = second.astype(BF16)
        second_low[part, :] = low
        for at in range(parts):
            span = slice(at * width, (at + 1) * width)
            value = dot(low, inner(at))
            cubic = (0.044715 * root) * (value * value)
            share = 0.5 * jnp.tanh(value * (cubic + root)) + 0.5
            passed = value * share
            active[part, span] = passed.astype(BF16)
            slope[:, span] = share + (passed - passed * share) * (6.0 * cubic + 2.0 * root)
        normal_three, inverse_three = normalize(second + dot(active[part, :], outer(0, wide)))
        out[part, :] = (normal_three * scales[2:3, :] + scales[5:6, :]).astype(BF16)
        incoming = out_grad[part, :].astype(F32)
        sums[2] += fold_rows(incoming * normal_three)
        sums[5] += fold_rows(incoming)
        grad_three = normalize_back(incoming, normal_three, inverse_three, scales[2:3, :])
        grad_low = grad_three.astype(BF16)
        branch[part, :] = grad_low
        for at in range(parts):
            span = slice(at * width, (at + 1) * width)
            grad_inner[part, span] = (dot_nt(grad_low, outer(at * width, (at + 1) * width)) * slope[:, span]).astype(BF16)
        whole = jnp.concatenate([inner(at) for at in range(parts)], axis=1)
        grad_second = grad_three + dot_nt(grad_inner[part, :], whole)
        sums[1] += fold_rows(grad_second * normal_two)
        sums[4] += fold_rows(grad_second)
        result = normalize_back(grad_second, normal_two, inverse_two, scales[1:2, :])
        grad_two[part, :] = result
        cross_branch[part, :] = result.astype(BF16)

    chunks(rows, 512, one)
    scale_grads[...] = jnp.sum(sums[...], axis=1)
    copies.push(out, grad_two, scale_grads)
    inside = parts * BLOCK

    def put(first, row, value):
        for at in range(value.shape[0] // BLOCK):
            block = first + at
            spot = jnp.where(spots[0] == 1, (block % 8) * 4 + block // 8, block)
            grads[spot, row : row + BLOCK, :] = value[at * BLOCK : (at + 1) * BLOCK]

    for at in range(parts):
        span = slice(at * width, (at + 1) * width)
        put(0, at * BLOCK, dot_tn(second_low[...], grad_inner[:, span]).astype(BF16))
    copies.push_part(grads.at[:, 0:inside, :], inner_grads.at[:, 0:inside, :])
    copies.need(cross_mixed_t)
    half_width = cross_mixed_t.shape[1]
    for half in range(cross_mixed_t.shape[0]):
        put(half * half_width // BLOCK, inside, dot(cross_mixed_t[half], cross_branch[...]).astype(BF16))
    copies.push_part(grads.at[:, inside : inside + BLOCK, :], inner_grads.at[:, inside : inside + BLOCK, :])
    put_blocks(spots, grads_out, 0, each, 0, dot_tn(active[...], branch[...]).astype(BF16))
    hand_out(copies, grads_out, keep, send)


def back_projections(grad_rows, weight, grad, grad_t):
    def one(part):
        value = dot_nt(grad_rows[part, :], weight[...]).astype(BF16)
        lay_rows(value, grad, part)
        lay_columns(value, grad_t, part)

    chunks(grad.shape[1], 1024, one)


def round_grads(query_grad_t, key_grad, value_grad, query_low, key_low, value_low):
    def one(part):
        for half in range(key_low.shape[0]):
            query_low[half, part, :] = (query_grad_t[half, :, part] * HEAD_DIM**-0.5).T.astype(BF16)
            key_low[half, part, :] = (key_grad[half, part, :] * math.log(2.0)).astype(BF16)
            value_low[half, part, :] = value_grad[half, part, :].astype(BF16)

    chunks(key_low.shape[1], 512, one)


def back_product(low, part, weight):
    wide = low.shape[2]
    return sum(dot_nt(low[half, part, :], weight[:, half * wide : (half + 1) * wide]) for half in range(low.shape[0]))


def weight_grad(spots, grads, row, left, low):
    wide = low.shape[2]
    for half in range(low.shape[0]):
        value = dot_tn(left[...], low[half]).astype(BF16)
        span = slice(half * wide, (half + 1) * wide)
        for at in range(value.shape[0] // BLOCK):
            grads[place(spots, at), row : row + BLOCK, span] = value[at * BLOCK : (at + 1) * BLOCK]


def cross_backward_body(
    copies, grad_two, out_weight, mixed_t, queries_t, keys, kaug, qaug, values, log_mass, queries, keys_t,
    query_weight, scales, hidden, encoder, self_mixed_t, scale_grads, windows, spots,
    grad_one, self_branch, key_low, value_low, keep, send,
    branch, first_low, query_low, keys_both, grad, grad_t, delta, query_grad_t, key_grad, value_grad, sums, grads,
):
    rows, width = hidden.shape
    copies.need(grad_two, out_weight)

    def prepare(part):
        branch[part, :] = grad_two[part, :].astype(BF16)

    chunks(rows, 512, prepare)
    back_projections(branch, out_weight, grad, grad_t)
    copies.need(mixed_t)
    row_deltas(mixed_t, grad_t, delta)
    copies.need(queries_t, keys, kaug, qaug, values, log_mass, queries, keys_t)
    keys_both[0] = keys_t[...]
    add_shifted(keys_both)
    attend_back(
        windows, 2, queries, queries_t, keys, keys_both, values, kaug, qaug, log_mass, delta, grad, grad_t,
        query_grad_t, key_grad, value_grad,
    )
    round_grads(query_grad_t, key_grad, value_grad, query_low, key_low, value_low)
    copies.push(key_low, value_low)
    copies.need(query_weight, scales, hidden)
    sums[...] = jnp.zeros_like(sums)

    def finish(part):
        normal, inverse = normalize(hidden[part, :])
        first_low[part, :] = (normal * scales[0:1, :] + scales[3:4, :]).astype(BF16)
        incoming = grad_two[part, :] + back_product(query_low, part, query_weight)
        sums[0] += fold_rows(incoming * normal)
        sums[1] += fold_rows(incoming)
        result = normalize_back(incoming, normal, inverse, scales[0:1, :])
        grad_one[part, :] = result
        self_branch[part, :] = result.astype(BF16)

    chunks(rows, 512, finish)
    copies.push(self_branch, grad_one)
    copies.need(encoder, self_mixed_t, scale_grads)
    weight_grad(spots, grads, 0, first_low, query_low)
    weight_grad(spots, grads, BLOCK, encoder, key_low)
    weight_grad(spots, grads, 2 * BLOCK, encoder, value_low)
    half_width = self_mixed_t.shape[1]
    for half in range(self_mixed_t.shape[0]):
        value = dot(self_mixed_t[half], self_branch[...]).astype(BF16)
        put_blocks(spots, grads, half * half_width // BLOCK, BLOCK, 3 * BLOCK, value)
    at = iota((BLOCK, width), 0)
    own = jnp.sum(sums[...], axis=1)
    below = jnp.concatenate([scale_grads[...], jnp.zeros_like(scale_grads)], axis=0)
    every = jnp.where(at == 0, own[0:1], jnp.where(at == 3, own[1:2], below))
    for block in range(width // BLOCK):
        shift = (width - block * BLOCK) % width
        turned = every if shift == 0 else pltpu.roll(every, shift, 1)
        grads[place(spots, block), 4 * BLOCK : 5 * BLOCK, :] = turned.astype(BF16)
    hand_out(copies, grads, keep, send)


def self_backward_body(
    copies, branch, weight, mixed_t, queries_t, keys, kaug, qaug, values, log_mass, queries, keys_t, tokens, windows, spots,
    query_low, key_low, value_low, keep, send,
    keys_both, grad, grad_t, delta, query_grad_t, key_grad, value_grad, grads,
):
    copies.need(branch, weight)
    back_projections(branch, weight, grad, grad_t)
    copies.need(mixed_t)
    row_deltas(mixed_t, grad_t, delta)
    copies.need(queries_t, keys, kaug, qaug, values, log_mass, queries, keys_t)
    keys_both[0] = keys_t[...]
    add_shifted(keys_both)
    attend_back(
        windows, 0, queries, queries_t, keys, keys_both, values, kaug, qaug, log_mass, delta, grad, grad_t,
        query_grad_t, key_grad, value_grad,
    )
    round_grads(query_grad_t, key_grad, value_grad, query_low, key_low, value_low)
    copies.push(query_low, key_low, value_low)
    copies.need(tokens)
    for which, low in enumerate((query_low, key_low, value_low)):
        weight_grad(spots, grads, which * BLOCK, tokens, low)
    hand_out(copies, grads, keep, send)


def encoder_grad_body(copies, key_low, value_low, weights, encoder_grad):
    copies.need(key_low, value_low, weights)

    def one(part):
        value = back_product(key_low, part, weights.at[0]) + back_product(value_low, part, weights.at[1])
        encoder_grad[part, :] = value.astype(BF16)

    chunks(encoder_grad.shape[0], 1024, one)
    copies.push(encoder_grad)


def tokens_grad_body(copies, grad_one, weights, query_low, key_low, value_low, tokens_grad):
    copies.need(grad_one, weights, query_low, key_low, value_low)

    def one(part):
        value = grad_one[part, :]
        for which, low in enumerate((query_low, key_low, value_low)):
            value = value + back_product(low, part, weights.at[which])
        tokens_grad[part, :] = value.astype(BF16)

    chunks(grad_one.shape[0], 1024, one)
    copies.push(tokens_grad)


def fold_body(groups, copies, *refs):
    count = sum(2 * len(terms) for terms, _ in groups)
    terms_refs, results = list(refs[:count]), list(refs[count:])
    for terms, axis in groups:
        keep, send = results.pop(0), results.pop(0)
        for row, column in terms:
            kept, came = terms_refs.pop(0), terms_refs.pop(0)
            copies.need(kept)
            lead, (high, wide) = kept.shape[:-2], kept.shape[-2:]
            for number in range(math.prod(lead)):
                index, left = [], number
                for size in reversed(lead):
                    index.insert(0, left % size)
                    left //= size
                value = (kept[tuple(index)].astype(F32) + came[tuple(index)].astype(F32)).astype(BF16)
                target = keep if index.pop(axis) == 0 else send
                target[(*index, slice(row, row + high), slice(column, column + wide))] = value


def order_body(copies, total, spots, keep, send):
    copies.need(total)
    near, far = (spots[1] >> 3) & 1, (spots[1] >> 4) & 1
    for block in range(2):
        keep[block] = total[near + 2 * (far ^ block)]
        send[block] = total[(1 - near) + 2 * (far ^ block)]


def inner_total_body(keep, came, ffn_in, cross_out):
    width = cross_out.shape[1]
    parts = ffn_in.shape[1] // width

    def total(first):
        return keep[first : first + BLOCK, :].astype(F32) + came[first : first + BLOCK, :].astype(F32)

    for part in range(parts):
        ffn_in[:, part * width : (part + 1) * width] = total(part * BLOCK)
    cross_out[...] = total(parts * BLOCK)


def total_body(keep, came, cross_qkv, self_out, gain, offset, self_qkv, ffn_out):
    def total(first, rows):
        return keep[first : first + rows, :].astype(F32) + came[first : first + rows, :].astype(F32)

    for which in range(3):
        cross_qkv[which] = total(which * BLOCK, BLOCK)
        self_qkv[which] = total((5 + which) * BLOCK, BLOCK)
    self_out[...] = total(3 * BLOCK, BLOCK)
    ffn_out[...] = total(8 * BLOCK, ffn_out.shape[0])
    scales = total(4 * BLOCK, BLOCK)
    gain[...] = scales[0:3, : gain.shape[1]]
    offset[...] = scales[3:6, : offset.shape[1]]


def exchange(value, bit, devices):
    with jax.named_scope("across_" + ("core", "x", "y", "z", "zz")[bit] if bit < 5 else "across"):
        return exchange_bit(value, bit, devices)


def exchange_bit(value, bit, devices):
    return lax.ppermute(value, AXES, [(at, at ^ (1 << bit)) for at in range(devices)])


def bit_count(devices):
    return devices.bit_length() - 1


def join_body(*refs):
    count = len(refs) // 3
    for at in range(count):
        first, second, target = refs[2 * at], refs[2 * at + 1], refs[2 * count + at]
        for block in range(first.shape[0]):
            target[block] = first[block]
            target[first.shape[0] + block] = second[block]


def join(name, pairs, after=(), through=()):
    outs = [((2 * first.shape[0], *first.shape[1:]), first.dtype) for first, _ in pairs]
    return call_near(join_body, name, outs, [one for pair in pairs for one in pair], 1, after, through)


def join_split_body(by_rows, *refs):
    count = len(by_rows)
    for at, rows_cut in enumerate(by_rows):
        first, second, upper, lower = refs[2 * at], refs[2 * at + 1], refs[2 * count + 2 * at], refs[2 * count + 2 * at + 1]
        rows, width = upper.shape[1:]
        for block in range(2 * first.shape[0]):
            source = first if block < first.shape[0] else second
            spot = block % first.shape[0]
            upper[block] = source[spot, 0:rows, 0:width]
            lower[block] = source[spot, rows:, :] if rows_cut else source[spot, :, width:]


def join_split(name, pairs, by_rows, after=()):
    outs = []
    for (first, _), rows_cut in zip(pairs, by_rows):
        blocks, rows, width = first.shape
        outs += [((2 * blocks, rows // 2, width) if rows_cut else (2 * blocks, rows, width // 2), BF16)] * 2
    return call_near(lambda *refs: join_split_body(by_rows, *refs), name, outs, [one for pair in pairs for one in pair], 1, after)[0]


def gather_both(self_held, cross_held, prepared, devices):
    come, cross_come = exchange(self_held, 4, devices), exchange(cross_held, 4, devices)
    (self_held,), _ = join("join_self_one", [(self_held, come)])
    come = exchange(self_held, 3, devices)
    left, right = join_split("join_self_two", [(self_held, come)], (False,), (cross_come,))
    left_come, right_come = exchange(left, 2, devices), exchange(right, 1, devices)
    (cross_held,), _ = join("join_cross", [(cross_held, cross_come)])
    cross_come = exchange(cross_held, 3, devices)
    (left, right), _ = join("join_self_three", [(left, left_come), (right, right_come)], (prepared, cross_come))
    left_come, right_come = exchange(left, 1, devices), exchange(right, 2, devices)
    upper, lower = join_split("join_split", [(cross_held, cross_come)], (True,))
    upper_come, lower_come = exchange(upper, 2, devices), exchange(lower, 1, devices)
    (upper, lower), (left_come, right_come) = join(
        "join_halves", [(upper, upper_come), (lower, lower_come)], (), (left_come, right_come)
    )
    self_pieces = [left, left_come, exchange(left, 0, devices), exchange(left_come, 0, devices)]
    self_pieces += [right, right_come, exchange(right, 0, devices), exchange(right_come, 0, devices)]
    return self_pieces, (upper, lower, exchange(upper, 1, devices), exchange(lower, 2, devices))


def gather_plain(block, per, blocks):
    every = lax.all_gather(block, AXES, axis=0, tiled=False)
    parts = every.shape[1] // per
    every = every.reshape(every.shape[0], parts, per, every.shape[2]).transpose(1, 0, 2, 3)
    every = every.reshape(parts, blocks, -1, every.shape[3]).transpose(1, 0, 2, 3)
    every = every.reshape(blocks, -1, every.shape[3])
    return [every[at : at + blocks // 4] for at in range(0, blocks, blocks // 4)]


def fold(name, groups, after=(), through=(), far=False, from_far=False):
    ins, outs, shapes = [], [], []
    for terms, axis in groups:
        high = max(row + kept.shape[-2] for kept, _, row, _ in terms)
        wide = max(column + kept.shape[-1] for kept, _, _, column in terms)
        lead = list(terms[0][0].shape[:-2])
        lead.pop(axis)
        for kept, came, _, _ in terms:
            ins += [kept, came]
        outs += [((*lead, high, wide), BF16)] * 2
        shapes.append(([(row, column) for _, _, row, column in terms], axis))
    after = [pltpu.with_memory_space_constraint(one, pltpu.HBM) for one in after]
    near = range(1 if from_far else 0, len(ins), 2 if from_far else 1)
    stay = range(1 if far else 0, len(outs), 2 if far else 1)
    results = call(
        lambda *refs: fold_body(shapes, *refs), name, outs, ins, (), 2, after=after, through=through, near=near, stay=stay,
        limit=16,
    )
    passed = results[len(outs) :]
    return [tuple(results[at : at + 2]) for at in range(0, len(outs), 2)] + list(passed)


def local(
    tokens, encoder, out_grad, self_qkv, self_out, cross_qkv, cross_out, ffn_in, ffn_out, ln_gain, ln_bias,
    tgt_lengths, tgt_pad, src_segments,
):
    devices = lax.axis_size("dp") * lax.axis_size("fsdp")
    me = lax.axis_index(AXES)
    token_rows, encoder_rows = tokens[0], encoder[0]
    rows, width = token_rows.shape
    wide = ffn_in.shape[1]
    own = self_out.shape[0]
    blocks = width // BLOCK
    direct = devices == blocks and devices == 32
    parts = wide // width
    each = wide // blocks
    heads = width // HEAD_DIM

    number = me.astype(jnp.int32)
    if direct:
        spots = jnp.stack([jnp.int32(1), number, mirrored(number)])
    else:
        spots = jnp.zeros((3,), jnp.int32)

    square, tall = (rows, width), (width, rows)
    self_kaug, self_qaug, cross_kaug, cross_qaug, windows = call(
        prep_body, "prep",
        [((rows, TILE), BF16), ((MASK_ROWS, rows), BF16)] * 2 + [((4, rows // TILE), jnp.int32)],
        [tgt_lengths[0], tgt_pad, src_segments[0].reshape(-1, TILE)],
        (0, 1), 2, out_smem=(4,),
    )
    if direct:
        self_block, cross_block, ffn_block = call(
            pack_body, "pack",
            [((1, 3 * BLOCK, width), BF16), ((1, 6 * BLOCK, width), BF16), ((parts * BLOCK + each, width), BF16)],
            [self_qkv, self_out, cross_qkv, cross_out, ffn_in, ffn_out, ln_gain, ln_bias], (), 1,
        )
        self_pieces, (upper, lower, upper_came, lower_came) = gather_both(self_block, cross_block, self_kaug, devices)
        ready = (upper, lower)
        ffn_all = lax.all_gather(ffn_block, AXES, axis=0, tiled=False)
    else:
        inner_rows = jnp.concatenate([ffn_in[:, at * width : (at + 1) * width] for at in range(parts)], axis=0)
        cross_block = jnp.concatenate([cross_qkv.reshape(-1, width), cross_out, self_out], axis=0)
        self_pieces = gather_plain(self_qkv.reshape(-1, width), own, blocks)
        self_pieces = [piece[:, :, : width // 2] for piece in self_pieces] + [piece[:, :, width // 2 :] for piece in self_pieces]
        ready = ()
        cross_pieces = gather_plain(cross_block, own, blocks)
        scale_all = lax.all_gather(jnp.concatenate([ln_gain, ln_bias], axis=0), AXES, axis=1, tiled=True)
        scale_all = scale_all.reshape(-1, blocks, BLOCK).transpose(1, 0, 2)
        scale_all = jnp.pad(scale_all, ((0, 0), (0, BLOCK - scale_all.shape[1]), (0, width - BLOCK)))
        lower_pieces = [
            jnp.concatenate([piece[:, 3 * BLOCK :], scale_all[at * blocks // 4 : (at + 1) * blocks // 4]], axis=1)
            for at, piece in enumerate(cross_pieces)
        ]
        cross_pieces = [piece[:, : 3 * BLOCK] for piece in cross_pieces] + lower_pieces
        inner_all = jnp.concatenate(gather_plain(inner_rows, own, blocks), axis=0)
        outer_all = jnp.concatenate(gather_plain(ffn_out, ffn_out.shape[0], blocks), axis=0)
        ffn_all = jnp.concatenate([inner_all, outer_all], axis=1)

    halves, halves_t, masses = (2, rows, width // 2), (2, width // 2, rows), (2, 8, rows)
    saved = [(halves, BF16), (halves_t, BF16), (halves, BF16), (halves_t, BF16), (halves, BF16), (halves_t, BF16), (masses, F32)]
    both_t = (2, *halves_t)
    pipeline = [(both_t, BF16), ((2, rows, 2 * TILE), F32), ((2, rows, 2 * TILE), BF16)]
    queries, queries_t, keys, keys_t, values, mixed_t, log_mass, weights = call(
        self_forward_body, "self_forward", saved + [((3, width, width), BF16)],
        [*self_pieces, token_rows, self_kaug, self_qaug, spots, windows],
        (len(self_pieces) + 3, len(self_pieces) + 4), 15, pipeline, after=ready, limit=30,
    )
    if direct:
        _, (upper_came, lower_came) = call_near(
            lambda: None, "gate", [], [], 1, (mixed_t,), (upper_came, lower_came)
        )
        cross_pieces = [
            upper, upper_came, exchange(upper, 0, devices), exchange(upper_came, 0, devices),
            lower, lower_came, exchange(lower, 0, devices), exchange(lower_came, 0, devices),
        ]
    (
        hidden_one, hidden_two, cross_queries, cross_queries_t, cross_keys, cross_keys_t, cross_values,
        cross_mixed_t, cross_mass, cross_weights, scales,
    ) = call(
        cross_forward_body, "cross_forward",
        [(square, F32)] * 2 + saved + [((5, width, width), BF16), ((BLOCK, width), F32)],
        [*cross_pieces, token_rows, mixed_t, encoder_rows, cross_kaug, cross_qaug, spots, windows],
        (13, 14), 18, pipeline + [(square, F32)], near=(3, 7) if direct else (), limit=40,
    )
    inside = parts * BLOCK + BLOCK
    result, grad_two, scale_grads, inner_grads, outer_keep, outer_send = call(
        feed_forward_body, "feed_forward",
        [(square, BF16), (square, F32), ((8, width), F32), ((blocks, inside, width), BF16)]
        + [((blocks // 2, each, width), BF16)] * 2,
        [ffn_all, hidden_two, out_grad[0], scales, cross_mixed_t, spots],
        (5,), 30,
        [
            (square, BF16), ((rows, wide), BF16), ((512, wide), F32), (square, BF16), ((rows, wide), BF16), (square, BF16),
            ((8, 8, width), F32), ((blocks, inside, width), BF16), ((blocks, each, width), BF16),
        ],
        by_part=(3, 4), stay=(5,), limit=54,
    )
    if direct:
        outer_came = exchange(outer_send, 0, devices)
        near_groups = [[8 * at + other for other in range(8)] for at in range(4)]
        inner_sum = lax.psum_scatter(inner_grads, AXES, scatter_dimension=0, axis_index_groups=near_groups, tiled=True)
    work = [(both_t, BF16), (halves, BF16), (halves_t, BF16), (masses, F32), (halves_t, F32), (halves, F32), (halves, F32)]
    grad_one, self_branch, cross_key_low, cross_value_low, cross_keep, cross_send, *carried = call(
        cross_backward_body, "cross_backward",
        [(square, F32), (square, BF16)] + [(halves, BF16)] * 2 + [((blocks // 2, 5 * BLOCK, width), BF16)] * 2,
        [
            grad_two, (cross_weights, 3), cross_mixed_t, cross_queries_t, cross_keys, cross_kaug, cross_qaug, cross_values,
            cross_mass, cross_queries, cross_keys_t, (cross_weights, 0), scales, hidden_one, encoder_rows, mixed_t,
            scale_grads, windows, spots,
        ],
        (17, 18), 25,
        [(square, BF16)] * 2 + [(halves, BF16)] + work + [((2, 8, width), F32), ((blocks, 5 * BLOCK, width), BF16)],
        by_part=(4,), stay=(5,), carry=(outer_keep,) if direct else (),
    )

    grid = (2, 2, 2, 2)
    after, carry = (), ()
    if direct:

        def cube(value):
            return value.reshape(grid + value.shape[1:])

        (outer_keep,) = carried
        (outer_keep, outer_send), cross_send = fold(
            "fold_outer", [([(cube(outer_keep), cube(outer_came), 0, 0)], 0)], (self_branch,), (cross_send,), True
        )
        cross_came = exchange(cross_send, 0, devices)
        outer_came = exchange(outer_send, 1, devices)
        after, carry = (outer_send,), (outer_keep, cross_keep)
    query_low, key_low, value_low, self_keep, self_send, *carried = call(
        self_backward_body, "self_backward",
        [(halves, BF16)] * 3 + [((blocks // 2, 3 * BLOCK, width), BF16)] * 2,
        [
            self_branch, (cross_weights, 4), mixed_t, queries_t, keys, self_kaug, self_qaug, values, log_mass, queries, keys_t,
            token_rows, windows, spots,
        ],
        (12, 13), 25, work + [((blocks, 3 * BLOCK, width), BF16)], after=after, stay=(3, 4), carry=carry, limit=36,
    )
    after = ()
    if direct:
        outer_keep, cross_keep = carried
        (outer_keep, outer_send), (cross_keep, cross_send), self_send = fold(
            "fold_first",
            [([(outer_keep, outer_came, 0, 0)], 0), ([(cube(cross_keep), cube(cross_came), 0, 0)], 0)], (query_low,),
            (self_send,),
        )
        self_came = exchange(self_send, 0, devices)
        inner_keep, inner_send = call(
            order_body, "inner_order", [((2, inside, width), BF16)] * 2, [inner_sum, spots], (1,), 1, stay=(0, 1), limit=16,
        )
        inner_came = exchange(inner_send, 3, devices)
        outer_came = exchange(outer_send, 2, devices)
        cross_came = exchange(cross_send, 1, devices)
        (self_keep, self_send), inner_sum = fold(
            "fold_self", [([(cube(self_keep), cube(self_came), 0, 0)], 1)], (),
            (pltpu.with_memory_space_constraint(inner_sum, pltpu.HBM),),
        )
        self_came = exchange(self_send, 2, devices)
        after = (cross_send, self_send)
    (encoder_grad,) = call(
        encoder_grad_body, "encoder_grad", [(square, BF16)],
        [cross_key_low, cross_value_low, (cross_weights, slice(1, 3))], (), 4, after=after, limit=16,
    )
    if direct:
        (inner_keep, inner_send), (cross_keep, cross_send), (self_keep, self_send) = fold(
            "fold_second",
            [
                ([(inner_keep, inner_came, 0, 0)], 0), ([(cross_keep, cross_came, 0, 0)], 0),
                ([(self_keep, self_came, 0, 0)], 0),
            ],
            (encoder_grad,),
        )
        inner_came = exchange(inner_send, 4, devices)
        cross_came = exchange(cross_send, 2, devices)
        self_came = exchange(self_send, 1, devices)
        after = (cross_send, self_send)
    (tokens_grad,) = call(
        tokens_grad_body, "tokens_grad", [(square, BF16)], [grad_one, weights, query_low, key_low, value_low], (), 5,
        after=after, limit=20,
    )
    if direct:
        (ffn_in_grad, cross_out_grad), _ = call_near(
            inner_total_body, "inner_total", [((own, wide), F32), ((own, width), F32)], [inner_keep, inner_came], 1,
            stay=False,
        )
        ((rest_keep, rest_send),) = fold(
            "fold_third",
            [
                ([(cross_keep, cross_came, 0, 0), (self_keep, self_came, 5 * BLOCK, 0), (outer_keep, outer_came, 8 * BLOCK, 0)], 0),
            ],
            (tokens_grad, ffn_in_grad),
        )
        rest_came = exchange(rest_send, 3, devices)
        ((rest_keep, rest_send),) = fold("fold_fourth", [([(rest_keep, rest_came, 0, 0)], 0)])
        rest_came = exchange(rest_send, 4, devices)
        (cross_qkv_grad, self_out_grad, gain_grad, offset_grad, self_qkv_grad, ffn_out_grad), _ = call_near(
            total_body, "total",
            [
                ((3, own, width), F32), ((own, width), F32), ((3, own), F32), ((3, own), F32), ((3, own, width), F32),
                ((each, width), F32),
            ],
            [rest_keep, rest_came], 1, stay=False,
        )
    else:

        def add_up(grads, first, last, per):
            piece = grads[:, first:last].reshape(blocks, -1, per, width).transpose(1, 0, 2, 3)
            piece = piece.reshape(piece.shape[0], blocks * per, width)
            return lax.psum_scatter(piece.astype(F32), AXES, scatter_dimension=1, tiled=True)

        cross_grads = jnp.concatenate([cross_keep, cross_send], axis=0)
        self_grads = jnp.concatenate([self_keep, self_send], axis=0)
        inner_sum = add_up(inner_grads, 0, parts * BLOCK, BLOCK)
        ffn_in_grad = inner_sum.transpose(1, 0, 2).reshape(own, wide)
        ffn_out_grad = add_up(jnp.concatenate([outer_keep, outer_send], axis=0), 0, each, each)[0]
        cross_out_grad = add_up(inner_grads, parts * BLOCK, inside, BLOCK)[0]
        cross_qkv_grad = add_up(cross_grads, 0, 3 * BLOCK, BLOCK)
        self_out_grad = add_up(cross_grads, 3 * BLOCK, 4 * BLOCK, BLOCK)[0]
        scale_parts = cross_grads[:, 4 * BLOCK : 4 * BLOCK + 6, :BLOCK].astype(F32)
        scale_parts = scale_parts.transpose(1, 0, 2).reshape(6, width)
        scale_sum = lax.psum_scatter(scale_parts, AXES, scatter_dimension=1, tiled=True)
        gain_grad, offset_grad = scale_sum[:3], scale_sum[3:]
        self_qkv_grad = add_up(self_grads, 0, 3 * BLOCK, BLOCK)
    return (
        result[None], tokens_grad[None], encoder_grad[None], self_qkv_grad, self_out_grad, cross_qkv_grad,
        cross_out_grad, ffn_in_grad, ffn_out_grad, gain_grad, offset_grad,
    )


def solution(mesh):
    rows, first, second = P(AXES, None, None), P(AXES, None), P(None, AXES, None)
    columns = P(None, AXES)
    in_specs = (
        rows, rows, rows, second, first, second, first, first, first, columns, columns, first, P(AXES), first,
    )
    out_specs = (rows, rows, rows, second, first, second, first, first, first, columns, columns)
    return jax.shard_map(local, mesh=mesh, in_specs=in_specs, out_specs=out_specs, check_vma=False)
```
